128 devices in a mesh: shard: 16 (over y, z_hi, core), context: 8 (over x, z_lo).
Axes of the slice: x: 4, y: 4, z: 4 (z_hi: 2, z_lo: 2; z = z_hi * 2 + z_lo), core: 2. Of those that a mesh axis runs over, the one named last changes fastest.
Arguments:
- inputs: bfloat16 [16384, 1024], P(('shard', 'context')), may hold values from -6 to 6
- ln_gain: float32 [1024], replicated, may hold values from 0.1 to 1.9
- ln_bias: float32 [1024], replicated, may hold values from -2 to 2
- w_in: bfloat16 [7168, 1024], P('shard'), may hold values from -2 to 2
- b_in: float32 [7168], replicated, may hold values from -2 to 2
- w_out: bfloat16 [1024, 5120], P('shard'), may hold values from -2 to 2
- b_out: float32 [1024], replicated, may hold values from -2 to 2
- cotangent: bfloat16 [16384, 1024], P(('shard', 'context')), may hold values from -24 to 24
Outputs:
- out: bfloat16 [16384, 1024], P(('shard', 'context'))
- grad_inputs: bfloat16 [16384, 1024], P(('shard', 'context'))
- grad_ln_gain: float32 [1024], replicated
- grad_ln_bias: float32 [1024], replicated
- grad_w_in: float32 [7168, 1024], P('shard')
- grad_b_in: float32 [7168], replicated
- grad_w_out: float32 [1024, 5120], P('shard')
- grad_b_out: float32 [1024], replicated
The draws below stay inside these ranges and needn't reach their ends.
All inputs are finite; a program needn't handle non-finite values.
Results may differ from the reference program's by a relative error of at most 0.018.
Values may be sent and summed in bfloat16 or wider, within the bound.
No kernel may reach another device: no remote copies, remote signals or barrier semaphores. Data moves between devices by JAX's collectives and lax.ppermute only.
A program may use at most 128 MiB of HBM per device.

```python
import jax
import jax.numpy as jnp
from jax import lax

D = 1024
FF = 4096
H = 16
HD = 64
ROT = 32
SEQ = 1024
TOKENS = 16384
N_SHARD = 16


def draw_w_in(key, part):
    key = jax.random.fold_in(key, 11)
    normal_part = jnp.clip(jax.random.normal(key, (3 * D + FF, D), jnp.float32), -6.0, 6.0)
    row_index = jnp.arange(3 * D + FF)[:, None]
    factor = jnp.where(row_index < 2 * D, 1.5, 1.0) * D ** (-0.5)
    return (normal_part * factor).astype(jnp.bfloat16)


def draw_w_out(key, part):
    key = jax.random.fold_in(key, 23)
    normal_part = jnp.clip(jax.random.normal(key, (D, D + FF), jnp.float32), -6.0, 6.0)
    column_index = jnp.arange(D + FF)[None, :]
    factor = jnp.where(column_index < D, 2.0 * D ** (-0.5), FF ** (-0.5))
    return (normal_part * factor).astype(jnp.bfloat16)


def with_spikes(values, own_key, source, target, blocks, factor):
    def block_of(dim):
        return (jnp.arange(values.shape[dim]) // (values.shape[dim] // blocks)).reshape((-1,) + (1,) * (values.ndim - 1 - dim))

    one_side = jax.random.permutation(own_key, blocks)[block_of(target)]
    other_side = (block_of(target) + blocks // 2) % blocks
    return jnp.where((block_of(source) == one_side) | (block_of(source) == other_side), factor * values, values)


def block_levels(stream_key, shape, cuts, least, high):
    def one(position, shards_of):
        draws = jax.random.uniform(jax.random.fold_in(jax.random.fold_in(stream_key, 6), position), (shards_of,), jnp.float32, least / len(cuts), high / len(cuts))
        return jnp.repeat(jnp.exp(draws), shape[position] // shards_of).reshape((-1,) + (1,) * (len(shape) - position - 1))

    loudness = one(*cuts[0])
    for cut in cuts[1:]:
        loudness = loudness * one(*cut)
    return loudness


def gaussian(stream_key, shape, width, most, pieces=(), kind=jnp.bfloat16):
    values = width * jax.random.normal(stream_key, shape, jnp.float32)
    if pieces:
        values = values * block_levels(stream_key, shape, pieces, -0.22, 0.18)
    return jnp.clip(values, -most, most).astype(kind)


def gaussian_with(key, extent, spread, most, cuts, heavy, held_as=jnp.bfloat16):
    values = spread * jax.random.normal(key, extent, jnp.float32)
    if cuts:
        values = values * block_levels(key, extent, cuts, -0.22, 0.18)
    return jnp.clip(with_spikes(values, jax.random.fold_in(key, 3), *heavy), -most, most).astype(held_as)


def setup_inputs(seed: int = 0) -> dict:
    arg_keys = jax.random.split(jax.random.key(seed), 9)
    return {
        "inputs": gaussian(arg_keys[0], (TOKENS, D), 1.0, 6.0, ((0, 128),)),
        "ln_gain": jnp.clip(1.0 + 0.18 * jax.random.normal(arg_keys[1], (D,), jnp.float32), 0.1, 1.9),
        "ln_bias": gaussian(arg_keys[2], (D,), 0.3, 2.0, (), jnp.float32),
        "w_in": draw_w_in(jax.random.fold_in(arg_keys[8], 71), 0),
        "b_in": gaussian(arg_keys[4], (3 * D + FF,), 0.3, 2.0, (), jnp.float32),
        "w_out": draw_w_out(jax.random.fold_in(arg_keys[8], 71), 0),
        "b_out": gaussian(arg_keys[6], (D,), 0.3, 2.0, (), jnp.float32),
        "cotangent": gaussian_with(arg_keys[7], (TOKENS, D), 1.0, 24.0, ((0, 128),), (0, 1, 128, 5.5)),
    }


@jax.custom_vjp
def low(v):
    return lax.optimization_barrier(v.astype(jnp.bfloat16)).astype(jnp.float32)

@jax.custom_vjp
def low_back(v):
    return v

def low_keep(v):
    return (low(v), None)

def low_pass(kept, grad):
    return (grad,)

def back_keep(v):
    return (v, None)

def back_low(kept, grad):
    return (low(grad),)
low.defvjp(low_keep, low_pass)
low_back.defvjp(back_keep, back_low)
epsilon = 1e-05
highest = lax.Precision.HIGHEST

def angles_of(length):
    steps = jnp.arange(ROT // 2).astype(jnp.float32)
    inverse = 10000.0 ** (-2.0 * steps / ROT)
    return jnp.arange(length).astype(jnp.float32)[:, None] * inverse[None, :]

def rotate(values, angles):
    half = ROT // 2
    first = values[..., :half]
    second = values[..., half:ROT]
    remaining = values[..., ROT:]
    cosine = jnp.cos(angles)[:, None, :]
    sine = jnp.sin(angles)[:, None, :]
    return jnp.concatenate([first * cosine - second * sine, second * cosine + first * sine, remaining], axis=-1)

def forward(rows_in, gain, shift, weight_in, bias_in, weight_out, bias_out):
    average = lax.optimization_barrier(jnp.mean(rows_in, axis=-1, keepdims=True))
    centred = rows_in - average
    variance = lax.optimization_barrier(jnp.mean(centred * centred, axis=-1, keepdims=True))
    normed = centred * lax.rsqrt(variance + epsilon) * gain + shift
    hidden = low(normed)
    projected = jnp.dot(hidden, weight_in.T, precision=highest) + bias_in
    projected = low_back(projected)
    angles = angles_of(SEQ)
    query = rotate(projected[:, :D].reshape(SEQ, H, HD), angles)
    keys = rotate(projected[:, D:2 * D].reshape(SEQ, H, HD), angles)
    values = projected[:, 2 * D:3 * D].reshape(SEQ, H, HD)
    query = low(low_back(query))
    keys = low(low_back(keys))
    values = low(low_back(values))
    scores = jnp.einsum('qhd,khd->hqk', query, keys, precision=highest) * HD ** (-0.5)
    scores = low_back(scores)
    allowed = jnp.arange(SEQ)[:, None] >= jnp.arange(SEQ)[None, :]
    scores = jnp.where(allowed[None], scores, -1e+30)
    largest = lax.optimization_barrier(jnp.max(scores, axis=-1, keepdims=True))
    raised = jnp.exp(scores - largest)
    probs = raised / lax.optimization_barrier(jnp.sum(raised, axis=-1, keepdims=True))
    weights = low(probs)
    attn = jnp.einsum('hqk,khd->qhd', weights, values, precision=highest).reshape(SEQ, D)
    attn = low(low_back(attn))
    gated = low(jax.nn.gelu(projected[:, 3 * D:], approximate=True))
    joined = jnp.concatenate([attn, gated], axis=1)
    return rows_in + jnp.dot(joined, weight_out.T, precision=highest) + bias_out

def reference(inputs, ln_gain, ln_bias, w_in, b_in, w_out, b_out, cotangent):
    params = (ln_gain.astype(jnp.float32), ln_bias.astype(jnp.float32), w_in.astype(jnp.float32), b_in.astype(jnp.float32), w_out.astype(jnp.float32), b_out.astype(jnp.float32))
    sequences = inputs.astype(jnp.float32).reshape(N_SHARD, SEQ, D)
    cot_rows = cotangent.astype(jnp.float32).reshape(N_SHARD, SEQ, D)

    def step(totals, pair):
        rows_in, cot_seq = pair
        result, pullback = jax.vjp(forward, rows_in, *params)
        grads = pullback(cot_seq)
        new_totals = tuple((total + grad for total, grad in zip(totals, grads[1:])))
        return (new_totals, (result, grads[0]))
    start_totals = tuple((jnp.zeros(param.shape, jnp.float32) for param in params))
    totals, (results, grad_rows) = lax.scan(step, start_totals, (sequences, cot_rows))
    out = results.reshape(TOKENS, D).astype(jnp.bfloat16)
    grad_inputs = grad_rows.reshape(TOKENS, D).astype(jnp.bfloat16)
    return (out, grad_inputs, totals[0], totals[1], totals[2], totals[3], totals[4], totals[5])
```

```python
import functools

import jax
import jax.numpy as jnp
import numpy as np
from jax import lax
from jax.sharding import Mesh
from jax.sharding import PartitionSpec as P

D = 1024
FF = 4096
H = 16
HD = 64
ROT = 32
SEQ = 1024
EPS = 1e-05
BF = jnp.bfloat16
F32 = jnp.float32

SHARD = ("y", "zh", "core")
CONTEXT = ("x", "zl")

HEADS = ((0, 7), (8, 1), (14, 9), (6, 15), (12, 5), (4, 13), (10, 3), (2, 11))
UNITS_PER_SHARD = 7


def deal_units():
    columns = [[[], []] for _ in range(8)]
    qkv = [[kind * H + head for kind in range(3) for head in pair] for pair in HEADS]
    taken = [{unit // UNITS_PER_SHARD for unit in units} for units in qkv]
    order = []

    def place(unit):
        if unit == 112:
            return True
        shard, parity = unit // UNITS_PER_SHARD, unit % 2
        choices = sorted(range(8), key=lambda c: len(columns[c][0]) + len(columns[c][1]))
        for c in choices:
            if shard in taken[c] or len(columns[c][parity]) == 4:
                continue
            taken[c].add(shard)
            columns[c][parity].append(unit)
            if place(unit + 1):
                return True
            taken[c].remove(shard)
            columns[c][parity].pop()
        return False

    assert place(48)
    for c in range(8):
        pairs = [unit for pair in zip(*columns[c]) for unit in pair]
        order.append(qkv[c] + pairs)
    return np.array(order, np.int32)


UNITS = deal_units()
SLOT = UNITS // UNITS_PER_SHARD
SEND = np.zeros((16, 8), np.int32)
for _c in range(8):
    for _u in UNITS[_c]:
        SEND[_u // UNITS_PER_SHARD, _c] = _u % UNITS_PER_SHARD
HOME = np.zeros((112, 2), np.int32)
for _c in range(8):
    for _i, _u in enumerate(UNITS[_c]):
        HOME[_u] = (_c, _i)
COLUMN_UNITS = np.concatenate([np.array(HEADS, np.int32), UNITS[:, 6:] - 32], axis=1)
COLUMN_HOME = np.zeros((80, 2), np.int32)
for _c in range(8):
    for _i, _u in enumerate(COLUMN_UNITS[_c]):
        COLUMN_HOME[_u] = (_c, _i)


def swap(values, axis):
    return lax.ppermute(values, axis, [(0, 1), (1, 0)])


def ordered(index, mine, other, axis):
    first = jnp.where(index == 0, mine, other)
    second = jnp.where(index == 0, other, mine)
    return jnp.stack([first, second], axis=axis)


def spread(values, axes, count):
    copies = jnp.broadcast_to(values[None], (count,) + values.shape)
    return lax.all_to_all(copies, axes, 0, 0, tiled=True)


def gather_context(values):
    zl = lax.axis_index("zl")
    pair = ordered(zl, values, swap(values, "zl"), 0)
    return spread(pair, "x", 4).reshape((8,) + values.shape)


def scatter_context(parts):
    zl = lax.axis_index("zl")
    arrived = lax.all_to_all(parts.reshape((4, 2) + parts.shape[1:]), "x", 0, 0, tiled=True)
    total = jnp.sum(arrived.astype(F32), axis=0)
    mine = lax.dynamic_index_in_dim(total, zl, 0, keepdims=False)
    other = lax.dynamic_index_in_dim(total, 1 - zl, 0, keepdims=False)
    return mine + swap(other.astype(BF), "zl").astype(F32)


def gather_shard(values):
    core = lax.axis_index("core")
    near = spread(values, ("y", "zh"), 8)
    far = swap(near, "core")
    return ordered(core, near, far, 1).reshape((16,) + values.shape)


def scatter_shard(parts):
    core = lax.axis_index("core")
    halves = parts.reshape((8, 2) + parts.shape[1:])
    mine = lax.dynamic_index_in_dim(halves, core, 1, keepdims=False)
    other = lax.dynamic_index_in_dim(halves, 1 - core, 1, keepdims=False)
    near = (mine.astype(F32) + swap(other, "core").astype(F32)).astype(BF)
    arrived = lax.all_to_all(near, ("y", "zh"), 0, 0, tiled=True)
    return jnp.sum(arrived.astype(F32), axis=0)


def against(left, right):
    return lax.dot_general(left, right, (((1,), (1,)), ((), ())), preferred_element_type=F32)


def over_tokens(left, right):
    return lax.dot_general(left, right, (((0,), (0,)), ((), ())), preferred_element_type=F32)


def gelu_tanh(values):
    return jax.nn.gelu(values, approximate=True)


def normal(rows):
    average = jnp.mean(rows, axis=-1, keepdims=True)
    centred = rows - average
    variance = jnp.mean(centred * centred, axis=-1, keepdims=True)
    scale = lax.rsqrt(variance + EPS)
    return centred * scale, scale


def turn_tables():
    steps = jnp.arange(ROT // 2).astype(F32)
    angles = jnp.arange(SEQ).astype(F32)[:, None] * (10000.0 ** (-2.0 * steps / ROT))[None, :]
    cosine, sine = jnp.cos(angles), jnp.sin(angles)
    still = jnp.ones((SEQ, HD - ROT), F32)
    cosines = jnp.concatenate([cosine, cosine, still] * 2, axis=1)
    sines = jnp.concatenate([-sine, sine, 0.0 * still] * 2, axis=1)
    return cosines, sines


def turn(values, cosines, sines):
    lane = jnp.arange(2 * HD) % HD
    partner = jnp.where(lane < ROT // 2, jnp.roll(values, -(ROT // 2), 1), jnp.roll(values, ROT // 2, 1))
    return values * cosines + partner * sines


def on_device(inputs, ln_gain, ln_bias, w_in, b_in, w_out, b_out, cotangent):
    shard = lax.axis_index(SHARD)
    context = lax.axis_index(CONTEXT)
    scale = HD ** (-0.5)
    units = jnp.asarray(UNITS)[context]
    slots = jnp.asarray(SLOT)[context]

    x_all = gather_context(inputs).reshape(SEQ, D)
    unit = lax.dynamic_slice_in_dim(w_in, jnp.asarray(SEND)[shard, context] * 64, 64, 0)
    w_in_slots = gather_shard(unit)
    w_mine = w_in_slots[slots].reshape(896, D)
    column_units = jnp.asarray(COLUMN_UNITS)[context]
    w_out_part = w_out.reshape(64, 80, 64)[:, column_units].reshape(64, 640)
    w_out_mine = gather_shard(w_out_part).reshape(D, 640)
    cot_all = gather_context(cotangent).reshape(SEQ, D)
    bias = b_in.reshape(112, 64)[units].reshape(896)

    xhat, _ = normal(x_all.astype(F32))
    hidden = (xhat * ln_gain + ln_bias).astype(BF)
    projected = against(hidden, w_mine) + bias
    cosines, sines = turn_tables()
    query = turn(projected[:, :128], cosines, sines).astype(BF)
    keys = turn(projected[:, 128:256], cosines, sines).astype(BF)
    values = projected[:, 256:384].astype(BF)
    act = projected[:, 384:]
    gated = gelu_tanh(act).astype(BF)

    def heads(a):
        return a.reshape(SEQ, 2, HD)

    place = jnp.arange(SEQ)
    scores = jnp.einsum("qhd,khd->hqk", heads(query), heads(keys), preferred_element_type=F32) * scale
    scores = jnp.where((place[:, None] >= place[None, :])[None], scores, -1e30)
    raised = jnp.exp(scores - jnp.max(scores, axis=-1, keepdims=True))
    probs = raised / jnp.sum(raised, axis=-1, keepdims=True)
    weights = probs.astype(BF)
    attn = jnp.einsum("hqk,khd->qhd", weights, heads(values), preferred_element_type=F32).reshape(SEQ, 128).astype(BF)
    joined = jnp.concatenate([attn, gated], axis=1)
    out_part = against(joined, w_out_mine).astype(BF)
    mixed = scatter_context(out_part.reshape(8, 128, D))
    out = (inputs.astype(F32) + mixed + b_out).astype(BF)

    grad_joined = jnp.dot(cot_all, w_out_mine, preferred_element_type=F32)
    grad_attn = grad_joined[:, :128].astype(BF)
    grad_act = jax.vjp(gelu_tanh, act)[1](grad_joined[:, 128:])[0]
    grad_values = jnp.einsum("hqk,qhd->khd", weights, heads(grad_attn), preferred_element_type=F32).reshape(SEQ, 128)
    grad_probs = jnp.einsum("qhd,khd->hqk", heads(grad_attn), heads(values), preferred_element_type=F32)
    delta = jnp.sum(grad_probs * probs, axis=-1, keepdims=True)
    grad_scores = (probs * (grad_probs - delta)).astype(BF)
    grad_query = jnp.einsum("hqk,khd->qhd", grad_scores, heads(keys), preferred_element_type=F32) * scale
    grad_keys = jnp.einsum("hqk,qhd->khd", grad_scores, heads(query), preferred_element_type=F32) * scale
    grad_query = grad_query.reshape(SEQ, 128).astype(BF).astype(F32)
    grad_keys = grad_keys.reshape(SEQ, 128).astype(BF).astype(F32)
    grad_proj = jnp.concatenate(
        [turn(grad_query, cosines, -sines), turn(grad_keys, cosines, -sines), grad_values, grad_act], axis=1
    ).astype(BF)

    grad_normed = jnp.dot(grad_proj, w_mine, preferred_element_type=F32)
    grad_hidden = scatter_context(grad_normed.astype(BF).reshape(8, 128, D))
    grad_w_in = over_tokens(grad_proj, hidden).astype(BF).reshape(14, 64, D)
    grad_w_in = jnp.zeros((16, 64, D), BF).at[slots].set(grad_w_in)
    grad_w_out = over_tokens(cot_all, joined).astype(BF).reshape(16, 64, 640)
    grad_w_in = scatter_shard(grad_w_in).astype(BF)
    grad_w_out = scatter_shard(grad_w_out).astype(BF)
    grad_w_in = gather_context(grad_w_in)
    grad_w_out = gather_context(grad_w_out)
    homes = jnp.asarray(HOME[:, 0].reshape(16, 7))[shard]
    grad_w_in = grad_w_in[homes].reshape(448, D).astype(F32)
    grad_w_out = grad_w_out.reshape(8, 64, 10, 64).transpose(0, 2, 1, 3).reshape(80, 64, 64)
    grad_w_out = grad_w_out[COLUMN_HOME[:, 0] * 10 + COLUMN_HOME[:, 1]].transpose(1, 0, 2).reshape(64, 5120).astype(F32)

    small = jnp.concatenate(
        [
            jnp.sum(grad_proj.astype(F32), axis=0),
            jnp.sum(grad_normed * xhat, axis=0),
            jnp.sum(grad_normed, axis=0),
            jnp.sum(cotangent.astype(F32), axis=0),
        ]
    ).reshape(31, 128)
    small = jnp.sum(spread(small, SHARD, 16).reshape(16, 31, 128), axis=0)
    small = spread(small, CONTEXT, 8).reshape(8, 31 * 128)
    grad_b_in = small[:, :896].reshape(112, 64)[HOME[:, 0] * 14 + HOME[:, 1]].reshape(7168)
    rest = jnp.sum(small[:, 896:], axis=0)
    grad_gain, grad_shift, grad_b_out = rest[:D], rest[D : 2 * D], rest[2 * D :]

    own, own_scale = normal(inputs.astype(F32))
    pulled = grad_hidden * ln_gain
    grad_rows = (
        pulled
        - jnp.mean(pulled, axis=-1, keepdims=True)
        - own * jnp.mean(pulled * own, axis=-1, keepdims=True)
    ) * own_scale
    grad_inputs = (cotangent.astype(F32) + grad_rows).astype(BF)
    return (out, grad_inputs, grad_gain, grad_shift, grad_w_in, grad_b_in, grad_w_out, grad_b_out)


def solution(mesh):
    fine = Mesh(mesh.devices.reshape(4, 2, 2, 4, 2), SHARD + CONTEXT)
    rows = P(SHARD + CONTEXT, None)
    in_specs = (rows, P(), P(), P(SHARD, None), P(), P(SHARD, None), P(), rows)
    out_specs = (rows, rows, P(), P(), P(SHARD, None), P(), P(SHARD, None), P())
    return jax.shard_map(on_device, mesh=fine, in_specs=in_specs, out_specs=out_specs, check_vma=False)
```

```python
import functools
import math

import jax
import jax.numpy as jnp
import numpy as np
from jax import lax
from jax.experimental import pallas as pl
from jax.experimental.pallas import tpu as pltpu
from jax.sharding import Mesh
from jax.sharding import PartitionSpec as P

D = 1024
FF = 4096
H = 16
HD = 64
ROT = 32
SEQ = 1024
EPS = 1e-05
BF = jnp.bfloat16
F32 = jnp.float32
MIB = 1 << 20

SHARD = ("y", "zh", "core")
CONTEXT = ("x", "zl")

HEADS = ((0, 7), (8, 1), (14, 9), (6, 15), (12, 5), (4, 13), (10, 3), (2, 11))
UNITS_PER_SHARD = 7


def deal_units():
    columns = [[[], []] for _ in range(8)]
    qkv = [[kind * H + head for kind in range(3) for head in pair] for pair in HEADS]
    taken = [{unit // UNITS_PER_SHARD for unit in units} for units in qkv]
    order = []

    def place(unit):
        if unit == 112:
            return True
        shard, parity = unit // UNITS_PER_SHARD, unit % 2
        choices = sorted(range(8), key=lambda c: len(columns[c][0]) + len(columns[c][1]))
        for c in choices:
            if shard in taken[c] or len(columns[c][parity]) == 4:
                continue
            taken[c].add(shard)
            columns[c][parity].append(unit)
            if place(unit + 1):
                return True
            taken[c].remove(shard)
            columns[c][parity].pop()
        return False

    assert place(48)
    for c in range(8):
        pairs = [unit for pair in zip(*columns[c]) for unit in pair]
        order.append(qkv[c] + pairs)
    return np.array(order, np.int32)


UNITS = deal_units()
SLOT = UNITS // UNITS_PER_SHARD
SEND = np.zeros((16, 8), np.int32)
for _c in range(8):
    for _u in UNITS[_c]:
        SEND[_u // UNITS_PER_SHARD, _c] = _u % UNITS_PER_SHARD
HOME = np.zeros((112, 2), np.int32)
for _c in range(8):
    for _i, _u in enumerate(UNITS[_c]):
        HOME[_u] = (_c, _i)
COLUMN_UNITS = np.concatenate([np.array(HEADS, np.int32), UNITS[:, 6:] - 32], axis=1)
COLUMN_HOME = np.zeros((80, 2), np.int32)
for _c in range(8):
    for _i, _u in enumerate(COLUMN_UNITS[_c]):
        COLUMN_HOME[_u] = (_c, _i)


TABLE = np.concatenate([SLOT, COLUMN_UNITS // 2, UNITS // 2], axis=1).astype(np.int32)
SHARD_TABLE = np.concatenate([SEND, HOME[:, 0].reshape(16, 7)], axis=1).astype(np.int32)

def nn(left, right):
    return lax.dot_general(left, right, (((1,), (0,)), ((), ())), preferred_element_type=F32)


def nt(left, right):
    return lax.dot_general(left, right, (((1,), (1,)), ((), ())), preferred_element_type=F32)


def tn(left, right):
    return lax.dot_general(left, right, (((0,), (0,)), ((), ())), preferred_element_type=F32)


def normal(rows):
    average = jnp.mean(rows, axis=-1, keepdims=True)
    centred = rows - average
    variance = jnp.mean(centred * centred, axis=-1, keepdims=True)
    scale = lax.rsqrt(variance + EPS)
    return centred * scale, scale


def turn(values, cosines, sines):
    lane = lax.broadcasted_iota(jnp.int32, values.shape, 1) % HD
    ahead = pltpu.roll(values, 2 * HD - ROT // 2, 1)
    behind = pltpu.roll(values, ROT // 2, 1)
    return values * cosines + jnp.where(lane < ROT // 2, ahead, behind) * sines


def head_mask(values, head):
    lane = lax.broadcasted_iota(jnp.int32, values.shape, 1)
    return jnp.where((lane // HD) == head, values, jnp.zeros_like(values))


SCALE2 = HD ** (-0.5) * math.log2(math.e)
GELU_C = math.sqrt(2.0 / math.pi)
BLOCK = 256


def causal(shape, first_key, first_query):
    key = first_key + lax.broadcasted_iota(jnp.int32, shape, 0)
    query = first_query + lax.broadcasted_iota(jnp.int32, shape, 1)
    return key <= query


def block_scores(q_block, k_head, block):
    extent = (block + 1) * BLOCK
    scores = nt(k_head[:extent], q_block) * SCALE2
    last = scores[block * BLOCK:]
    last = jnp.where(causal(last.shape, 0, 0), last, -1e30)
    if block == 0:
        return last
    return jnp.concatenate([scores[: block * BLOCK], last], axis=0)


def place_pair(zl, pair, a, b):
    @pl.when(zl == 0)
    def _():
        a[...] = pair[:128]
        b[...] = pair[128:]

    @pl.when(zl != 0)
    def _():
        a[...] = pair[128:]
        b[...] = pair[:128]


def prepare_kernel(ids, table, shard_table, w_in, w_out, b_in, message, bias):
    shard, context = ids[3], ids[4]
    unit = shard_table[shard, context]
    rows = w_in[pl.ds(pl.multiple_of(unit * HD, HD), HD), :]
    lower = lax.broadcasted_iota(jnp.int32, (HD, 128), 1) < HD
    tiles = []
    for j in range(5):
        even = w_out[:, pl.ds(pl.multiple_of(table[context, 14 + 2 * j] * 128, 128), 128)]
        odd = w_out[:, pl.ds(pl.multiple_of(table[context, 15 + 2 * j] * 128, 128), 128)]
        tiles.append(jnp.where(lower, even, odd))
    for copy in range(8):
        message[copy, :, :D] = rows
        for j in range(5):
            message[copy, :, D + j * 128 : D + (j + 1) * 128] = tiles[j]
    lower = lax.broadcasted_iota(jnp.int32, (1, 128), 1) < HD
    for j in range(7):
        even = b_in[pl.ds(table[context, 24 + 2 * j], 1), :]
        odd = b_in[pl.ds(table[context, 25 + 2 * j], 1), :]
        bias[:, j * 128 : (j + 1) * 128] = jnp.where(lower, even, odd)


def forward_kernel(ids, table, a0, b0, al, bl, ar, br, af, bf, near, far, bias, gain, shift, cosines, sines,
                   hidden, xhat, weights_in, weights_out, qkv, slope, joined, lse,
                   oa, ob, ra, rb, fa, fb, la, lb):
    x, zl, core, context = ids[0], ids[1], ids[2], ids[4]
    for i in range(14):
        slot = table[context, i]
        row, odd = slot // 2, slot % 2
        rows = pl.ds(i * HD, HD)

        @pl.when(odd == core)
        def _():
            weights_in[rows, :] = near[row, :, :D]

        @pl.when(odd != core)
        def _():
            weights_in[rows, :] = far[row, :, :D]

    for j in range(8):
        weights_out[pl.ds(pl.multiple_of(j * 128 + core * HD, HD), HD), :] = near[j, :, D:]
        weights_out[pl.ds(pl.multiple_of(j * 128 + (1 - core) * HD, HD), HD), :] = far[j, :, D:]

    for step, (a, b) in enumerate(((a0, b0), (ar, br), (af, bf), (al, bl))):
        for piece, which in ((a, zl), (b, 1 - zl)):
            first = (lax.rem(x + step, 4) * 2 + which) * 128
            rows = pl.ds(pl.multiple_of(first, 128), 128)
            normed, _ = normal(piece[...].astype(F32))
            xhat[rows, :] = normed.astype(BF)
            hidden[rows, :] = (normed * gain[...] + shift[...]).astype(BF)

    @pl.loop(0, 4)
    def _(i):
        rows = pl.ds(pl.multiple_of(i * 256, 256), 256)
        proj = nt(hidden[rows, :], weights_in[...]) + bias[...]
        cos_rows, sin_rows = cosines[rows, :], sines[rows, :]
        qkv[rows, 0:128] = turn(proj[:, 0:128], cos_rows, sin_rows).astype(BF)
        qkv[rows, 128:256] = turn(proj[:, 128:256], cos_rows, sin_rows).astype(BF)
        qkv[rows, 256:384] = proj[:, 256:384].astype(BF)
        act = proj[:, 384:]
        square = act * act
        th = jnp.tanh(GELU_C * act * (1.0 + 0.044715 * square))
        half = 0.5 * (1.0 + th)
        joined[rows, 128:] = (act * half).astype(BF)
        slope[rows, :] = (
            half + 0.5 * act * (1.0 - th * th) * (GELU_C * (1.0 + 3 * 0.044715 * square))
        ).astype(BF)

    keys, values = qkv[:, 128:256], qkv[:, 256:384]
    for head in range(2):
        k_head = head_mask(keys, head)
        v_head = head_mask(values, head)
        for block in range(SEQ // BLOCK):
            rows = pl.ds(block * BLOCK, BLOCK)
            scores = block_scores(qkv[rows, 0:128], k_head, block)
            largest = jnp.max(scores, axis=0, keepdims=True)
            raised = jnp.exp2(scores - largest)
            mass = jnp.sum(raised, axis=0, keepdims=True)
            lse[head : head + 1, block * BLOCK : (block + 1) * BLOCK] = largest + jnp.log2(mass)
            probs = (raised * (1.0 / mass)).astype(BF)
            result = tn(probs, v_head[: (block + 1) * BLOCK])
            if head == 0:
                joined[rows, 0:128] = result.astype(BF)
            else:
                joined[rows, 0:128] = (joined[rows, 0:128].astype(F32) + result).astype(BF)

    for step, a, b in ((2, fa, fb), (1, ra, rb), (3, la, lb), (0, oa, ob)):
        rows = pl.ds(pl.multiple_of(lax.rem(x + step, 4) * 256, 256), 256)
        place_pair(zl, nt(joined[rows, :], weights_out[...]).astype(BF), a, b)


def backward_out_kernel(ids, a0, b0, al, bl, ar, br, af, bf, weights_out, slope, joined,
                        grad_attn, grad_ff, near, far, grad_b_out, cot):
    x, zl, core = ids[0], ids[1], ids[2]
    for step, (a, b) in enumerate(((a0, b0), (ar, br), (af, bf), (al, bl))):
        for piece, which in ((a, zl), (b, 1 - zl)):
            first = (lax.rem(x + step, 4) * 2 + which) * 128
            cot[pl.ds(pl.multiple_of(first, 128), 128), :] = piece[...]
    grad_b_out[...] = jnp.zeros_like(grad_b_out)

    @pl.loop(0, 4)
    def _(i):
        rows = pl.ds(pl.multiple_of(i * 256, 256), 256)
        grad = nn(cot[rows, :], weights_out[...])
        grad_attn[rows, :] = grad[:, :128].astype(BF)
        grad_ff[rows, :] = (grad[:, 128:] * slope[rows, :].astype(F32)).astype(BF)
        grad_b_out[0:1, :] += jnp.sum(cot[rows, :].astype(F32), axis=0, keepdims=True)

    for i in range(4):
        grad = tn(cot[:, i * 256 : (i + 1) * 256], joined[...]).astype(BF)
        for j in (0, 1):
            pair = grad[j * 128 : (j + 1) * 128]

            @pl.when(core == 0)
            def _():
                near[2 * i + j, :, :] = pair[:HD]
                far[2 * i + j, :, :] = pair[HD:]

            @pl.when(core != 0)
            def _():
                near[2 * i + j, :, :] = pair[HD:]
                far[2 * i + j, :, :] = pair[:HD]


def backward_in_kernel(ids, table, qkv, lse, grad_attn, grad_ff, weights_in, hidden, xhat, cosines, sines,
                       near, far, oa, ob, ra, rb, fa, fb, la, lb, grad_bias, small,
                       grad_proj, grad_q, grad_k, grad_v):
    x, zl, core, context = ids[0], ids[1], ids[2], ids[4]
    keys, values = qkv[:, 128:256], qkv[:, 256:384]
    grad_k[...] = jnp.zeros_like(grad_k)
    grad_v[...] = jnp.zeros_like(grad_v)
    for head in range(2):
        k_head = head_mask(keys, head)
        v_head = head_mask(values, head)
        for block in range(SEQ // BLOCK):
            rows = pl.ds(block * BLOCK, BLOCK)
            extent = (block + 1) * BLOCK
            scores = block_scores(qkv[rows, 0:128], k_head, block)
            probs = jnp.exp2(scores - lse[head : head + 1, block * BLOCK : (block + 1) * BLOCK])
            grad_out = grad_attn[rows, :]
            grad_probs = nt(v_head[:extent], grad_out)
            delta = jnp.sum(grad_probs * probs, axis=0, keepdims=True)
            grad_scores = (probs * (grad_probs - delta)).astype(BF)
            grad_v[:extent, :] += nn(probs.astype(BF), head_mask(grad_out, head))
            grad_k[:extent, :] += nn(grad_scores, head_mask(qkv[rows, 0:128], head))
            result = tn(grad_scores, k_head[:extent])
            if head == 0:
                grad_q[rows, :] = result
            else:
                grad_q[rows, :] += result
    scale = HD ** (-0.5)
    cos_all, sin_all = cosines[...], -sines[...]
    grad_proj[:, 0:128] = turn((grad_q[...] * scale).astype(BF).astype(F32), cos_all, sin_all).astype(BF)
    grad_proj[:, 128:256] = turn((grad_k[...] * scale).astype(BF).astype(F32), cos_all, sin_all).astype(BF)
    grad_proj[:, 256:384] = grad_v[...].astype(BF)
    grad_proj[:, 384:] = grad_ff[...]

    for row in range(8):
        near[row, :, :] = jnp.zeros((HD, D), BF)
        far[row, :, :] = jnp.zeros((HD, D), BF)
    for i in range(7):
        grad = tn(grad_proj[:, i * 128 : (i + 1) * 128], hidden[...]).astype(BF)
        for j in (0, 1):
            slot = table[context, 2 * i + j]
            row, odd = slot // 2, slot % 2

            @pl.when(odd == core)
            def _():
                near[row, :, :] = grad[j * HD : (j + 1) * HD]

            @pl.when(odd != core)
            def _():
                far[row, :, :] = grad[j * HD : (j + 1) * HD]

    small[...] = jnp.zeros_like(small)
    grad_bias[...] = jnp.zeros_like(grad_bias)
    for step, a, b in ((2, fa, fb), (1, ra, rb), (3, la, lb), (0, oa, ob)):
        rows = pl.ds(pl.multiple_of(lax.rem(x + step, 4) * 256, 256), 256)
        proj = grad_proj[rows, :]
        grad = nn(proj, weights_in[...])
        place_pair(zl, grad.astype(BF), a, b)
        small[0:1, :] += jnp.sum(grad * xhat[rows, :].astype(F32), axis=0, keepdims=True)
        small[1:2, :] += jnp.sum(grad, axis=0, keepdims=True)
        grad_bias[0:1, :] += jnp.sum(proj.astype(F32), axis=0, keepdims=True)


def finish_out_kernel(oa, ra, la, far, inputs, b_out, out):
    mixed = (oa[...].astype(F32) + ra[...].astype(F32)) + (la[...].astype(F32) + far[...].astype(F32))
    out[...] = (inputs[...].astype(F32) + mixed + b_out[...]).astype(BF)


def finish_in_kernel(oa, ra, la, far, inputs, cotangent, gain, grad_inputs):
    grad = (oa[...].astype(F32) + ra[...].astype(F32)) + (la[...].astype(F32) + far[...].astype(F32))
    own, scale = normal(inputs[...].astype(F32))
    pulled = grad * gain[...]
    rows = (
        pulled
        - jnp.mean(pulled, axis=-1, keepdims=True)
        - own * jnp.mean(pulled * own, axis=-1, keepdims=True)
    ) * scale
    grad_inputs[...] = (cotangent[...].astype(F32) + rows).astype(BF)


def add_kernel(left, right, total):
    total[...] = (left[...].astype(F32) + right[...].astype(F32)).astype(BF)


def add3_kernel(one, two, three, total):
    total[...] = (one[...].astype(F32) + two[...].astype(F32) + three[...].astype(F32)).astype(BF)


def sum_kernel(parts, total):
    total[...] = jnp.sum(parts[...].astype(F32), axis=0).astype(BF)


def finish_weights_kernel(ids, shard_table, a0, b0, al, bl, ar, br, af, bf, grad_w_in, grad_w_out, held):
    x, zl, shard = ids[0], ids[1], ids[3]
    for step, (a, b) in enumerate(((a0, b0), (ar, br), (af, bf), (al, bl))):
        for piece, which in ((a, zl), (b, 1 - zl)):
            held[lax.rem(x + step, 4) * 2 + which] = piece[...]
    for i in range(7):
        grad_w_in[i * HD : (i + 1) * HD, :] = held[shard_table[shard, 8 + i], :, :D].astype(F32)
    lower = lax.broadcasted_iota(jnp.int32, (HD, 128), 1) < HD
    for t in range(40):
        tiles = []
        for unit in (2 * t, 2 * t + 1):
            c, i = (int(n) for n in COLUMN_HOME[unit])
            first = D + (i // 2) * 128
            tiles.append(held[c, :, first : first + 128].astype(F32))
        grad_w_out[:, t * 128 : (t + 1) * 128] = jnp.where(lower, *tiles)


VM = pl.BlockSpec(memory_space=pltpu.VMEM)
SM = pl.BlockSpec(memory_space=pltpu.SMEM)
S = jax.ShapeDtypeStruct


def kernel(body, outs, scalars, operands, name, scratch=()):
    return pl.pallas_call(
        body,
        out_shape=outs,
        in_specs=[SM] * len(scalars) + [VM] * len(operands),
        out_specs=jax.tree.map(lambda _: VM, outs),
        scratch_shapes=list(scratch),
        compiler_params=pltpu.CompilerParams(vmem_limit_bytes=56 * MIB),
        name=name,
    )(*scalars, *operands)


def shift(values, axis, by):
    count = 4
    return lax.ppermute(values, axis, [(i, (i + by) % count) for i in range(count)])


def swap(values, axis):
    return lax.ppermute(values, axis, [(0, 1), (1, 0)])


def gather_context(own):
    al, ar = shift(own, "x", 1), shift(own, "x", -1)
    partner = swap(own, "zl")
    bl, br = shift(partner, "x", 1), shift(partner, "x", -1)
    af, bf = shift(al, "x", 1), shift(br, "x", -1)
    return own, partner, al, bl, ar, br, af, bf


def add(left, right):
    return kernel(add_kernel, S(left.shape, BF), (), (left, right), "add")


def scatter_context(oa, ob, ra, rb, fa, fb, la, lb):
    fb = shift(fb, "x", -1)
    rb = shift(rb, "x", 1)
    fa = shift(fa, "x", 1)
    lb = shift(add(lb, fb), "x", -1)
    ra = shift(add(ra, fa), "x", 1)
    la = shift(la, "x", -1)
    ob = kernel(add3_kernel, S(ob.shape, BF), (), (ob, rb, lb), "add3")
    return oa, ra, la, swap(ob, "zl")


def scatter_shard(near, far):
    near = kernel(add_kernel, S(near.shape, BF), (), (near, swap(far, "core")), "add_core")
    arrived = lax.all_to_all(near, ("y", "zh"), 0, 0, tiled=True)
    return kernel(sum_kernel, S(near.shape[1:], BF), (), (arrived,), "sum8")


def spread(values, axes, count):
    copies = jnp.broadcast_to(values[None], (count,) + values.shape)
    return lax.all_to_all(copies, axes, 0, 0, tiled=True)


def turn_tables():
    steps = jnp.arange(ROT // 2).astype(F32)
    angles = jnp.arange(SEQ).astype(F32)[:, None] * (10000.0 ** (-2.0 * steps / ROT))[None, :]
    cosine, sine = jnp.cos(angles), jnp.sin(angles)
    still = jnp.ones((SEQ, HD - ROT), F32)
    cosines = jnp.concatenate([cosine, cosine, still] * 2, axis=1)
    sines = jnp.concatenate([-sine, sine, 0.0 * still] * 2, axis=1)
    return cosines, sines


def on_device(inputs, ln_gain, ln_bias, w_in, b_in, w_out, b_out, cotangent):
    ids = jnp.stack(
        [lax.axis_index("x"), lax.axis_index("zl"), lax.axis_index("core"), lax.axis_index(SHARD), lax.axis_index(CONTEXT)]
    ).astype(jnp.int32)
    table, shard_table = jnp.asarray(TABLE), jnp.asarray(SHARD_TABLE)
    cosines, sines = turn_tables()
    gain, shift_row = ln_gain[None], ln_bias[None]

    tokens = gather_context(inputs)
    message, bias = kernel(
        prepare_kernel, (S((8, HD, 1664), BF), S((1, 896), F32)), (ids, table, shard_table),
        (w_in, w_out, b_in.reshape(56, 128)), "prepare",
    )
    near = lax.all_to_all(message, ("y", "zh"), 0, 0, tiled=True)
    far = swap(near, "core")
    cots = gather_context(cotangent)

    chunk = S((128, D), BF)
    hidden, xhat, weights_in, weights_out, qkv, slope, joined, lse, *parts = kernel(
        forward_kernel,
        (S((SEQ, D), BF), S((SEQ, D), BF), S((896, D), BF), S((D, 640), BF), S((SEQ, 384), BF),
         S((SEQ, 512), BF), S((SEQ, 640), BF), S((8, SEQ), F32)) + (chunk,) * 8,
        (ids, table), (*tokens, near, far, bias, gain, shift_row, cosines, sines), "forward",
    )
    terms = scatter_context(*parts)
    out = kernel(finish_out_kernel, chunk, (), (*terms, inputs, b_out[None]), "finish_out")

    slots = lambda columns: S((8, HD, columns), BF)
    grad_attn, grad_ff, near_out, far_out, grad_b_out = kernel(
        backward_out_kernel,
        (S((SEQ, 128), BF), S((SEQ, 512), BF), slots(640), slots(640), S((8, D), F32)),
        (ids,), (*cots, weights_out, slope, joined), "backward_out", [pltpu.VMEM((SEQ, D), BF)],
    )
    grad_w_out = scatter_shard(near_out, far_out)

    near_in, far_in, *parts, grad_bias, small = kernel(
        backward_in_kernel,
        (slots(D), slots(D)) + (chunk,) * 8 + (S((8, 896), F32), S((8, D), F32)),
        (ids, table), (qkv, lse, grad_attn, grad_ff, weights_in, hidden, xhat, cosines, sines), "backward_in",
        [pltpu.VMEM((SEQ, 896), BF)] + [pltpu.VMEM((SEQ, 128), F32)] * 3,
    )
    grad_w_in = scatter_shard(near_in, far_in)
    terms = scatter_context(*parts)
    grad_inputs = kernel(finish_in_kernel, chunk, (), (*terms, inputs, cotangent, gain), "finish_in")

    pieces = gather_context(jnp.concatenate([grad_w_in, grad_w_out], axis=1))
    grad_w_in, grad_w_out = kernel(
        finish_weights_kernel, (S((448, D), F32), S((HD, 5120), F32)), (ids, shard_table), pieces, "finish_weights",
        [pltpu.VMEM((8, HD, 1664), BF)],
    )

    vectors = jnp.concatenate([grad_bias[0], small[0], small[1], grad_b_out[0]]).reshape(31, 128)
    vectors = jnp.sum(spread(vectors, SHARD, 16).reshape(16, 31, 128), axis=0)
    vectors = spread(vectors, CONTEXT, 8).reshape(8, 31 * 128)
    grad_b_in = vectors[:, :896].reshape(112, 64)[HOME[:, 0] * 14 + HOME[:, 1]].reshape(7168)
    grad_gain = jnp.sum(vectors[:, 896 : 896 + D], axis=0)
    grad_shift = jnp.sum(vectors[:, 896 + D : 896 + 2 * D], axis=0)
    return (out, grad_inputs, grad_gain, grad_shift, grad_w_in, grad_b_in, grad_w_out, vectors[0, 896 + 2 * D :])


def solution(mesh):
    fine = Mesh(mesh.devices.reshape(4, 2, 2, 4, 2), SHARD + CONTEXT)
    rows = P(SHARD + CONTEXT, None)
    in_specs = (rows, P(), P(), P(SHARD, None), P(), P(SHARD, None), P(), rows)
    out_specs = (rows, rows, P(), P(), P(SHARD, None), P(), P(SHARD, None), P())
    return jax.shard_map(on_device, mesh=fine, in_specs=in_specs, out_specs=out_specs, check_vma=False)
```

```python
import functools
import math

import jax
import jax.numpy as jnp
import numpy as np
from jax import lax
from jax.experimental import pallas as pl
from jax.experimental.pallas import tpu as pltpu
from jax.sharding import Mesh
from jax.sharding import PartitionSpec as P

D = 1024
FF = 4096
H = 16
HD = 64
ROT = 32
SEQ = 1024
EPS = 1e-05
BF = jnp.bfloat16
F32 = jnp.float32
MIB = 1 << 20

SHARD = ("y", "zh", "core")
CONTEXT = ("x", "zl")

HEADS = ((0, 7), (8, 1), (14, 9), (6, 15), (12, 5), (4, 13), (10, 3), (2, 11))
UNITS_PER_SHARD = 7


def deal_units():
    columns = [[[], []] for _ in range(8)]
    qkv = [[kind * H + head for kind in range(3) for head in pair] for pair in HEADS]
    taken = [{unit // UNITS_PER_SHARD for unit in units} for units in qkv]
    order = []

    def place(unit):
        if unit == 112:
            return True
        shard, parity = unit // UNITS_PER_SHARD, unit % 2
        choices = sorted(range(8), key=lambda c: len(columns[c][0]) + len(columns[c][1]))
        for c in choices:
            if shard in taken[c] or len(columns[c][parity]) == 4:
                continue
            taken[c].add(shard)
            columns[c][parity].append(unit)
            if place(unit + 1):
                return True
            taken[c].remove(shard)
            columns[c][parity].pop()
        return False

    assert place(48)
    for c in range(8):
        pairs = [unit for pair in zip(*columns[c]) for unit in pair]
        order.append(qkv[c] + pairs)
    return np.array(order, np.int32)


UNITS = deal_units()
SLOT = UNITS // UNITS_PER_SHARD
SEND = np.zeros((16, 8), np.int32)
for _c in range(8):
    for _u in UNITS[_c]:
        SEND[_u // UNITS_PER_SHARD, _c] = _u % UNITS_PER_SHARD
HOME = np.zeros((112, 2), np.int32)
for _c in range(8):
    for _i, _u in enumerate(UNITS[_c]):
        HOME[_u] = (_c, _i)
COLUMN_UNITS = np.concatenate([np.array(HEADS, np.int32), UNITS[:, 6:] - 32], axis=1)
COLUMN_HOME = np.zeros((80, 2), np.int32)
for _c in range(8):
    for _i, _u in enumerate(COLUMN_UNITS[_c]):
        COLUMN_HOME[_u] = (_c, _i)


TABLE = np.concatenate([SLOT, COLUMN_UNITS // 2, UNITS // 2], axis=1).astype(np.int32)
SHARD_TABLE = np.concatenate([SEND, HOME[:, 0].reshape(16, 7)], axis=1).astype(np.int32)

def nn(left, right):
    return lax.dot_general(left, right, (((1,), (0,)), ((), ())), preferred_element_type=F32)


def nt(left, right):
    return lax.dot_general(left, right, (((1,), (1,)), ((), ())), preferred_element_type=F32)


def tn(left, right):
    return lax.dot_general(left, right, (((0,), (0,)), ((), ())), preferred_element_type=F32)


def normal(rows):
    average = jnp.mean(rows, axis=-1, keepdims=True)
    centred = rows - average
    variance = jnp.mean(centred * centred, axis=-1, keepdims=True)
    scale = lax.rsqrt(variance + EPS)
    return centred * scale, scale


def turn(values, cosines, sines):
    lane = lax.broadcasted_iota(jnp.int32, values.shape, 1) % HD
    ahead = pltpu.roll(values, 2 * HD - ROT // 2, 1)
    behind = pltpu.roll(values, ROT // 2, 1)
    return values * cosines + jnp.where(lane < ROT // 2, ahead, behind) * sines


def head_mask(values, head):
    lane = lax.broadcasted_iota(jnp.int32, values.shape, 1)
    return jnp.where((lane // HD) == head, values, jnp.zeros_like(values))


SCALE2 = HD ** (-0.5) * math.log2(math.e)
GELU_C = math.sqrt(2.0 / math.pi)
BLOCK = 256


def causal(shape, first_key, first_query):
    key = first_key + lax.broadcasted_iota(jnp.int32, shape, 0)
    query = first_query + lax.broadcasted_iota(jnp.int32, shape, 1)
    return key <= query


def block_scores(q_block, k_head, block):
    extent = (block + 1) * BLOCK
    scores = nt(k_head[:extent], q_block) * SCALE2
    last = scores[block * BLOCK:]
    last = jnp.where(causal(last.shape, 0, 0), last, -1e30)
    if block == 0:
        return last
    return jnp.concatenate([scores[: block * BLOCK], last], axis=0)


def place_pair(zl, pair, a, b):
    @pl.when(zl == 0)
    def _():
        a[...] = pair[:128]
        b[...] = pair[128:]

    @pl.when(zl != 0)
    def _():
        a[...] = pair[128:]
        b[...] = pair[:128]


def prepare_kernel(ids, table, shard_table, w_in, w_out, b_in, message, bias):
    shard, context = ids[3], ids[4]
    unit = shard_table[shard, context]
    rows = w_in[pl.ds(pl.multiple_of(unit * HD, HD), HD), :]
    lower = lax.broadcasted_iota(jnp.int32, (HD, 128), 1) < HD
    tiles = []
    for j in range(5):
        even = w_out[:, pl.ds(pl.multiple_of(table[context, 14 + 2 * j] * 128, 128), 128)]
        odd = w_out[:, pl.ds(pl.multiple_of(table[context, 15 + 2 * j] * 128, 128), 128)]
        tiles.append(jnp.where(lower, even, odd))
    message[:, :D] = rows
    for j in range(5):
        message[:, D + j * 128 : D + (j + 1) * 128] = tiles[j]
    lower = lax.broadcasted_iota(jnp.int32, (1, 128), 1) < HD
    for j in range(7):
        even = b_in[pl.ds(table[context, 24 + 2 * j], 1), :]
        odd = b_in[pl.ds(table[context, 25 + 2 * j], 1), :]
        bias[:, j * 128 : (j + 1) * 128] = jnp.where(lower, even, odd)


def project_kernel(ids, table, a0, b0, al, bl, ar, br, af, bf, *refs):
    near, far = refs[:8], refs[8:16]
    (bias, gain, shift, cosines, sines,
     hidden, xhat, weights_in, weights_out, qkv, slope, gated, held) = refs[16:]
    x, zl, core, context, y, zh = ids[0], ids[1], ids[2], ids[4], ids[5], ids[6]
    for step, first in enumerate((0, 4, 6, 2)):
        for piece, which in ((first, zh), (first + 1, 1 - zh)):
            pair = lax.rem(y + step, 4) * 2 + which
            held[2 * pair + core] = near[piece][:, :D]
            held[2 * pair + 1 - core] = far[piece][:, :D]
            weights_out[pl.ds(pl.multiple_of((2 * pair + core) * HD, HD), HD), :] = near[piece][:, D:]
            weights_out[pl.ds(pl.multiple_of((2 * pair + 1 - core) * HD, HD), HD), :] = far[piece][:, D:]
    for i in range(14):
        weights_in[i * HD : (i + 1) * HD, :] = held[table[context, i]]

    for step, (a, b) in enumerate(((a0, b0), (ar, br), (af, bf), (al, bl))):
        for piece, which in ((a, zl), (b, 1 - zl)):
            first = (lax.rem(x + step, 4) * 2 + which) * 128
            rows = pl.ds(pl.multiple_of(first, 128), 128)
            normed, _ = normal(piece[...].astype(F32))
            xhat[rows, :] = normed.astype(BF)
            hidden[rows, :] = (normed * gain[...] + shift[...]).astype(BF)

    @pl.loop(0, 4)
    def _(i):
        rows = pl.ds(pl.multiple_of(i * 256, 256), 256)
        proj = nt(hidden[rows, :], weights_in[...]) + bias[...]
        cos_rows, sin_rows = cosines[rows, :], sines[rows, :]
        qkv[rows, 0:128] = turn(proj[:, 0:128], cos_rows, sin_rows).astype(BF)
        qkv[rows, 128:256] = turn(proj[:, 128:256], cos_rows, sin_rows).astype(BF)
        qkv[rows, 256:384] = proj[:, 256:384].astype(BF)
        act = proj[:, 384:]
        square = act * act
        th = jnp.tanh(GELU_C * act * (1.0 + 0.044715 * square))
        half = 0.5 * (1.0 + th)
        gated[rows, :] = (act * half).astype(BF)
        slope[rows, :] = (
            half + 0.5 * act * (1.0 - th * th) * (GELU_C * (1.0 + 3 * 0.044715 * square))
        ).astype(BF)


def attend_kernel(ids, qkv, gated, weights_out, joined, lse, oa, ob, ra, rb, fa, fb, la, lb):
    x, zl = ids[0], ids[1]
    joined[:, 128:] = gated[...]
    keys, values = qkv[:, 128:256], qkv[:, 256:384]
    for head in range(2):
        k_head = head_mask(keys, head)
        v_head = head_mask(values, head)
        for block in range(SEQ // BLOCK):
            rows = pl.ds(block * BLOCK, BLOCK)
            scores = block_scores(qkv[rows, 0:128], k_head, block)
            largest = jnp.max(scores, axis=0, keepdims=True)
            raised = jnp.exp2(scores - largest)
            mass = jnp.sum(raised, axis=0, keepdims=True)
            lse[head : head + 1, block * BLOCK : (block + 1) * BLOCK] = largest + jnp.log2(mass)
            probs = (raised * (1.0 / mass)).astype(BF)
            result = tn(probs, v_head[: (block + 1) * BLOCK])
            if head == 0:
                joined[rows, 0:128] = result.astype(BF)
            else:
                joined[rows, 0:128] = (joined[rows, 0:128].astype(F32) + result).astype(BF)

    for step, a, b in ((2, fa, fb), (1, ra, rb), (3, la, lb), (0, oa, ob)):
        rows = pl.ds(pl.multiple_of(lax.rem(x + step, 4) * 256, 256), 256)
        place_pair(zl, nt(joined[rows, :], weights_out[...]).astype(BF), a, b)


def backward_out_kernel(ids, a0, b0, al, bl, ar, br, af, bf, weights_out, slope, joined,
                        grad_attn, grad_ff, near, far, grad_b_out, cot):
    x, zl, core = ids[0], ids[1], ids[2]
    for step, (a, b) in enumerate(((a0, b0), (ar, br), (af, bf), (al, bl))):
        for piece, which in ((a, zl), (b, 1 - zl)):
            first = (lax.rem(x + step, 4) * 2 + which) * 128
            cot[pl.ds(pl.multiple_of(first, 128), 128), :] = piece[...]
    grad_b_out[...] = jnp.zeros_like(grad_b_out)

    @pl.loop(0, 4)
    def _(i):
        rows = pl.ds(pl.multiple_of(i * 256, 256), 256)
        grad = nn(cot[rows, :], weights_out[...])
        grad_attn[rows, :] = grad[:, :128].astype(BF)
        grad_ff[rows, :] = (grad[:, 128:] * slope[rows, :].astype(F32)).astype(BF)
        grad_b_out[0:1, :] += jnp.sum(cot[rows, :].astype(F32), axis=0, keepdims=True)

    for i in range(4):
        grad = tn(cot[:, i * 256 : (i + 1) * 256], joined[...]).astype(BF)
        for j in (0, 1):
            pair = grad[j * 128 : (j + 1) * 128]

            @pl.when(core == 0)
            def _():
                near[2 * i + j, :, :] = pair[:HD]
                far[2 * i + j, :, :] = pair[HD:]

            @pl.when(core != 0)
            def _():
                near[2 * i + j, :, :] = pair[HD:]
                far[2 * i + j, :, :] = pair[:HD]


def backward_in_kernel(ids, table, qkv, lse, grad_attn, grad_ff, weights_in, hidden, xhat, cosines, sines,
                       near, far, oa, ob, ra, rb, fa, fb, la, lb, grad_bias, small,
                       grad_proj, grad_q, grad_k, grad_v):
    x, zl, core, context = ids[0], ids[1], ids[2], ids[4]
    keys, values = qkv[:, 128:256], qkv[:, 256:384]
    grad_k[...] = jnp.zeros_like(grad_k)
    grad_v[...] = jnp.zeros_like(grad_v)
    for head in range(2):
        k_head = head_mask(keys, head)
        v_head = head_mask(values, head)
        for block in range(SEQ // BLOCK):
            rows = pl.ds(block * BLOCK, BLOCK)
            extent = (block + 1) * BLOCK
            scores = block_scores(qkv[rows, 0:128], k_head, block)
            probs = jnp.exp2(scores - lse[head : head + 1, block * BLOCK : (block + 1) * BLOCK])
            grad_out = grad_attn[rows, :]
            grad_probs = nt(v_head[:extent], grad_out)
            delta = jnp.sum(grad_probs * probs, axis=0, keepdims=True)
            grad_scores = (probs * (grad_probs - delta)).astype(BF)
            grad_v[:extent, :] += nn(probs.astype(BF), head_mask(grad_out, head))
            grad_k[:extent, :] += nn(grad_scores, head_mask(qkv[rows, 0:128], head))
            result = tn(grad_scores, k_head[:extent])
            if head == 0:
                grad_q[rows, :] = result
            else:
                grad_q[rows, :] += result
    scale = HD ** (-0.5)
    cos_all, sin_all = cosines[...], -sines[...]
    grad_proj[:, 0:128] = turn((grad_q[...] * scale).astype(BF).astype(F32), cos_all, sin_all).astype(BF)
    grad_proj[:, 128:256] = turn((grad_k[...] * scale).astype(BF).astype(F32), cos_all, sin_all).astype(BF)
    grad_proj[:, 256:384] = grad_v[...].astype(BF)
    grad_proj[:, 384:] = grad_ff[...]

    for row in range(8):
        near[row, :, :] = jnp.zeros((HD, D), BF)
        far[row, :, :] = jnp.zeros((HD, D), BF)
    for i in range(7):
        grad = tn(grad_proj[:, i * 128 : (i + 1) * 128], hidden[...]).astype(BF)
        for j in (0, 1):
            slot = table[context, 2 * i + j]
            row, odd = slot // 2, slot % 2

            @pl.when(odd == core)
            def _():
                near[row, :, :] = grad[j * HD : (j + 1) * HD]

            @pl.when(odd != core)
            def _():
                far[row, :, :] = grad[j * HD : (j + 1) * HD]

    small[...] = jnp.zeros_like(small)
    grad_bias[...] = jnp.zeros_like(grad_bias)
    for step, a, b in ((2, fa, fb), (1, ra, rb), (3, la, lb), (0, oa, ob)):
        rows = pl.ds(pl.multiple_of(lax.rem(x + step, 4) * 256, 256), 256)
        proj = grad_proj[rows, :]
        grad = nn(proj, weights_in[...])
        place_pair(zl, grad.astype(BF), a, b)
        small[0:1, :] += jnp.sum(grad * xhat[rows, :].astype(F32), axis=0, keepdims=True)
        small[1:2, :] += jnp.sum(grad, axis=0, keepdims=True)
        grad_bias[0:1, :] += jnp.sum(proj.astype(F32), axis=0, keepdims=True)


def finish_out_kernel(oa, ra, la, far, inputs, b_out, out):
    mixed = (oa[...].astype(F32) + ra[...].astype(F32)) + (la[...].astype(F32) + far[...].astype(F32))
    out[...] = (inputs[...].astype(F32) + mixed + b_out[...]).astype(BF)


def finish_in_kernel(oa, ra, la, far, inputs, cotangent, gain, grad_inputs):
    grad = (oa[...].astype(F32) + ra[...].astype(F32)) + (la[...].astype(F32) + far[...].astype(F32))
    own, scale = normal(inputs[...].astype(F32))
    pulled = grad * gain[...]
    rows = (
        pulled
        - jnp.mean(pulled, axis=-1, keepdims=True)
        - own * jnp.mean(pulled * own, axis=-1, keepdims=True)
    ) * scale
    grad_inputs[...] = (cotangent[...].astype(F32) + rows).astype(BF)


def finish_weights_kernel(ids, shard_table, a0, b0, al, bl, ar, br, af, bf, grad_w_in, grad_w_out, held):
    x, zl, shard = ids[0], ids[1], ids[3]
    for step, (a, b) in enumerate(((a0, b0), (ar, br), (af, bf), (al, bl))):
        for piece, which in ((a, zl), (b, 1 - zl)):
            held[lax.rem(x + step, 4) * 2 + which] = piece[...]
    for i in range(7):
        grad_w_in[i * HD : (i + 1) * HD, :] = held[shard_table[shard, 8 + i], :, :D].astype(F32)
    lower = lax.broadcasted_iota(jnp.int32, (HD, 128), 1) < HD
    for t in range(40):
        tiles = []
        for unit in (2 * t, 2 * t + 1):
            c, i = (int(n) for n in COLUMN_HOME[unit])
            first = D + (i // 2) * 128
            tiles.append(held[c, :, first : first + 128].astype(F32))
        grad_w_out[:, t * 128 : (t + 1) * 128] = jnp.where(lower, *tiles)


VM = pl.BlockSpec(memory_space=pltpu.VMEM)
SM = pl.BlockSpec(memory_space=pltpu.SMEM)
S = jax.ShapeDtypeStruct


def kernel(body, outs, scalars, operands, name, us, scratch=()):
    return pl.pallas_call(
        body,
        out_shape=outs,
        in_specs=[SM] * len(scalars) + [VM] * len(operands),
        out_specs=jax.tree.map(lambda _: VM, outs),
        scratch_shapes=list(scratch),
        compiler_params=pltpu.CompilerParams(vmem_limit_bytes=56 * MIB),
        cost_estimate=pl.CostEstimate(flops=int(us * 1e9), bytes_accessed=int(us * 3e6), transcendentals=0),
        name=name,
    )(*scalars, *operands)


def shift(values, axis, by):
    count = 4
    return lax.ppermute(values, axis, [(i, (i + by) % count) for i in range(count)])


def swap(values, axis):
    return lax.ppermute(values, axis, [(0, 1), (1, 0)])


def gather_ring(own, ring, pair):
    partner = swap(own, pair)
    al, ar = shift(own, ring, 1), shift(own, ring, -1)
    bl, br = shift(partner, ring, 1), shift(partner, ring, -1)
    af, bf = shift(al, ring, 1), shift(br, ring, -1)
    return own, partner, al, bl, ar, br, af, bf


def gather_context(own):
    return gather_ring(own, "x", "zl")


def add(*terms):
    return sum(term.astype(F32) for term in terms).astype(BF)


def scatter_context(oa, ob, ra, rb, fa, fb, la, lb):
    fb = shift(fb, "x", -1)
    rb = shift(rb, "x", 1)
    fa = shift(fa, "x", 1)
    lb = shift(add(lb, fb), "x", -1)
    ra = shift(add(ra, fa), "x", 1)
    la = shift(la, "x", -1)
    ob = add(ob, rb, lb)
    return oa, ra, la, swap(ob, "zl")


def scatter_shard(near, far):
    near = add(near, swap(far, "core"))
    arrived = lax.all_to_all(near, ("y", "zh"), 0, 0, tiled=True)
    return jnp.sum(arrived.astype(F32), axis=0).astype(BF)


def spread(values, axes, count):
    copies = jnp.broadcast_to(values[None], (count,) + values.shape)
    return lax.all_to_all(copies, axes, 0, 0, tiled=True)


def turn_tables():
    steps = np.arange(ROT // 2)
    angles = np.arange(SEQ)[:, None] * (10000.0 ** (-2.0 * steps / ROT))[None, :]
    cosine, sine = np.cos(angles), np.sin(angles)
    still = np.ones((SEQ, HD - ROT))
    cosines = np.concatenate([cosine, cosine, still] * 2, axis=1)
    sines = np.concatenate([-sine, sine, 0.0 * still] * 2, axis=1)
    return jnp.asarray(cosines.astype(np.float32)), jnp.asarray(sines.astype(np.float32))


def on_device(inputs, ln_gain, ln_bias, w_in, b_in, w_out, b_out, cotangent):
    ids = jnp.stack(
        [lax.axis_index(axes) for axes in ("x", "zl", "core", SHARD, CONTEXT, "y", "zh")]
    ).astype(jnp.int32)
    table, shard_table = jnp.asarray(TABLE), jnp.asarray(SHARD_TABLE)
    cosines, sines = turn_tables()
    gain, shift_row = ln_gain[None], ln_bias[None]

    tokens = gather_context(inputs)
    message, bias = kernel(
        prepare_kernel, (S((HD, 1664), BF), S((1, 896), F32)), (ids, table, shard_table),
        (w_in, w_out, b_in.reshape(56, 128)), "prepare", 2,
    )
    near = gather_ring(message, "y", "zh")
    far = [swap(piece, "core") for piece in near]
    cots = gather_context(lax.optimization_barrier((cotangent, tokens[2], tokens[5]))[0])

    chunk = S((128, D), BF)
    hidden, xhat, weights_in, weights_out, qkv, slope, gated = kernel(
        project_kernel,
        (S((SEQ, D), BF), S((SEQ, D), BF), S((896, D), BF), S((D, 640), BF), S((SEQ, 384), BF),
         S((SEQ, 512), BF), S((SEQ, 512), BF)),
        (ids, table), (*tokens, *near, *far, bias, gain, shift_row, cosines, sines), "project", 10,
        [pltpu.VMEM((16, HD, D), BF)],
    )
    joined, lse, *parts = kernel(
        attend_kernel, (S((SEQ, 640), BF), S((8, SEQ), F32)) + (chunk,) * 8,
        (ids,), (qkv, gated, weights_out), "attend", 8,
    )
    terms = scatter_context(*parts)
    out = kernel(finish_out_kernel, chunk, (), (*terms, inputs, b_out[None]), "finish_out", 2)

    slots = lambda columns: S((8, HD, columns), BF)
    grad_attn, grad_ff, near_out, far_out, grad_b_out = kernel(
        backward_out_kernel,
        (S((SEQ, 128), BF), S((SEQ, 512), BF), slots(640), slots(640), S((8, D), F32)),
        (ids,), (*cots, weights_out, slope, joined), "backward_out", 9, [pltpu.VMEM((SEQ, D), BF)],
    )
    grad_w_out = scatter_shard(near_out, far_out)

    near_in, far_in, *parts, grad_bias, small = kernel(
        backward_in_kernel,
        (slots(D), slots(D)) + (chunk,) * 8 + (S((8, 896), F32), S((8, D), F32)),
        (ids, table), (qkv, lse, grad_attn, grad_ff, weights_in, hidden, xhat, cosines, sines), "backward_in", 17,
        [pltpu.VMEM((SEQ, 896), BF)] + [pltpu.VMEM((SEQ, 128), F32)] * 3,
    )
    grad_w_in = scatter_shard(near_in, far_in)
    terms = scatter_context(*parts)
    grad_inputs = kernel(finish_in_kernel, chunk, (), (*terms, inputs, cotangent, gain), "finish_in", 2)

    pieces = gather_context(jnp.concatenate([grad_w_in, grad_w_out], axis=1))
    grad_w_in, grad_w_out = kernel(
        finish_weights_kernel, (S((448, D), F32), S((HD, 5120), F32)), (ids, shard_table), pieces, "finish_weights", 3,
        [pltpu.VMEM((8, HD, 1664), BF)],
    )

    vectors = jnp.concatenate([grad_bias[0], small[0], small[1], grad_b_out[0]]).reshape(31, 128)
    vectors = jnp.sum(spread(vectors, SHARD, 16).reshape(16, 31, 128), axis=0)
    vectors = spread(vectors, CONTEXT, 8).reshape(8, 31 * 128)
    grad_b_in = vectors[:, :896].reshape(112, 64)[HOME[:, 0] * 14 + HOME[:, 1]].reshape(7168)
    grad_gain = jnp.sum(vectors[:, 896 : 896 + D], axis=0)
    grad_shift = jnp.sum(vectors[:, 896 + D : 896 + 2 * D], axis=0)
    return (out, grad_inputs, grad_gain, grad_shift, grad_w_in, grad_b_in, grad_w_out, vectors[0, 896 + 2 * D :])


def solution(mesh):
    fine = Mesh(mesh.devices.reshape(4, 2, 2, 4, 2), SHARD + CONTEXT)
    rows = P(SHARD + CONTEXT, None)
    in_specs = (rows, P(), P(), P(SHARD, None), P(), P(SHARD, None), P(), rows)
    out_specs = (rows, rows, P(), P(), P(SHARD, None), P(), P(SHARD, None), P())
    return jax.shard_map(on_device, mesh=fine, in_specs=in_specs, out_specs=out_specs, check_vma=False)
```

```python
import functools
import math

import jax
import jax.numpy as jnp
import numpy as np
from jax import lax
from jax.experimental import pallas as pl
from jax.experimental.pallas import tpu as pltpu
from jax.sharding import Mesh
from jax.sharding import PartitionSpec as P

D = 1024
FF = 4096
H = 16
HD = 64
ROT = 32
SEQ = 1024
EPS = 1e-05
BF = jnp.bfloat16
F32 = jnp.float32
MIB = 1 << 20

SHARD = ("y", "zh", "core")
CONTEXT = ("x", "zl")

HEADS = ((0, 7), (8, 1), (14, 9), (6, 15), (12, 5), (4, 13), (10, 3), (2, 11))
UNITS_PER_SHARD = 7


def deal_units():
    columns = [[[], []] for _ in range(8)]
    qkv = [[kind * H + head for kind in range(3) for head in pair] for pair in HEADS]
    taken = [{unit // UNITS_PER_SHARD for unit in units} for units in qkv]
    order = []

    def place(unit):
        if unit == 112:
            return True
        shard, parity = unit // UNITS_PER_SHARD, unit % 2
        choices = sorted(range(8), key=lambda c: len(columns[c][0]) + len(columns[c][1]))
        for c in choices:
            if shard in taken[c] or len(columns[c][parity]) == 4:
                continue
            taken[c].add(shard)
            columns[c][parity].append(unit)
            if place(unit + 1):
                return True
            taken[c].remove(shard)
            columns[c][parity].pop()
        return False

    assert place(48)
    for c in range(8):
        pairs = [unit for pair in zip(*columns[c]) for unit in pair]
        order.append(qkv[c] + pairs)
    return np.array(order, np.int32)


UNITS = deal_units()
SLOT = UNITS // UNITS_PER_SHARD
SEND = np.zeros((16, 8), np.int32)
for _c in range(8):
    for _u in UNITS[_c]:
        SEND[_u // UNITS_PER_SHARD, _c] = _u % UNITS_PER_SHARD
HOME = np.zeros((112, 2), np.int32)
for _c in range(8):
    for _i, _u in enumerate(UNITS[_c]):
        HOME[_u] = (_c, _i)
COLUMN_UNITS = np.concatenate([np.array(HEADS, np.int32), UNITS[:, 6:] - 32], axis=1)
COLUMN_HOME = np.zeros((80, 2), np.int32)
for _c in range(8):
    for _i, _u in enumerate(COLUMN_UNITS[_c]):
        COLUMN_HOME[_u] = (_c, _i)


TABLE = np.concatenate([SLOT, COLUMN_UNITS // 2, UNITS // 2], axis=1).astype(np.int32)
SHARD_TABLE = np.concatenate([SEND, HOME[:, 0].reshape(16, 7)], axis=1).astype(np.int32)

def nn(left, right):
    return lax.dot_general(left, right, (((1,), (0,)), ((), ())), preferred_element_type=F32)


def nt(left, right):
    return lax.dot_general(left, right, (((1,), (1,)), ((), ())), preferred_element_type=F32)


def tn(left, right):
    return lax.dot_general(left, right, (((0,), (0,)), ((), ())), preferred_element_type=F32)


def normal(rows):
    average = jnp.mean(rows, axis=-1, keepdims=True)
    centred = rows - average
    variance = jnp.mean(centred * centred, axis=-1, keepdims=True)
    scale = lax.rsqrt(variance + EPS)
    return centred * scale, scale


def turn(values, cosines, sines):
    lane = lax.broadcasted_iota(jnp.int32, values.shape, 1) % HD
    ahead = pltpu.roll(values, 2 * HD - ROT // 2, 1)
    behind = pltpu.roll(values, ROT // 2, 1)
    return values * cosines + jnp.where(lane < ROT // 2, ahead, behind) * sines


def head_mask(values, head):
    lane = lax.broadcasted_iota(jnp.int32, values.shape, 1)
    return jnp.where((lane // HD) == head, values, jnp.zeros_like(values))


SCALE2 = HD ** (-0.5) * math.log2(math.e)
GELU_C = math.sqrt(2.0 / math.pi)
BLOCK = 256


def causal(shape, first_key, first_query):
    key = first_key + lax.broadcasted_iota(jnp.int32, shape, 0)
    query = first_query + lax.broadcasted_iota(jnp.int32, shape, 1)
    return key <= query


def block_scores(q_block, k_head, block):
    extent = (block + 1) * BLOCK
    scores = nt(k_head[:extent], q_block) * SCALE2
    last = scores[block * BLOCK:]
    last = jnp.where(causal(last.shape, 0, 0), last, -1e30)
    if block == 0:
        return last
    return jnp.concatenate([scores[: block * BLOCK], last], axis=0)


def place_pair(zl, pair, a, b):
    @pl.when(zl == 0)
    def _():
        a[...] = pair[:128]
        b[...] = pair[128:]

    @pl.when(zl != 0)
    def _():
        a[...] = pair[128:]
        b[...] = pair[:128]


def prepare_kernel(ids, table, shard_table, w_in, w_out, b_in, message, bias):
    shard, context = ids[3], ids[4]
    unit = shard_table[shard, context]
    rows = w_in[pl.ds(pl.multiple_of(unit * HD, HD), HD), :]
    lower = lax.broadcasted_iota(jnp.int32, (HD, 128), 1) < HD
    tiles = []
    for j in range(5):
        even = w_out[:, pl.ds(pl.multiple_of(table[context, 14 + 2 * j] * 128, 128), 128)]
        odd = w_out[:, pl.ds(pl.multiple_of(table[context, 15 + 2 * j] * 128, 128), 128)]
        tiles.append(jnp.where(lower, even, odd))
    message[:, :D] = rows
    for j in range(5):
        message[:, D + j * 128 : D + (j + 1) * 128] = tiles[j]
    lower = lax.broadcasted_iota(jnp.int32, (1, 128), 1) < HD
    for j in range(7):
        even = b_in[pl.ds(table[context, 24 + 2 * j], 1), :]
        odd = b_in[pl.ds(table[context, 25 + 2 * j], 1), :]
        bias[:, j * 128 : (j + 1) * 128] = jnp.where(lower, even, odd)


def project_kernel(ids, table, a0, b0, al, bl, ar, br, af, bf, *refs):
    near, far = refs[:8], refs[8:16]
    (bias, gain, shift, cosines, sines,
     hidden, xhat, weights, weights_out, qkv, slope, gated, held) = refs[16:]
    x, zl, core, context, y, zh = ids[0], ids[1], ids[2], ids[4], ids[5], ids[6]
    for step, first in enumerate((0, 4, 6, 2)):
        for piece, which in ((first, zh), (first + 1, 1 - zh)):
            pair = lax.rem(y + step, 4) * 2 + which
            held[2 * pair + core] = near[piece][:, :D]
            held[2 * pair + 1 - core] = far[piece][:, :D]
            weights_out[pl.ds(pl.multiple_of((2 * pair + core) * HD, HD), HD), :] = near[piece][:, D:]
            weights_out[pl.ds(pl.multiple_of((2 * pair + 1 - core) * HD, HD), HD), :] = far[piece][:, D:]
    for i in range(14):
        weights[i * HD : (i + 1) * HD, :] = held[table[context, i]]

    for step, (a, b) in enumerate(((a0, b0), (ar, br), (af, bf), (al, bl))):
        for piece, which in ((a, zl), (b, 1 - zl)):
            first = (lax.rem(x + step, 4) * 2 + which) * 128
            rows = pl.ds(pl.multiple_of(first, 128), 128)
            normed, _ = normal(piece[...].astype(F32))
            xhat[rows, :] = normed.astype(BF)
            hidden[rows, :] = (normed * gain[...] + shift[...]).astype(BF)

    @pl.loop(0, 4)
    def _(i):
        rows = pl.ds(pl.multiple_of(i * 256, 256), 256)
        proj = nt(hidden[rows, :], weights[...]) + bias[...]
        cos_rows, sin_rows = cosines[rows, :], sines[rows, :]
        qkv[rows, 0:128] = turn(proj[:, 0:128], cos_rows, sin_rows).astype(BF)
        qkv[rows, 128:256] = turn(proj[:, 128:256], cos_rows, sin_rows).astype(BF)
        qkv[rows, 256:384] = proj[:, 256:384].astype(BF)
        act = proj[:, 384:]
        square = act * act
        th = jnp.tanh(GELU_C * act * (1.0 + 0.044715 * square))
        half = 0.5 * (1.0 + th)
        gated[rows, :] = (act * half).astype(BF)
        slope[rows, :] = (
            half + 0.5 * act * (1.0 - th * th) * (GELU_C * (1.0 + 3 * 0.044715 * square))
        ).astype(BF)


def attend_kernel(qkv, gated, joined, lse):
    joined[:, 128:] = gated[...]
    keys, values = qkv[:, 128:256], qkv[:, 256:384]
    for head in range(2):
        k_head = head_mask(keys, head)
        v_head = head_mask(values, head)
        for block in range(SEQ // BLOCK):
            rows = pl.ds(block * BLOCK, BLOCK)
            scores = block_scores(qkv[rows, 0:128], k_head, block)
            largest = jnp.max(scores, axis=0, keepdims=True)
            raised = jnp.exp2(scores - largest)
            mass = jnp.sum(raised, axis=0, keepdims=True)
            lse[head : head + 1, block * BLOCK : (block + 1) * BLOCK] = largest + jnp.log2(mass)
            probs = (raised * (1.0 / mass)).astype(BF)
            result = tn(probs, v_head[: (block + 1) * BLOCK])
            if head == 0:
                joined[rows, 0:128] = result.astype(BF)
            else:
                joined[rows, 0:128] = (joined[rows, 0:128].astype(F32) + result).astype(BF)


def project_out_kernel(ids, joined, weights, oa, ob, ra, rb, fa, fb, la, lb):
    x, zl = ids[0], ids[1]
    for step, a, b in ((2, fa, fb), (1, ra, rb), (3, la, lb), (0, oa, ob)):
        rows = pl.ds(pl.multiple_of(lax.rem(x + step, 4) * 256, 256), 256)
        place_pair(zl, nt(joined[rows, :], weights[...]).astype(BF), a, b)


def backward_out_kernel(ids, a0, b0, al, bl, ar, br, af, bf, weights_out, slope, joined,
                        grad_attn, grad_ff, near, far, grad_b_out, cot):
    x, zl, core = ids[0], ids[1], ids[2]
    for step, (a, b) in enumerate(((a0, b0), (ar, br), (af, bf), (al, bl))):
        for piece, which in ((a, zl), (b, 1 - zl)):
            first = (lax.rem(x + step, 4) * 2 + which) * 128
            cot[pl.ds(pl.multiple_of(first, 128), 128), :] = piece[...]
    grad_b_out[...] = jnp.broadcast_to(jnp.sum(a0[...].astype(F32), axis=0, keepdims=True), grad_b_out.shape)

    @pl.loop(0, 4)
    def _(i):
        rows = pl.ds(pl.multiple_of(i * 256, 256), 256)
        grad = nn(cot[rows, :], weights_out[...])
        grad_attn[rows, :] = grad[:, :128].astype(BF)
        grad_ff[rows, :] = (grad[:, 128:] * slope[rows, :].astype(F32)).astype(BF)

    for i in range(4):
        grad = tn(cot[:, i * 256 : (i + 1) * 256], joined[...]).astype(BF)
        for j in (0, 1):
            pair = grad[j * 128 : (j + 1) * 128]

            @pl.when(core == 0)
            def _():
                near[2 * i + j, :, :] = pair[:HD]
                far[2 * i + j, :, :] = pair[HD:]

            @pl.when(core != 0)
            def _():
                near[2 * i + j, :, :] = pair[HD:]
                far[2 * i + j, :, :] = pair[:HD]


def backward_attend_kernel(qkv, lse, grad_attn, grad_ff, cosines, sines, grad_proj, grad_q, grad_k, grad_v):
    keys, values = qkv[:, 128:256], qkv[:, 256:384]
    grad_k[...] = jnp.zeros_like(grad_k)
    grad_v[...] = jnp.zeros_like(grad_v)
    for head in range(2):
        k_head = head_mask(keys, head)
        v_head = head_mask(values, head)
        for block in range(SEQ // BLOCK):
            rows = pl.ds(block * BLOCK, BLOCK)
            extent = (block + 1) * BLOCK
            scores = block_scores(qkv[rows, 0:128], k_head, block)
            probs = jnp.exp2(scores - lse[head : head + 1, block * BLOCK : (block + 1) * BLOCK])
            grad_out = grad_attn[rows, :]
            grad_probs = nt(v_head[:extent], grad_out)
            delta = jnp.sum(grad_probs * probs, axis=0, keepdims=True)
            grad_scores = (probs * (grad_probs - delta)).astype(BF)
            grad_v[:extent, :] += nn(probs.astype(BF), head_mask(grad_out, head))
            grad_k[:extent, :] += nn(grad_scores, head_mask(qkv[rows, 0:128], head))
            result = tn(grad_scores, k_head[:extent])
            if head == 0:
                grad_q[rows, :] = result
            else:
                grad_q[rows, :] += result
    scale = HD ** (-0.5)
    cos_all, sin_all = cosines[...], -sines[...]
    grad_proj[:, 0:128] = turn((grad_q[...] * scale).astype(BF).astype(F32), cos_all, sin_all).astype(BF)
    grad_proj[:, 128:256] = turn((grad_k[...] * scale).astype(BF).astype(F32), cos_all, sin_all).astype(BF)
    grad_proj[:, 256:384] = grad_v[...].astype(BF)
    grad_proj[:, 384:] = grad_ff[...]


def split(values):
    high = values.astype(BF)
    return high, (values - high.astype(F32)).astype(BF)


def backward_in_kernel(ids, table, grad_proj, weights, hidden, xhat, grad_b_out,
                       near, far, oa, ob, ra, rb, fa, fb, la, lb, vectors):
    x, zl, core, context = ids[0], ids[1], ids[2], ids[4]
    grad_gain, grad_shift, grad_bias = (jnp.zeros((1, n), F32) for n in (D, D, 896))
    for step, a, b in ((2, fa, fb), (1, ra, rb), (3, la, lb), (0, oa, ob)):
        rows = pl.ds(pl.multiple_of(lax.rem(x + step, 4) * 256, 256), 256)
        proj = grad_proj[rows, :]
        grad = nn(proj, weights[...])
        place_pair(zl, grad.astype(BF), a, b)
        grad_gain += jnp.sum(grad * xhat[rows, :].astype(F32), axis=0, keepdims=True)
        grad_shift += jnp.sum(grad, axis=0, keepdims=True)
        grad_bias += jnp.sum(proj.astype(F32), axis=0, keepdims=True)
    for j in range(8):
        lanes = slice(j * 128, (j + 1) * 128)
        vectors[j : j + 1, :] = grad_gain[:, lanes]
        vectors[8 + j : 9 + j, :] = grad_shift[:, lanes]
        vectors[16 + j : 17 + j, :] = grad_b_out[0:1, lanes]
        vectors[24 + j : 25 + j, :] = grad_bias[:, lanes] if j < 7 else jnp.zeros((1, 128), F32)
    high, low = split(vectors[...])
    for row in range(8):
        near[row, :, :D] = jnp.zeros((HD, D), BF)
        far[row, :, :D] = jnp.zeros((HD, D), BF)
        for ref in (near, far):
            ref[row, :32, D:] = high
            ref[row, 32:, D:] = low
    for i in range(7):
        grad = tn(grad_proj[:, i * 128 : (i + 1) * 128], hidden[...]).astype(BF)
        for j in (0, 1):
            slot = table[context, 2 * i + j]
            row, odd = slot // 2, slot % 2

            @pl.when(odd == core)
            def _():
                near[row, :, :D] = grad[j * HD : (j + 1) * HD]

            @pl.when(odd != core)
            def _():
                far[row, :, :D] = grad[j * HD : (j + 1) * HD]


def add_slots_kernel(near, far, total):
    total[:, :, :D] = (near[:, :, :D].astype(F32) + far[:, :, :D].astype(F32)).astype(BF)
    vectors = sum(ref[0, rows, D:].astype(F32) for ref in (near, far) for rows in (slice(0, 32), slice(32, 64)))
    high, low = split(vectors)
    for row in range(8):
        total[row, :32, D:] = high
        total[row, 32:, D:] = low


def sum_slots_kernel(parts, total):
    total[:, :D] = jnp.sum(parts[:, :, :D].astype(F32), axis=0).astype(BF)
    high, low = split(jnp.sum(parts[:, :32, D:].astype(F32) + parts[:, 32:, D:].astype(F32), axis=0))
    total[:32, D:] = high
    total[32:, D:] = low


def finish_out_kernel(oa, ra, la, far, inputs, b_out, out):
    mixed = (oa[...].astype(F32) + ra[...].astype(F32)) + (la[...].astype(F32) + far[...].astype(F32))
    out[...] = (inputs[...].astype(F32) + mixed + b_out[...]).astype(BF)


def finish_in_kernel(oa, ra, la, far, inputs, cotangent, gain, grad_inputs):
    grad = (oa[...].astype(F32) + ra[...].astype(F32)) + (la[...].astype(F32) + far[...].astype(F32))
    own, scale = normal(inputs[...].astype(F32))
    pulled = grad * gain[...]
    rows = (
        pulled
        - jnp.mean(pulled, axis=-1, keepdims=True)
        - own * jnp.mean(pulled * own, axis=-1, keepdims=True)
    ) * scale
    grad_inputs[...] = (cotangent[...].astype(F32) + rows).astype(BF)


def hold_pieces(ids, pieces, held):
    x, zl = ids[0], ids[1]
    for step, first in enumerate((0, 4, 6, 2)):
        for piece, which in ((pieces[first], zl), (pieces[first + 1], 1 - zl)):
            held[lax.rem(x + step, 4) * 2 + which] = piece[...]


def finish_w_in_kernel(ids, shard_table, *refs):
    pieces, (grad_w_in, vectors, held) = refs[:8], refs[8:]
    hold_pieces(ids, pieces, held)
    for i in range(7):
        grad_w_in[i * HD : (i + 1) * HD, :] = held[shard_table[ids[3], 8 + i], :, :D].astype(F32)
    terms = [held[c, :32, D:].astype(F32) + held[c, 32:, D:].astype(F32) for c in range(8)]
    vectors[0:24, :] = sum(term[:24] for term in terms)
    lower = lax.broadcasted_iota(jnp.int32, (1, 128), 1) < HD
    for row in range(56):
        (c, i), (d, j) = (tuple(int(n) for n in HOME[unit]) for unit in (2 * row, 2 * row + 1))
        vectors[24 + row : 25 + row, :] = jnp.where(
            lower, terms[c][24 + i // 2 : 25 + i // 2], terms[d][24 + j // 2 : 25 + j // 2]
        )


def finish_w_out_kernel(ids, *refs):
    pieces, (grad_w_out, held) = refs[:8], refs[8:]
    hold_pieces(ids, pieces, held)
    lower = lax.broadcasted_iota(jnp.int32, (HD, 128), 1) < HD
    for t in range(40):
        tiles = []
        for unit in (2 * t, 2 * t + 1):
            c, i = (int(n) for n in COLUMN_HOME[unit])
            first = (i // 2) * 128
            tiles.append(held[c, :, first : first + 128].astype(F32))
        grad_w_out[:, t * 128 : (t + 1) * 128] = jnp.where(lower, *tiles)


VM = pl.BlockSpec(memory_space=pltpu.VMEM)
SM = pl.BlockSpec(memory_space=pltpu.SMEM)
S = jax.ShapeDtypeStruct


def kernel(body, outs, scalars, operands, name, us, scratch=()):
    return pl.pallas_call(
        body,
        out_shape=outs,
        in_specs=[SM] * len(scalars) + [VM] * len(operands),
        out_specs=jax.tree.map(lambda _: VM, outs),
        scratch_shapes=list(scratch),
        compiler_params=pltpu.CompilerParams(vmem_limit_bytes=56 * MIB),
        cost_estimate=pl.CostEstimate(flops=int(us * 1e9), bytes_accessed=int(us * 3e6), transcendentals=0),
        name=name,
    )(*scalars, *operands)


def shift(values, axis, by):
    count = 4
    return lax.ppermute(values, axis, [(i, (i + by) % count) for i in range(count)])


def swap(values, axis):
    return lax.ppermute(values, axis, [(0, 1), (1, 0)])


def gather_ring(own, ring, pair):
    partner = swap(own, pair)
    al, ar = shift(own, ring, 1), shift(own, ring, -1)
    bl, br = shift(partner, ring, 1), shift(partner, ring, -1)
    af, bf = shift(al, ring, 1), shift(br, ring, -1)
    return own, partner, al, bl, ar, br, af, bf


def gather_context(own):
    return gather_ring(own, "x", "zl")


def add(*terms):
    return sum(term.astype(F32) for term in terms).astype(BF)


def after(values, *events):
    return lax.optimization_barrier((values,) + events)


def turn_tables():
    steps = np.arange(ROT // 2)
    angles = np.arange(SEQ)[:, None] * (10000.0 ** (-2.0 * steps / ROT))[None, :]
    cosine, sine = np.cos(angles), np.sin(angles)
    still = np.ones((SEQ, HD - ROT))
    cosines = np.concatenate([cosine, cosine, still] * 2, axis=1)
    sines = np.concatenate([-sine, sine, 0.0 * still] * 2, axis=1)
    return jnp.asarray(cosines.astype(np.float32)), jnp.asarray(sines.astype(np.float32))


def on_device(inputs, ln_gain, ln_bias, w_in, b_in, w_out, b_out, cotangent):
    ids = jnp.stack(
        [lax.axis_index(axes) for axes in ("x", "zl", "core", SHARD, CONTEXT, "y", "zh")]
    ).astype(jnp.int32)
    table, shard_table = jnp.asarray(TABLE), jnp.asarray(SHARD_TABLE)
    cosines, sines = turn_tables()
    gain, shift_row = ln_gain[None], ln_bias[None]

    message, bias = kernel(
        prepare_kernel, (S((HD, 1664), BF), S((1, 896), F32)), (ids, table, shard_table),
        (w_in, w_out, b_in.reshape(56, 128)), "prepare", 2,
    )
    right, left = lambda v: shift(v, "x", 1), lambda v: shift(v, "x", -1)
    up, down = lambda v: shift(v, "y", 1), lambda v: shift(v, "y", -1)
    b0, al, ar = swap(inputs, "zl"), right(inputs), left(inputs)
    message, b0 = after(message, b0)
    wb, wal, war = swap(message, "zh"), up(message), down(message)
    bl, br = right(b0), left(b0)
    wb, al, ar = after(wb, al, ar)
    af = right(al)
    wbl, wbr = up(wb), down(wb)
    wal, war, br = after(wal, war, br)
    bf, waf = left(br), up(wal)
    wbr, waf = after(wbr, waf)
    wbf = down(wbr)
    near = [message, wb, wal, wbl, war, wbr, waf, wbf]
    far = [swap(piece, "core") for piece in near]
    cotangent, af, bl = after(cotangent, af, bl)
    cb, cal, car = swap(cotangent, "zl"), right(cotangent), left(cotangent)

    chunk = S((128, D), BF)
    hidden, xhat, weights_in, weights_out, qkv, slope, gated = kernel(
        project_kernel,
        (S((SEQ, D), BF), S((SEQ, D), BF), S((896, D), BF), S((D, 640), BF), S((SEQ, 384), BF),
         S((SEQ, 512), BF), S((SEQ, 512), BF)),
        (ids, table), (inputs, b0, al, bl, ar, br, af, bf, *near, *far, bias, gain, shift_row, cosines, sines),
        "project", 11, [pltpu.VMEM((16, HD, D), BF)],
    )
    qkv, cb, cal, car = after(qkv, cb, cal, car)
    cbl, cbr, caf = right(cb), left(cb), right(cal)
    joined, lse = kernel(attend_kernel, (S((SEQ, 640), BF), S((8, SEQ), F32)), (), (qkv, gated), "attend", 5)
    joined, cbl, cbr, caf = after(joined, cbl, cbr, caf)
    cbf = left(cbr)
    oa, ob, ra, rb, fa, fb, la, lb = kernel(
        project_out_kernel, (chunk,) * 8, (ids,), (joined, weights_out), "project_out", 4
    )
    fa, fb, rb, la = right(fa), left(fb), right(rb), left(la)

    slots = lambda columns: S((8, HD, columns), BF)
    grad_attn, grad_ff, near_out, far_out, grad_b_out = kernel(
        backward_out_kernel,
        (S((SEQ, 128), BF), S((SEQ, 512), BF), slots(640), slots(640), S((8, D), F32)),
        (ids,), (cotangent, cb, cal, cbl, car, cbr, caf, cbf, weights_out, slope, joined), "backward_out", 9,
        [pltpu.VMEM((SEQ, D), BF)],
    )
    far_out = swap(far_out, "core")
    grad_attn, fa, fb, rb, la = after(grad_attn, fa, fb, rb, la)
    ra, lb = right(add(ra, fa)), left(add(lb, fb))

    grad_proj = kernel(
        backward_attend_kernel, S((SEQ, 896), BF), (), (qkv, lse, grad_attn, grad_ff, cosines, sines),
        "backward_attend", 8, [pltpu.VMEM((SEQ, 128), F32)] * 3,
    )
    grad_proj, ra, lb, far_out = after(grad_proj, ra, lb, far_out)
    ob = swap(add(ob, rb, lb), "zl")
    near_out = lax.all_to_all(add(near_out, far_out), ("y", "zh"), 0, 0, tiled=True)

    near_in, far_in, goa, gob, gra, grb, gfa, gfb, gla, glb = kernel(
        backward_in_kernel, (slots(D + 128), slots(D + 128)) + (chunk,) * 8, (ids, table),
        (grad_proj, weights_in, hidden, xhat, grad_b_out), "backward_in", 10, [pltpu.VMEM((32, 128), F32)],
    )
    far_in, ob, near_out = after(far_in, ob, near_out)
    far_in = swap(far_in, "core")
    gfa, gfb, grb, gla = right(gfa), left(gfb), right(grb), left(gla)
    near_in = kernel(add_slots_kernel, slots(D + 128), (), (near_in, far_in), "add_slots", 2)
    near_in = lax.all_to_all(near_in, ("y", "zh"), 0, 0, tiled=True)

    part, gfa, gfb = after(add(*near_out), gfa, gfb)
    gra, glb = right(add(gra, gfa)), left(add(glb, gfb))
    pb, pal, par = swap(part, "zl"), right(part), left(part)
    pb, glb = after(pb, glb)
    gob = swap(add(gob, grb, glb), "zl")
    pbl, pbr, paf = right(pb), left(pb), right(pal)
    out = kernel(finish_out_kernel, chunk, (), (oa, ra, la, ob, inputs, b_out[None]), "finish_out", 2)
    pbr, out = after(pbr, out)
    pbf = left(pbr)

    near_in, pbl, paf, gob = after(near_in, pbl, paf, gob)
    slot = kernel(sum_slots_kernel, S((HD, D + 128), BF), (), (near_in,), "sum_slots", 2)
    pieces = gather_context(slot)
    grad_inputs = kernel(finish_in_kernel, chunk, (), (goa, gra, gla, gob, inputs, cotangent, gain), "finish_in", 3)
    grad_w_out = kernel(
        finish_w_out_kernel, S((HD, 5120), F32), (ids,), (part, pb, pal, pbl, par, pbr, paf, pbf),
        "finish_w_out", 3, [pltpu.VMEM((8, HD, 640), BF)],
    )
    grad_w_in, vectors = kernel(
        finish_w_in_kernel, (S((448, D), F32), S((80, 128), F32)), (ids, shard_table), pieces,
        "finish_w_in", 3, [pltpu.VMEM((8, HD, D + 128), BF)],
    )
    grad_gain, grad_shift, grad_b_out, grad_b_in = (
        vectors[first : first + rows].reshape(rows * 128) for first, rows in ((0, 8), (8, 8), (16, 8), (24, 56))
    )
    return (out, grad_inputs, grad_gain, grad_shift, grad_w_in, grad_b_in, grad_w_out, grad_b_out)


def solution(mesh):
    fine = Mesh(mesh.devices.reshape(4, 2, 2, 4, 2), SHARD + CONTEXT)
    rows = P(SHARD + CONTEXT, None)
    in_specs = (rows, P(), P(), P(SHARD, None), P(), P(SHARD, None), P(), rows)
    out_specs = (rows, rows, P(), P(), P(SHARD, None), P(), P(SHARD, None), P())
    return jax.shard_map(on_device, mesh=fine, in_specs=in_specs, out_specs=out_specs, check_vma=False)
```

```python
import functools
import math

import jax
import jax.numpy as jnp
import numpy as np
from jax import lax
from jax.experimental import pallas as pl
from jax.experimental.pallas import tpu as pltpu
from jax.sharding import Mesh
from jax.sharding import PartitionSpec as P

D = 1024
FF = 4096
H = 16
HD = 64
ROT = 32
SEQ = 1024
EPS = 1e-05
WIDE = D + 640
BF = jnp.bfloat16
F32 = jnp.float32
MIB = 1 << 20

SHARD = ("y", "zh", "core")
CONTEXT = ("x", "zl")

HEADS = ((0, 7), (8, 1), (14, 9), (6, 15), (12, 5), (4, 13), (10, 3), (2, 11))
UNITS_PER_SHARD = 7


def deal_units():
    columns = [[[], []] for _ in range(8)]
    qkv = [[kind * H + head for kind in range(3) for head in pair] for pair in HEADS]
    taken = [{unit // UNITS_PER_SHARD for unit in units} for units in qkv]
    order = []

    def place(unit):
        if unit == 112:
            return True
        shard, parity = unit // UNITS_PER_SHARD, unit % 2
        choices = sorted(range(8), key=lambda c: len(columns[c][0]) + len(columns[c][1]))
        for c in choices:
            if shard in taken[c] or len(columns[c][parity]) == 4:
                continue
            taken[c].add(shard)
            columns[c][parity].append(unit)
            if place(unit + 1):
                return True
            taken[c].remove(shard)
            columns[c][parity].pop()
        return False

    assert place(48)
    for c in range(8):
        pairs = [unit for pair in zip(*columns[c]) for unit in pair]
        order.append(qkv[c] + pairs)
    return np.array(order, np.int32)


UNITS = deal_units()
SLOT = UNITS // UNITS_PER_SHARD
SEND = np.zeros((16, 8), np.int32)
for _c in range(8):
    for _u in UNITS[_c]:
        SEND[_u // UNITS_PER_SHARD, _c] = _u % UNITS_PER_SHARD
HOME = np.zeros((112, 2), np.int32)
for _c in range(8):
    for _i, _u in enumerate(UNITS[_c]):
        HOME[_u] = (_c, _i)
COLUMN_UNITS = np.concatenate([np.array(HEADS, np.int32), UNITS[:, 6:] - 32], axis=1)
COLUMN_HOME = np.zeros((80, 2), np.int32)
for _c in range(8):
    for _i, _u in enumerate(COLUMN_UNITS[_c]):
        COLUMN_HOME[_u] = (_c, _i)


TABLE = np.concatenate([SLOT, COLUMN_UNITS // 2, UNITS // 2], axis=1).astype(np.int32)
SHARD_TABLE = np.concatenate([SEND, HOME[:, 0].reshape(16, 7)], axis=1).astype(np.int32)

def nn(left, right):
    return lax.dot_general(left, right, (((1,), (0,)), ((), ())), preferred_element_type=F32)


def nt(left, right):
    return lax.dot_general(left, right, (((1,), (1,)), ((), ())), preferred_element_type=F32)


def tn(left, right):
    return lax.dot_general(left, right, (((0,), (0,)), ((), ())), preferred_element_type=F32)


def normal(rows):
    average = jnp.mean(rows, axis=-1, keepdims=True)
    centred = rows - average
    variance = jnp.mean(centred * centred, axis=-1, keepdims=True)
    scale = lax.rsqrt(variance + EPS)
    return centred * scale, scale


def turn(values, cosines, sines):
    lane = lax.broadcasted_iota(jnp.int32, values.shape, 1) % HD
    ahead = pltpu.roll(values, 2 * HD - ROT // 2, 1)
    behind = pltpu.roll(values, ROT // 2, 1)
    return values * cosines + jnp.where(lane < ROT // 2, ahead, behind) * sines


def head_mask(values, head):
    lane = lax.broadcasted_iota(jnp.int32, values.shape, 1)
    return jnp.where((lane // HD) == head, values, jnp.zeros_like(values))


SCALE2 = HD ** (-0.5) * math.log2(math.e)
GELU_C = math.sqrt(2.0 / math.pi)
BLOCK = 256


def causal(shape, first_key, first_query):
    key = first_key + lax.broadcasted_iota(jnp.int32, shape, 0)
    query = first_query + lax.broadcasted_iota(jnp.int32, shape, 1)
    return key <= query


def block_scores(q_block, k_head, block):
    extent = (block + 1) * BLOCK
    scores = nt(k_head[:extent], q_block) * SCALE2
    last = scores[block * BLOCK:]
    last = jnp.where(causal(last.shape, 0, 0), last, -1e30)
    if block == 0:
        return last
    return jnp.concatenate([scores[: block * BLOCK], last], axis=0)


def index_of(ring, step, which, mine):
    return lax.rem(ring + step, 4) * 2 + (mine if which == 0 else 1 - mine)


def prepare_kernel(ids, table, shard_table, w_in, w_out, b_in, message, bias):
    shard, context = ids[3], ids[4]
    unit = shard_table[shard, context]
    message[:, :D] = w_in[pl.ds(pl.multiple_of(unit * HD, HD), HD), :]
    lower = lax.broadcasted_iota(jnp.int32, (HD, 128), 1) < HD
    for j in range(5):
        even = w_out[:, pl.ds(pl.multiple_of(table[context, 14 + 2 * j] * 128, 128), 128)]
        odd = w_out[:, pl.ds(pl.multiple_of(table[context, 15 + 2 * j] * 128, 128), 128)]
        tile = jnp.where(lower, even, odd)
        message[:, D + j * 128 : D + (j + 1) * 128] = tile
    lower = lax.broadcasted_iota(jnp.int32, (1, 128), 1) < HD
    for j in range(7):
        even = b_in[pl.ds(table[context, 24 + 2 * j], 1), :]
        odd = b_in[pl.ds(table[context, 25 + 2 * j], 1), :]
        bias[:, j * 128 : (j + 1) * 128] = jnp.where(lower, even, odd)


def project_kernel(ids, table, a0, b0, ar, br, af, bf, al, bl,
                   na0, nb0, nar, nbr, naf, nbf, nal, nbl, fa0, fb0, far_, fbr, faf, fbf, fal, fbl,
                   bias, gain, shift, cosines, sines, xhat, weights, weights_out, qkv, slope, gated, hidden, held):
    x, zl, core, context, y, zh = ids[0], ids[1], ids[2], ids[4], ids[5], ids[6]
    near = ((na0, nb0), (nar, nbr), (naf, nbf), (nal, nbl))
    far = ((fa0, fb0), (far_, fbr), (faf, fbf), (fal, fbl))
    for step in range(4):
        for which in (0, 1):
            place = 2 * index_of(y, step, which, zh)
            for piece, slot in ((near[step][which], place + core), (far[step][which], place + 1 - core)):
                held[slot] = piece[:, :D]
                weights_out[pl.ds(pl.multiple_of(slot * HD, HD), HD), :] = piece[:, D:]
    for i in range(14):
        weights[i * HD : (i + 1) * HD, :] = held[table[context, i]]

    for step, pair in enumerate(((a0, b0), (ar, br), (af, bf), (al, bl))):
        for which in (0, 1):
            rows = pl.ds(pl.multiple_of(index_of(x, step, which, zl) * 128, 128), 128)
            normed, _ = normal(pair[which][...].astype(F32))
            xhat[rows, :] = normed.astype(BF)
            hidden[rows, :] = (normed * gain[...] + shift[...]).astype(BF)

    @pl.loop(0, 4)
    def _(i):
        rows = pl.ds(pl.multiple_of(i * 256, 256), 256)
        proj = nt(hidden[rows, :], weights[...]) + bias[...]
        cos_rows, sin_rows = cosines[rows, :], sines[rows, :]
        qkv[rows, 0:128] = turn(proj[:, 0:128], cos_rows, sin_rows).astype(BF)
        qkv[rows, 128:256] = turn(proj[:, 128:256], cos_rows, sin_rows).astype(BF)
        qkv[rows, 256:384] = proj[:, 256:384].astype(BF)
        act = proj[:, 384:]
        square = act * act
        th = jnp.tanh(GELU_C * act * (1.0 + 0.044715 * square))
        half = 0.5 * (1.0 + th)
        gated[rows, :] = (act * half).astype(BF)
        slope[rows, :] = (
            half + 0.5 * act * (1.0 - th * th) * (GELU_C * (1.0 + 3 * 0.044715 * square))
        ).astype(BF)


def attend_kernel(qkv, gated, joined, lse):
    joined[:, 128:] = gated[...]
    keys, values = qkv[:, 128:256], qkv[:, 256:384]
    for head in range(2):
        k_head = head_mask(keys, head)
        v_head = head_mask(values, head)
        for block in range(SEQ // BLOCK):
            rows = pl.ds(block * BLOCK, BLOCK)
            scores = block_scores(qkv[rows, 0:128], k_head, block)
            largest = jnp.max(scores, axis=0, keepdims=True)
            raised = jnp.exp2(scores - largest)
            mass = jnp.sum(raised, axis=0, keepdims=True)
            lse[head : head + 1, block * BLOCK : (block + 1) * BLOCK] = largest + jnp.log2(mass)
            probs = (raised * (1.0 / mass)).astype(BF)
            result = tn(probs, v_head[: (block + 1) * BLOCK])
            if head == 0:
                joined[rows, 0:128] = result.astype(BF)
            else:
                joined[rows, 0:128] = (joined[rows, 0:128].astype(F32) + result).astype(BF)


def store_pair(zl, product, a, b):
    @pl.when(zl == 0)
    def _():
        a[...] = product[:128]
        b[...] = product[128:]

    @pl.when(zl != 0)
    def _():
        a[...] = product[128:]
        b[...] = product[:128]


def project_out_kernel(ids, joined, weights, oa, ob, ra, rb, fa, fb, la, lb):
    x, zl = ids[0], ids[1]
    for step, a, b in ((2, fa, fb), (1, ra, rb), (3, la, lb), (0, oa, ob)):
        rows = pl.ds(pl.multiple_of(lax.rem(x + step, 4) * 256, 256), 256)
        store_pair(zl, nt(joined[rows, :], weights[...]).astype(BF), a, b)


def backward_out_kernel(ids, a0, b0, ar, br, af, bf, al, bl, weights_out, slope, grad_attn, grad_ff, cot):
    x, zl = ids[0], ids[1]
    for step, pair in enumerate(((a0, b0), (ar, br), (af, bf), (al, bl))):
        for which in (0, 1):
            cot[pl.ds(pl.multiple_of(index_of(x, step, which, zl) * 128, 128), 128), :] = pair[which][...]

    @pl.loop(0, 4)
    def _(i):
        rows = pl.ds(pl.multiple_of(i * 256, 256), 256)
        grad = nn(cot[rows, :], weights_out[...])
        grad_attn[rows, :] = grad[:, :128].astype(BF)
        grad_ff[rows, :] = (grad[:, 128:] * slope[rows, :].astype(F32)).astype(BF)


def backward_attend_kernel(qkv, lse, grad_attn, grad_ff, cosines, sines, grad_proj, grad_q, grad_k, grad_v):
    keys, values = qkv[:, 128:256], qkv[:, 256:384]
    grad_k[...] = jnp.zeros_like(grad_k)
    grad_v[...] = jnp.zeros_like(grad_v)
    for head in range(2):
        k_head = head_mask(keys, head)
        v_head = head_mask(values, head)
        for block in range(SEQ // BLOCK):
            rows = pl.ds(block * BLOCK, BLOCK)
            extent = (block + 1) * BLOCK
            scores = block_scores(qkv[rows, 0:128], k_head, block)
            probs = jnp.exp2(scores - lse[head : head + 1, block * BLOCK : (block + 1) * BLOCK])
            grad_out = grad_attn[rows, :]
            grad_probs = nt(v_head[:extent], grad_out)
            delta = jnp.sum(grad_probs * probs, axis=0, keepdims=True)
            grad_scores = (probs * (grad_probs - delta)).astype(BF)
            grad_v[:extent, :] += nn(probs.astype(BF), head_mask(grad_out, head))
            grad_k[:extent, :] += nn(grad_scores, head_mask(qkv[rows, 0:128], head))
            result = tn(grad_scores, k_head[:extent])
            if head == 0:
                grad_q[rows, :] = result
            else:
                grad_q[rows, :] += result
    scale = HD ** (-0.5)
    cos_all, sin_all = cosines[...], -sines[...]
    grad_proj[:, 0:128] = turn((grad_q[...] * scale).astype(BF).astype(F32), cos_all, sin_all).astype(BF)
    grad_proj[:, 128:256] = turn((grad_k[...] * scale).astype(BF).astype(F32), cos_all, sin_all).astype(BF)
    grad_proj[:, 256:384] = grad_v[...].astype(BF)
    grad_proj[:, 384:] = grad_ff[...]


def split(values):
    high = values.astype(BF)
    return high, (values - high.astype(F32)).astype(BF)


def slot_place(ids, slot):
    return lax.rem(slot // 4 - ids[5] + 4, 4), jnp.where((slot // 2) % 2 == ids[6], 0, 1)


def backward_w_in_kernel(ids, table, grad_proj, weights, xhat, gain, shift, own, near, far, vectors):
    core, context = ids[2], ids[4]
    ones = jnp.ones((SEQ, 128), BF)
    grad_gain, grad_shift = jnp.zeros((1, D), F32), jnp.zeros((1, D), F32)
    for step in range(4):
        for side in (0, 1):
            near[step, side, :, :D] = jnp.zeros((HD, D), BF)
            far[step, side, :, :D] = jnp.zeros((HD, D), BF)
    for i in range(7):
        proj = grad_proj[:, i * 128 : (i + 1) * 128]
        product = tn(proj, xhat[...])
        column = tn(proj, ones)
        vectors[24 + i : 25 + i, :] = column.T[0:1]
        column = column[:, 0:1]
        rows = weights[i * 128 : (i + 1) * 128, :].astype(F32)
        grad_gain += jnp.sum(product * rows, axis=0, keepdims=True)
        grad_shift += jnp.sum(column * rows, axis=0, keepdims=True)
        grad = (product * gain[...] + column * shift[...]).astype(BF)
        for j in (0, 1):
            slot = table[context, 2 * i + j]
            step, side = slot_place(ids, slot)

            @pl.when(slot % 2 == core)
            def _():
                near[step, side, :, :D] = grad[j * HD : (j + 1) * HD]

            @pl.when(slot % 2 != core)
            def _():
                far[step, side, :, :D] = grad[j * HD : (j + 1) * HD]

    vectors[31:32, :] = jnp.zeros((1, 128), F32)
    grad_b_out = jnp.sum(own[...].astype(F32), axis=0, keepdims=True)
    for j in range(8):
        lanes = slice(j * 128, (j + 1) * 128)
        vectors[j : j + 1, :] = grad_gain[:, lanes]
        vectors[8 + j : 9 + j, :] = grad_shift[:, lanes]
        vectors[16 + j : 17 + j, :] = grad_b_out[:, lanes]
    high, low = split(vectors[...])
    for step in range(4):
        for side in (0, 1):
            for ref in (near, far):
                ref[step, side, :32, D:] = high
                ref[step, side, 32:, D:] = low


def backward_w_out_kernel(ids, cot, joined, near, far):
    core = ids[2]
    for j in range(8):
        grad = tn(cot[:, j * 128 : (j + 1) * 128], joined[...]).astype(BF)
        step, side = slot_place(ids, 2 * j)

        @pl.when(core == 0)
        def _():
            near[step, side] = grad[:HD]
            far[step, side] = grad[HD:]

        @pl.when(core != 0)
        def _():
            near[step, side] = grad[HD:]
            far[step, side] = grad[:HD]


def backward_normed_kernel(ids, grad_proj, weights, oa, ob, ra, rb, fa, fb, la, lb):
    x, zl = ids[0], ids[1]
    for step, a, b in ((2, fa, fb), (1, ra, rb), (3, la, lb), (0, oa, ob)):
        rows = pl.ds(pl.multiple_of(lax.rem(x + step, 4) * 256, 256), 256)
        store_pair(zl, nn(grad_proj[rows, :], weights[...]).astype(BF), a, b)


def total_vectors(*terms):
    return split(sum(term[rows, :].astype(F32) for term in terms for rows in (slice(0, 32), slice(32, 64))))


def add_slots_kernel(near, far, *parts):
    high, low = total_vectors(near[0, 0, :, D:], far[0, 0, :, D:])
    for step, part in enumerate(parts):
        part[:, :, :D] = (near[step, :, :, :D].astype(F32) + far[step, :, :, :D].astype(F32)).astype(BF)
        for side in (0, 1):
            part[side, :32, D:] = high
            part[side, 32:, D:] = low


def sum_slots_kernel(i0, i1, i2, i3, o0, o1, o2, o3, mine, other):
    high, low = total_vectors(*(part[0, :, D:] for part in (i0, i1, i2, i3)))
    for side, total in enumerate((mine, other)):
        total[:, :D] = sum(part[side, :, :D].astype(F32) for part in (i0, i1, i2, i3)).astype(BF)
        total[:, D:WIDE] = sum(part[side].astype(F32) for part in (o0, o1, o2, o3)).astype(BF)
        total[:32, WIDE:] = high
        total[32:, WIDE:] = low


def pair_slots_kernel(mine, far, across, far_across, a, b):
    for total, terms in ((a, (mine, far)), (b, (across, far_across))):
        total[:, :WIDE] = sum(term[:, :WIDE].astype(F32) for term in terms).astype(BF)
        high, low = total_vectors(*(term[:, WIDE:] for term in terms))
        total[:32, WIDE:] = high
        total[32:, WIDE:] = low


def finish_out_kernel(oa, ra, la, far, inputs, b_out, out):
    mixed = sum(term[...].astype(F32) for term in (oa, ra, la, far))
    out[...] = (inputs[...].astype(F32) + mixed + b_out[...]).astype(BF)


def finish_in_kernel(oa, ra, la, far, inputs, cotangent, gain, grad_inputs):
    grad = sum(term[...].astype(F32) for term in (oa, ra, la, far))
    own, scale = normal(inputs[...].astype(F32))
    pulled = grad * gain[...]
    rows = (
        pulled
        - jnp.mean(pulled, axis=-1, keepdims=True)
        - own * jnp.mean(pulled * own, axis=-1, keepdims=True)
    ) * scale
    grad_inputs[...] = (cotangent[...].astype(F32) + rows).astype(BF)


def finish_weights_kernel(ids, shard_table, a0, b0, ar, br, af, bf, al, bl,
                          grad_w_in, grad_w_out, grad_gain, grad_shift, grad_b_out, grad_b_in, held):
    for step, pair in enumerate(((a0, b0), (ar, br), (af, bf), (al, bl))):
        for which in (0, 1):
            held[index_of(ids[0], step, which, ids[1])] = pair[which][...]
    for i in range(7):
        grad_w_in[i * HD : (i + 1) * HD, :] = held[shard_table[ids[3], 8 + i], :, :D].astype(F32)
    lower = lax.broadcasted_iota(jnp.int32, (HD, 128), 1) < HD
    for t in range(40):
        tiles = []
        for unit in (2 * t, 2 * t + 1):
            c, i = (int(n) for n in COLUMN_HOME[unit])
            first = D + (i // 2) * 128
            tiles.append(held[c, :, first : first + 128].astype(F32))
        grad_w_out[:, t * 128 : (t + 1) * 128] = jnp.where(lower, *tiles)
    terms = [held[c, :32, WIDE:].astype(F32) + held[c, 32:, WIDE:].astype(F32) for c in range(8)]
    total = sum(term[:24] for term in terms)
    grad_gain[...] = total[0:8]
    grad_shift[...] = total[8:16]
    grad_b_out[...] = total[16:24]
    lower = lax.broadcasted_iota(jnp.int32, (1, 128), 1) < HD
    for row in range(56):
        (c, i), (d, j) = (tuple(int(n) for n in HOME[unit]) for unit in (2 * row, 2 * row + 1))
        grad_b_in[row : row + 1, :] = jnp.where(
            lower, terms[c][24 + i // 2 : 25 + i // 2], terms[d][24 + j // 2 : 25 + j // 2]
        )


VM = pl.BlockSpec(memory_space=pltpu.VMEM)
SM = pl.BlockSpec(memory_space=pltpu.SMEM)
S = jax.ShapeDtypeStruct


def kernel(body, outs, scalars, operands, name, us, scratch=()):
    return pl.pallas_call(
        body,
        out_shape=outs,
        in_specs=[SM] * len(scalars) + [VM] * len(operands),
        out_specs=jax.tree.map(lambda _: VM, outs),
        scratch_shapes=list(scratch),
        compiler_params=pltpu.CompilerParams(vmem_limit_bytes=24 * MIB),
        cost_estimate=pl.CostEstimate(flops=int(us * 1e9), bytes_accessed=int(us * 3e6), transcendentals=0),
        name=name,
    )(*scalars, *operands)


def hbm(*arrays):
    return tuple(pltpu.with_memory_space_constraint(array, pltpu.HBM) for array in arrays)


def shift(values, axis, by):
    return lax.ppermute(values, axis, [(i, (i + by) % 4) for i in range(4)])


def swap(values, axis):
    return lax.ppermute(values, axis, [(0, 1), (1, 0)])


def gather_ring(pair, axis):
    ahead, behind = shift(pair, axis, -1), shift(pair, axis, 1)
    return pair, ahead, shift(pair, axis, 2), behind


def scatter_ring(p0, p1, p2, p3, axis):
    return p0, shift(p1, axis, 1), shift(p3, axis, -1), shift(p2, axis, 2)


def ordered(index, mine, other):
    return jnp.stack([jnp.where(index == 0, mine, other), jnp.where(index == 0, other, mine)])


def pick(pair, index):
    return lax.dynamic_index_in_dim(pair, index, 0, keepdims=False)


def add(*terms):
    return sum(term.astype(F32) for term in terms).astype(BF)


def after(values, *events):
    return lax.optimization_barrier((values,) + events)


def turn_tables():
    steps = np.arange(ROT // 2)
    angles = np.arange(SEQ)[:, None] * (10000.0 ** (-2.0 * steps / ROT))[None, :]
    cosine, sine = np.cos(angles), np.sin(angles)
    still = np.ones((SEQ, HD - ROT))
    cosines = np.concatenate([cosine, cosine, still] * 2, axis=1)
    sines = np.concatenate([-sine, sine, 0.0 * still] * 2, axis=1)
    return jnp.asarray(cosines.astype(np.float32)), jnp.asarray(sines.astype(np.float32))


def on_device(inputs, ln_gain, ln_bias, w_in, b_in, w_out, b_out, cotangent):
    ids = jnp.stack(
        [lax.axis_index(axes) for axes in ("x", "zl", "core", SHARD, CONTEXT, "y", "zh")]
    ).astype(jnp.int32)
    table, shard_table = jnp.asarray(TABLE), jnp.asarray(SHARD_TABLE)
    cosines, sines = turn_tables()
    gain, shift_row = ln_gain[None], ln_bias[None]
    right, left = lambda v: shift(v, "x", 1), lambda v: shift(v, "x", -1)

    slots = lambda columns: S((8, HD, columns), BF)
    chunk = S((128, D), BF)
    message, bias = kernel(
        prepare_kernel, (S((HD, 1664), BF), S((1, 896), F32)), (ids, *hbm(table, shard_table)),
        hbm(w_in, w_out, b_in.reshape(56, 128)), "prepare", 2,
    )
    up, down = lambda v: shift(v, "y", 1), lambda v: shift(v, "y", -1)
    first, message = after(inputs, message)
    b0, al, ar = swap(first, "zl"), right(first), left(first)
    later, b0_ = after(message, b0)
    nb0 = swap(later, "zh")
    nal, nar = up(message), down(message)
    bl, br, af = right(b0), left(b0), right(al)
    br, ar, al = after(br, ar, al)
    bf = left(br)
    nbl, nbr, naf = up(nb0), down(nb0), up(nal)
    nbf = down(nbr)
    nbf, af_, bl_ = after(nbf, af, bl)
    near = later, nb0, nar, nbr, naf, nbf, nal, nbl
    far = [swap(piece, "core") for piece in near]
    cot, bl_ = after(cotangent, bl_)
    cb0, cal, car, caf = swap(cot, "zl"), right(cot), left(cot), shift(cot, "x", 2)

    xhat, weights_in, weights_out, qkv, slope, gated = kernel(
        project_kernel,
        (S((SEQ, D), BF), S((896, D), BF), S((D, 640), BF), S((SEQ, 384), BF), S((SEQ, 512), BF), S((SEQ, 512), BF)),
        (ids, table), (inputs, b0_, ar, br, af_, bf, al, bl_, *near, *far, bias, gain, shift_row, cosines, sines),
        "project", 7, [pltpu.VMEM((SEQ, D), BF), pltpu.VMEM((16, HD, D), BF)],
    )
    qkv, cb0, cal, car = after(qkv, cb0, cal, car)
    cbl, cbr, cbf = right(cb0), left(cb0), shift(cb0, "x", 2)
    joined, lse = kernel(attend_kernel, (S((SEQ, 640), BF), S((8, SEQ), F32)), (), (qkv, gated), "attend", 3)
    oa, ob, ra, rb, fa, fb, la, lb = kernel(
        project_out_kernel, (chunk,) * 8, (ids,), (joined, weights_out), "project_out", 3
    )
    fa, fb, rb, la = right(fa), left(fb), right(rb), left(la)
    grad_attn, grad_ff, cots = kernel(
        backward_out_kernel, (S((SEQ, 128), BF), S((SEQ, 512), BF), S((SEQ, D), BF)), (ids,),
        (cot, cb0, car, cbr, caf, cbf, cal, cbl, weights_out, slope), "backward_out", 3,
    )
    grad_attn, fa, fb = after(grad_attn, fa, fb)
    ra, lb = right(add(ra, fa)), left(add(lb, fb))
    grad_proj = kernel(
        backward_attend_kernel, S((SEQ, 896), BF), (), (qkv, lse, grad_attn, grad_ff, cosines, sines),
        "backward_attend", 5, [pltpu.VMEM((SEQ, 128), F32)] * 3,
    )
    slots = lambda columns: S((4, 2, HD, columns), BF)
    wide = D + 128
    near_in, far_in = kernel(
        backward_w_in_kernel, (slots(wide), slots(wide)), (ids, table),
        (grad_proj, weights_in, xhat, gain, shift_row, cotangent), "backward_w_in", 6, [pltpu.VMEM((32, 128), F32)],
    )
    far_in = swap(far_in, "core")
    cots, rb, la, ra, lb = after(cots, rb, la, ra, lb)
    near_out, far_out = kernel(
        backward_w_out_kernel, (slots(640), slots(640)), (ids,), (cots, joined), "backward_w_out", 3
    )
    far_in, near_out, far_out = after(far_in, near_out, far_out)
    in_parts = kernel(add_slots_kernel, (S((2, HD, wide), BF),) * 4, (), (near_in, far_in), "add_slots", 1)
    in_parts, grad_proj = after(in_parts, grad_proj)
    in_parts = scatter_ring(*in_parts, "y")
    far_out = swap(far_out, "core")
    goa, gob, gra, grb, gfa, gfb, gla, glb = kernel(
        backward_normed_kernel, (chunk,) * 8, (ids,), (grad_proj, weights_in), "backward_normed", 4
    )
    far_out, gfa, gfb = after(far_out, gfa, gfb)
    out_parts = scatter_ring(*(add(near_out[k], far_out[k]) for k in range(4)), "y")
    gfa, gfb, grb, gla = right(gfa), left(gfb), right(grb), left(gla)

    slot = S((HD, WIDE + 128), BF)
    in_parts, gfa, gfb = after(in_parts, gfa, gfb)
    mine, other = kernel(sum_slots_kernel, (slot, slot), (), (*in_parts, *out_parts), "sum_slots", 2)
    gra, glb = right(add(gra, gfa)), left(add(glb, gfb))
    across, far = swap(mine, "zl"), swap(other, "zh")
    far_across = lax.ppermute(other, ("zh", "zl"), [(i, 3 - i) for i in range(4)])
    ob = swap(add(ob, rb, lb), "zl")
    out = kernel(finish_out_kernel, chunk, (), (oa, ra, la, ob, inputs, b_out[None]), "finish_out", 1)
    a0, b0 = kernel(pair_slots_kernel, (slot, slot), (), (mine, far, across, far_across), "pair_slots", 1)
    al, ar, bl, br = right(a0), left(a0), right(b0), left(b0)
    gob = swap(add(gob, grb, glb), "zl")
    af, bf = right(al), left(br)
    grad_inputs = kernel(finish_in_kernel, chunk, (), (goa, gra, gla, gob, inputs, cotangent, gain), "finish_in", 1)
    bf, grad_inputs, out = after(bf, grad_inputs, out)
    row = S((8, 128), F32)
    grad_w_in, grad_w_out, grad_gain, grad_shift, grad_b_out, grad_b_in = kernel(
        finish_weights_kernel, (S((448, D), F32), S((HD, 5120), F32), row, row, row, S((56, 128), F32)),
        (ids, shard_table), (a0, b0, ar, br, af, bf, al, bl), "finish_weights", 3, [pltpu.VMEM((8, HD, WIDE + 128), BF)],
    )
    return (
        out, grad_inputs, grad_gain.reshape(D), grad_shift.reshape(D),
        grad_w_in, grad_b_in.reshape(7168), grad_w_out, grad_b_out.reshape(D),
    )


def solution(mesh):
    fine = Mesh(mesh.devices.reshape(4, 2, 2, 4, 2), SHARD + CONTEXT)
    rows = P(SHARD + CONTEXT, None)
    in_specs = (rows, P(), P(), P(SHARD, None), P(), P(SHARD, None), P(), rows)
    out_specs = (rows, rows, P(), P(), P(SHARD, None), P(), P(SHARD, None), P())
    return jax.shard_map(on_device, mesh=fine, in_specs=in_specs, out_specs=out_specs, check_vma=False)
```

```python
import functools
import math

import jax
import jax.numpy as jnp
import numpy as np
from jax import lax
from jax.experimental import pallas as pl
from jax.experimental.pallas import tpu as pltpu
from jax.sharding import Mesh
from jax.sharding import PartitionSpec as P

D = 1024
FF = 4096
H = 16
HD = 64
ROT = 32
SEQ = 1024
EPS = 1e-05
WIDE = D + 640
BF = jnp.bfloat16
F32 = jnp.float32
MIB = 1 << 20

COST = {'prepare': 0.2, 'project': 0.7000000000000001, 'attend': 0.30000000000000004, 'project_out': 0.30000000000000004, 'backward_out': 0.30000000000000004, 'backward_attend': 0.5, 'backward_w_in': 0.6000000000000001, 'backward_w_out': 0.30000000000000004, 'add_slots': 0.1, 'backward_normed': 0.4, 'sum_slots': 0.2, 'finish_out': 0.1, 'pair_slots': 0.1, 'finish_in': 0.1, 'finish_weights': 0.30000000000000004}

SHARD = ("y", "zh", "core")
CONTEXT = ("x", "zl")

HEADS = ((0, 7), (8, 1), (14, 9), (6, 15), (12, 5), (4, 13), (10, 3), (2, 11))
UNITS_PER_SHARD = 7


def deal_units():
    columns = [[[], []] for _ in range(8)]
    qkv = [[kind * H + head for kind in range(3) for head in pair] for pair in HEADS]
    taken = [{unit // UNITS_PER_SHARD for unit in units} for units in qkv]
    order = []

    def place(unit):
        if unit == 112:
            return True
        shard, parity = unit // UNITS_PER_SHARD, unit % 2
        choices = sorted(range(8), key=lambda c: len(columns[c][0]) + len(columns[c][1]))
        for c in choices:
            if shard in taken[c] or len(columns[c][parity]) == 4:
                continue
            taken[c].add(shard)
            columns[c][parity].append(unit)
            if place(unit + 1):
                return True
            taken[c].remove(shard)
            columns[c][parity].pop()
        return False

    assert place(48)
    for c in range(8):
        pairs = [unit for pair in zip(*columns[c]) for unit in pair]
        order.append(qkv[c] + pairs)
    return np.array(order, np.int32)


UNITS = deal_units()
SLOT = UNITS // UNITS_PER_SHARD
SEND = np.zeros((16, 8), np.int32)
for _c in range(8):
    for _u in UNITS[_c]:
        SEND[_u // UNITS_PER_SHARD, _c] = _u % UNITS_PER_SHARD
HOME = np.zeros((112, 2), np.int32)
for _c in range(8):
    for _i, _u in enumerate(UNITS[_c]):
        HOME[_u] = (_c, _i)
COLUMN_UNITS = np.concatenate([np.array(HEADS, np.int32), UNITS[:, 6:] - 32], axis=1)
COLUMN_HOME = np.zeros((80, 2), np.int32)
for _c in range(8):
    for _i, _u in enumerate(COLUMN_UNITS[_c]):
        COLUMN_HOME[_u] = (_c, _i)


TABLE = np.concatenate([SLOT, COLUMN_UNITS // 2, UNITS // 2], axis=1).astype(np.int32)
SHARD_TABLE = np.concatenate([SEND, HOME[:, 0].reshape(16, 7)], axis=1).astype(np.int32)

def nn(left, right):
    return lax.dot_general(left, right, (((1,), (0,)), ((), ())), preferred_element_type=F32)


def nt(left, right):
    return lax.dot_general(left, right, (((1,), (1,)), ((), ())), preferred_element_type=F32)


def tn(left, right):
    return lax.dot_general(left, right, (((0,), (0,)), ((), ())), preferred_element_type=F32)


def normal(rows):
    average = jnp.mean(rows, axis=-1, keepdims=True)
    centred = rows - average
    variance = jnp.mean(centred * centred, axis=-1, keepdims=True)
    scale = lax.rsqrt(variance + EPS)
    return centred * scale, scale


def turn(values, cosines, sines):
    lane = lax.broadcasted_iota(jnp.int32, values.shape, 1) % HD
    ahead = pltpu.roll(values, 2 * HD - ROT // 2, 1)
    behind = pltpu.roll(values, ROT // 2, 1)
    return values * cosines + jnp.where(lane < ROT // 2, ahead, behind) * sines


def head_mask(values, head):
    lane = lax.broadcasted_iota(jnp.int32, values.shape, 1)
    return jnp.where((lane // HD) == head, values, jnp.zeros_like(values))


SCALE2 = HD ** (-0.5) * math.log2(math.e)
GELU_C = math.sqrt(2.0 / math.pi)
BLOCK = 256


def causal(shape, first_key, first_query):
    key = first_key + lax.broadcasted_iota(jnp.int32, shape, 0)
    query = first_query + lax.broadcasted_iota(jnp.int32, shape, 1)
    return key <= query


def block_scores(q_block, k_head, block):
    extent = (block + 1) * BLOCK
    scores = nt(k_head[:extent], q_block) * SCALE2
    last = scores[block * BLOCK:]
    last = jnp.where(causal(last.shape, 0, 0), last, -1e30)
    if block == 0:
        return last
    return jnp.concatenate([scores[: block * BLOCK], last], axis=0)


def index_of(ring, step, which, mine):
    return lax.rem(ring + step, 4) * 2 + (mine if which == 0 else 1 - mine)


def prepare_kernel(ids, table, shard_table, w_in, w_out, b_in, message, bias):
    shard, context = ids[3], ids[4]
    unit = shard_table[shard, context]
    message[:, :D] = w_in[pl.ds(pl.multiple_of(unit * HD, HD), HD), :]
    lower = lax.broadcasted_iota(jnp.int32, (HD, 128), 1) < HD
    for j in range(5):
        even = w_out[:, pl.ds(pl.multiple_of(table[context, 14 + 2 * j] * 128, 128), 128)]
        odd = w_out[:, pl.ds(pl.multiple_of(table[context, 15 + 2 * j] * 128, 128), 128)]
        tile = jnp.where(lower, even, odd)
        message[:, D + j * 128 : D + (j + 1) * 128] = tile
    lower = lax.broadcasted_iota(jnp.int32, (1, 128), 1) < HD
    for j in range(7):
        even = b_in[pl.ds(table[context, 24 + 2 * j], 1), :]
        odd = b_in[pl.ds(table[context, 25 + 2 * j], 1), :]
        bias[:, j * 128 : (j + 1) * 128] = jnp.where(lower, even, odd)


def project_kernel(ids, table, a0, b0, ar, br, af, bf, al, bl,
                   na0, nb0, nar, nbr, naf, nbf, nal, nbl, fa0, fb0, far_, fbr, faf, fbf, fal, fbl,
                   bias, gain, shift, cosines, sines, xhat, weights, weights_out, qkv, slope, gated, hidden, held):
    x, zl, core, context, y, zh = ids[0], ids[1], ids[2], ids[4], ids[5], ids[6]
    near = ((na0, nb0), (nar, nbr), (naf, nbf), (nal, nbl))
    far = ((fa0, fb0), (far_, fbr), (faf, fbf), (fal, fbl))
    for step in range(4):
        for which in (0, 1):
            place = 2 * index_of(y, step, which, zh)
            for piece, slot in ((near[step][which], place + core), (far[step][which], place + 1 - core)):
                held[slot] = piece[:, :D]
                weights_out[pl.ds(pl.multiple_of(slot * HD, HD), HD), :] = piece[:, D:]
    for i in range(14):
        weights[i * HD : (i + 1) * HD, :] = held[table[context, i]]

    for step, pair in enumerate(((a0, b0), (ar, br), (af, bf), (al, bl))):
        for which in (0, 1):
            rows = pl.ds(pl.multiple_of(index_of(x, step, which, zl) * 128, 128), 128)
            normed, _ = normal(pair[which][...].astype(F32))
            xhat[rows, :] = normed.astype(BF)
            hidden[rows, :] = (normed * gain[...] + shift[...]).astype(BF)

    @pl.loop(0, 4)
    def _(i):
        rows = pl.ds(pl.multiple_of(i * 256, 256), 256)
        proj = nt(hidden[rows, :], weights[...]) + bias[...]
        cos_rows, sin_rows = cosines[rows, :], sines[rows, :]
        qkv[rows, 0:128] = turn(proj[:, 0:128], cos_rows, sin_rows).astype(BF)
        qkv[rows, 128:256] = turn(proj[:, 128:256], cos_rows, sin_rows).astype(BF)
        qkv[rows, 256:384] = proj[:, 256:384].astype(BF)
        act = proj[:, 384:]
        square = act * act
        th = jnp.tanh(GELU_C * act * (1.0 + 0.044715 * square))
        half = 0.5 * (1.0 + th)
        gated[rows, :] = (act * half).astype(BF)
        slope[rows, :] = (
            half + 0.5 * act * (1.0 - th * th) * (GELU_C * (1.0 + 3 * 0.044715 * square))
        ).astype(BF)


def attend_kernel(qkv, gated, joined, lse):
    joined[:, 128:] = gated[...]
    keys, values = qkv[:, 128:256], qkv[:, 256:384]
    for head in range(2):
        k_head = head_mask(keys, head)
        v_head = head_mask(values, head)
        for block in range(SEQ // BLOCK):
            rows = pl.ds(block * BLOCK, BLOCK)
            scores = block_scores(qkv[rows, 0:128], k_head, block)
            largest = jnp.max(scores, axis=0, keepdims=True)
            raised = jnp.exp2(scores - largest)
            mass = jnp.sum(raised, axis=0, keepdims=True)
            lse[head : head + 1, block * BLOCK : (block + 1) * BLOCK] = largest + jnp.log2(mass)
            probs = (raised * (1.0 / mass)).astype(BF)
            result = tn(probs, v_head[: (block + 1) * BLOCK])
            if head == 0:
                joined[rows, 0:128] = result.astype(BF)
            else:
                joined[rows, 0:128] = (joined[rows, 0:128].astype(F32) + result).astype(BF)


def store_pair(zl, product, a, b):
    @pl.when(zl == 0)
    def _():
        a[...] = product[:128]
        b[...] = product[128:]

    @pl.when(zl != 0)
    def _():
        a[...] = product[128:]
        b[...] = product[:128]


def project_out_kernel(ids, joined, weights, oa, ob, ra, rb, fa, fb, la, lb):
    x, zl = ids[0], ids[1]
    for step, a, b in ((2, fa, fb), (1, ra, rb), (3, la, lb), (0, oa, ob)):
        rows = pl.ds(pl.multiple_of(lax.rem(x + step, 4) * 256, 256), 256)
        store_pair(zl, nt(joined[rows, :], weights[...]).astype(BF), a, b)


def backward_out_kernel(ids, a0, b0, ar, br, af, bf, al, bl, weights_out, slope, grad_attn, grad_ff, cot):
    x, zl = ids[0], ids[1]
    for step, pair in enumerate(((a0, b0), (ar, br), (af, bf), (al, bl))):
        for which in (0, 1):
            cot[pl.ds(pl.multiple_of(index_of(x, step, which, zl) * 128, 128), 128), :] = pair[which][...]

    @pl.loop(0, 4)
    def _(i):
        rows = pl.ds(pl.multiple_of(i * 256, 256), 256)
        grad = nn(cot[rows, :], weights_out[...])
        grad_attn[rows, :] = grad[:, :128].astype(BF)
        grad_ff[rows, :] = (grad[:, 128:] * slope[rows, :].astype(F32)).astype(BF)


def backward_attend_kernel(qkv, lse, grad_attn, grad_ff, cosines, sines, grad_proj, grad_q, grad_k, grad_v):
    keys, values = qkv[:, 128:256], qkv[:, 256:384]
    grad_k[...] = jnp.zeros_like(grad_k)
    grad_v[...] = jnp.zeros_like(grad_v)
    for head in range(2):
        k_head = head_mask(keys, head)
        v_head = head_mask(values, head)
        for block in range(SEQ // BLOCK):
            rows = pl.ds(block * BLOCK, BLOCK)
            extent = (block + 1) * BLOCK
            scores = block_scores(qkv[rows, 0:128], k_head, block)
            probs = jnp.exp2(scores - lse[head : head + 1, block * BLOCK : (block + 1) * BLOCK])
            grad_out = grad_attn[rows, :]
            grad_probs = nt(v_head[:extent], grad_out)
            delta = jnp.sum(grad_probs * probs, axis=0, keepdims=True)
            grad_scores = (probs * (grad_probs - delta)).astype(BF)
            grad_v[:extent, :] += nn(probs.astype(BF), head_mask(grad_out, head))
            grad_k[:extent, :] += nn(grad_scores, head_mask(qkv[rows, 0:128], head))
            result = tn(grad_scores, k_head[:extent])
            if head == 0:
                grad_q[rows, :] = result
            else:
                grad_q[rows, :] += result
    scale = HD ** (-0.5)
    cos_all, sin_all = cosines[...], -sines[...]
    grad_proj[:, 0:128] = turn((grad_q[...] * scale).astype(BF).astype(F32), cos_all, sin_all).astype(BF)
    grad_proj[:, 128:256] = turn((grad_k[...] * scale).astype(BF).astype(F32), cos_all, sin_all).astype(BF)
    grad_proj[:, 256:384] = grad_v[...].astype(BF)
    grad_proj[:, 384:] = grad_ff[...]


def split(values):
    high = values.astype(BF)
    return high, (values - high.astype(F32)).astype(BF)


def slot_place(ids, slot):
    return lax.rem(slot // 4 - ids[5] + 4, 4), jnp.where((slot // 2) % 2 == ids[6], 0, 1)


def backward_w_in_kernel(ids, table, grad_proj, weights, xhat, gain, shift, own, near, far, vectors):
    core, context = ids[2], ids[4]
    ones = jnp.ones((SEQ, 128), BF)
    grad_gain, grad_shift = jnp.zeros((1, D), F32), jnp.zeros((1, D), F32)
    for step in range(4):
        for side in (0, 1):
            near[step, side, :, :D] = jnp.zeros((HD, D), BF)
            far[step, side, :, :D] = jnp.zeros((HD, D), BF)
    for i in range(7):
        proj = grad_proj[:, i * 128 : (i + 1) * 128]
        product = tn(proj, xhat[...])
        column = tn(proj, ones)
        vectors[24 + i : 25 + i, :] = column.T[0:1]
        column = column[:, 0:1]
        rows = weights[i * 128 : (i + 1) * 128, :].astype(F32)
        grad_gain += jnp.sum(product * rows, axis=0, keepdims=True)
        grad_shift += jnp.sum(column * rows, axis=0, keepdims=True)
        grad = (product * gain[...] + column * shift[...]).astype(BF)
        for j in (0, 1):
            slot = table[context, 2 * i + j]
            step, side = slot_place(ids, slot)

            @pl.when(slot % 2 == core)
            def _():
                near[step, side, :, :D] = grad[j * HD : (j + 1) * HD]

            @pl.when(slot % 2 != core)
            def _():
                far[step, side, :, :D] = grad[j * HD : (j + 1) * HD]

    vectors[31:32, :] = jnp.zeros((1, 128), F32)
    grad_b_out = jnp.sum(own[...].astype(F32), axis=0, keepdims=True)
    for j in range(8):
        lanes = slice(j * 128, (j + 1) * 128)
        vectors[j : j + 1, :] = grad_gain[:, lanes]
        vectors[8 + j : 9 + j, :] = grad_shift[:, lanes]
        vectors[16 + j : 17 + j, :] = grad_b_out[:, lanes]
    high, low = split(vectors[...])
    for step in range(4):
        for side in (0, 1):
            for ref in (near, far):
                ref[step, side, :32, D:] = high
                ref[step, side, 32:, D:] = low


def backward_w_out_kernel(ids, cot, joined, near, far):
    core = ids[2]
    for j in range(8):
        grad = tn(cot[:, j * 128 : (j + 1) * 128], joined[...]).astype(BF)
        step, side = slot_place(ids, 2 * j)

        @pl.when(core == 0)
        def _():
            near[step, side] = grad[:HD]
            far[step, side] = grad[HD:]

        @pl.when(core != 0)
        def _():
            near[step, side] = grad[HD:]
            far[step, side] = grad[:HD]


def backward_normed_kernel(ids, grad_proj, weights, oa, ob, ra, rb, fa, fb, la, lb):
    x, zl = ids[0], ids[1]
    for step, a, b in ((2, fa, fb), (1, ra, rb), (3, la, lb), (0, oa, ob)):
        rows = pl.ds(pl.multiple_of(lax.rem(x + step, 4) * 256, 256), 256)
        store_pair(zl, nn(grad_proj[rows, :], weights[...]).astype(BF), a, b)


def total_vectors(*terms):
    return split(sum(term[rows, :].astype(F32) for term in terms for rows in (slice(0, 32), slice(32, 64))))


def add_slots_kernel(near_in, far_in, near_out, far_out, *parts):
    high, low = total_vectors(near_in[0, 0, :, D:], far_in[0, 0, :, D:])
    for step, part in enumerate(parts):
        part[:, :, :D] = (near_in[step, :, :, :D].astype(F32) + far_in[step, :, :, :D].astype(F32)).astype(BF)
        part[:, :, D:WIDE] = (near_out[step].astype(F32) + far_out[step].astype(F32)).astype(BF)
        for side in (0, 1):
            part[side, :32, WIDE:] = high
            part[side, 32:, WIDE:] = low


def sum_slots_kernel(p0, p1, p2, p3, mine, other):
    parts = (p0, p1, p2, p3)
    high, low = total_vectors(*(part[0, :, WIDE:] for part in parts))
    for side, total in enumerate((mine, other)):
        total[:, :WIDE] = sum(part[side, :, :WIDE].astype(F32) for part in parts).astype(BF)
        total[:32, WIDE:] = high
        total[32:, WIDE:] = low


def pair_slots_kernel(mine, far, across, far_across, a, b):
    for total, terms in ((a, (mine, far)), (b, (across, far_across))):
        total[:, :WIDE] = sum(term[:, :WIDE].astype(F32) for term in terms).astype(BF)
        high, low = total_vectors(*(term[:, WIDE:] for term in terms))
        total[:32, WIDE:] = high
        total[32:, WIDE:] = low


def finish_out_kernel(oa, ra, la, far, inputs, b_out, out):
    mixed = sum(term[...].astype(F32) for term in (oa, ra, la, far))
    out[...] = (inputs[...].astype(F32) + mixed + b_out[...]).astype(BF)


def finish_in_kernel(oa, ra, la, far, inputs, cotangent, gain, grad_inputs):
    grad = sum(term[...].astype(F32) for term in (oa, ra, la, far))
    own, scale = normal(inputs[...].astype(F32))
    pulled = grad * gain[...]
    rows = (
        pulled
        - jnp.mean(pulled, axis=-1, keepdims=True)
        - own * jnp.mean(pulled * own, axis=-1, keepdims=True)
    ) * scale
    grad_inputs[...] = (cotangent[...].astype(F32) + rows).astype(BF)


def finish_weights_kernel(ids, shard_table, a0, b0, ar, br, af, bf, al, bl,
                          grad_w_in, grad_w_out, grad_gain, grad_shift, grad_b_out, grad_b_in, held):
    for step, pair in enumerate(((a0, b0), (ar, br), (af, bf), (al, bl))):
        for which in (0, 1):
            held[index_of(ids[0], step, which, ids[1])] = pair[which][...]
    for i in range(7):
        grad_w_in[i * HD : (i + 1) * HD, :] = held[shard_table[ids[3], 8 + i], :, :D].astype(F32)
    lower = lax.broadcasted_iota(jnp.int32, (HD, 128), 1) < HD
    for t in range(40):
        tiles = []
        for unit in (2 * t, 2 * t + 1):
            c, i = (int(n) for n in COLUMN_HOME[unit])
            first = D + (i // 2) * 128
            tiles.append(held[c, :, first : first + 128].astype(F32))
        grad_w_out[:, t * 128 : (t + 1) * 128] = jnp.where(lower, *tiles)
    terms = [held[c, :32, WIDE:].astype(F32) + held[c, 32:, WIDE:].astype(F32) for c in range(8)]
    total = sum(term[:24] for term in terms)
    grad_gain[...] = total[0:8]
    grad_shift[...] = total[8:16]
    grad_b_out[...] = total[16:24]
    lower = lax.broadcasted_iota(jnp.int32, (1, 128), 1) < HD
    for row in range(56):
        (c, i), (d, j) = (tuple(int(n) for n in HOME[unit]) for unit in (2 * row, 2 * row + 1))
        grad_b_in[row : row + 1, :] = jnp.where(
            lower, terms[c][24 + i // 2 : 25 + i // 2], terms[d][24 + j // 2 : 25 + j // 2]
        )


VM = pl.BlockSpec(memory_space=pltpu.VMEM)
SM = pl.BlockSpec(memory_space=pltpu.SMEM)
S = jax.ShapeDtypeStruct


def kernel(body, outs, scalars, operands, name, us, scratch=()):
    return pl.pallas_call(
        body,
        out_shape=outs,
        in_specs=[SM] * len(scalars) + [VM] * len(operands),
        out_specs=jax.tree.map(lambda _: VM, outs),
        scratch_shapes=list(scratch),
        compiler_params=pltpu.CompilerParams(vmem_limit_bytes=24 * MIB),
        cost_estimate=pl.CostEstimate(flops=int(COST[name] * 1e9), bytes_accessed=int(COST[name] * 3e6), transcendentals=0),
        name=name,
    )(*scalars, *operands)


def hbm(*arrays):
    return tuple(pltpu.with_memory_space_constraint(array, pltpu.HBM) for array in arrays)


def shift(values, axis, by):
    return lax.ppermute(values, axis, [(i, (i + by) % 4) for i in range(4)])


def swap(values, axis):
    return lax.ppermute(values, axis, [(0, 1), (1, 0)])


def gather_ring(pair, axis):
    ahead, behind = shift(pair, axis, -1), shift(pair, axis, 1)
    return pair, ahead, shift(pair, axis, 2), behind


def scatter_ring(p0, p1, p2, p3, axis):
    return p0, shift(p1, axis, 1), shift(p3, axis, -1), shift(p2, axis, 2)


def ordered(index, mine, other):
    return jnp.stack([jnp.where(index == 0, mine, other), jnp.where(index == 0, other, mine)])


def pick(pair, index):
    return lax.dynamic_index_in_dim(pair, index, 0, keepdims=False)


def add(*terms):
    return sum(term.astype(F32) for term in terms).astype(BF)


def after(values, *events):
    return lax.optimization_barrier((values,) + events)


def turn_tables():
    steps = np.arange(ROT // 2)
    angles = np.arange(SEQ)[:, None] * (10000.0 ** (-2.0 * steps / ROT))[None, :]
    cosine, sine = np.cos(angles), np.sin(angles)
    still = np.ones((SEQ, HD - ROT))
    cosines = np.concatenate([cosine, cosine, still] * 2, axis=1)
    sines = np.concatenate([-sine, sine, 0.0 * still] * 2, axis=1)
    return jnp.asarray(cosines.astype(np.float32)), jnp.asarray(sines.astype(np.float32))


def on_device(inputs, ln_gain, ln_bias, w_in, b_in, w_out, b_out, cotangent):
    ids = jnp.stack(
        [lax.axis_index(axes) for axes in ("x", "zl", "core", SHARD, CONTEXT, "y", "zh")]
    ).astype(jnp.int32)
    table, shard_table = jnp.asarray(TABLE), jnp.asarray(SHARD_TABLE)
    cosines, sines = turn_tables()
    gain, shift_row = ln_gain[None], ln_bias[None]
    right, left = lambda v: shift(v, "x", 1), lambda v: shift(v, "x", -1)
    up, down = lambda v: shift(v, "y", 1), lambda v: shift(v, "y", -1)

    chunk = S((128, D), BF)
    message, bias = kernel(
        prepare_kernel, (S((HD, 1664), BF), S((1, 896), F32)), (ids, *hbm(table, shard_table)),
        hbm(w_in, w_out, b_in.reshape(56, 128)), "prepare", 2,
    )
    first = inputs
    first, message = after(inputs, message)
    b0, al, ar = swap(first, "zl"), right(first), left(first)
    later, b0_ = after(message, b0)
    nb0 = swap(later, "zh")
    nal, nar = up(message), down(message)
    bl, br, af = right(b0), left(b0), right(al)
    cot, cot_e = cotangent, None
    br, ar, al = after(br, ar, al)
    bf = left(br)
    nbl, nbr, naf = up(nb0), down(nb0), up(nal)
    nbf = down(nbr)
    af_, bl_ = af, bl
    nbf, af_, bl_ = after(nbf, af, bl)
    near = later, nb0, nar, nbr, naf, nbf, nal, nbl
    far = [swap(piece, "core") for piece in near]
    cot, bl_ = after(cot, bl_)
    cb0, cal, car = swap(cot, "zl"), right(cot), left(cot)
    caf = shift(cot, "x", 2)

    xhat, weights_in, weights_out, qkv, slope, gated = kernel(
        project_kernel,
        (S((SEQ, D), BF), S((896, D), BF), S((D, 640), BF), S((SEQ, 384), BF), S((SEQ, 512), BF), S((SEQ, 512), BF)),
        (ids, table), (inputs, b0_, ar, br, af_, bf, al, bl_, *near, *far, bias, gain, shift_row, cosines, sines),
        "project", 7, [pltpu.VMEM((SEQ, D), BF), pltpu.VMEM((16, HD, D), BF)],
    )
    qkv, cb0 = after(qkv, cb0)
    cbl, cbr = right(cb0), left(cb0)
    cbf = shift(cb0, "x", 2)
    joined, lse = kernel(attend_kernel, (S((SEQ, 640), BF), S((8, SEQ), F32)), (), (qkv, gated), "attend", 3)
    oa, ob, ra, rb, fa, fb, la, lb = kernel(
        project_out_kernel, (chunk,) * 8, (ids,), (joined, weights_out), "project_out", 3
    )
    fa, fb = right(fa), left(fb)
    grad_attn, grad_ff, cots = kernel(
        backward_out_kernel, (S((SEQ, 128), BF), S((SEQ, 512), BF), S((SEQ, D), BF)), (ids,),
        (cot, cb0, car, cbr, caf, cbf, cal, cbl, weights_out, slope), "backward_out", 3,
    )
    grad_attn, fa, fb = after(grad_attn, fa, fb)
    grad_proj = kernel(
        backward_attend_kernel, S((SEQ, 896), BF), (), (qkv, lse, grad_attn, grad_ff, cosines, sines),
        "backward_attend", 5, [pltpu.VMEM((SEQ, 128), F32)] * 3,
    )
    slots = lambda columns: S((4, 2, HD, columns), BF)
    wide = D + 128
    near_in, far_in = kernel(
        backward_w_in_kernel, (slots(wide), slots(wide)), (ids, table),
        (grad_proj, weights_in, xhat, gain, shift_row, cotangent), "backward_w_in", 6, [pltpu.VMEM((32, 128), F32)],
    )
    far_in = swap(far_in, "core")

    near_out, far_out = kernel(
        backward_w_out_kernel, (slots(640), slots(640)), (ids,), (cots, joined), "backward_w_out", 3
    )
    far_out = swap(far_out, "core")
    grad_proj, near_out = after(grad_proj, near_out)
    parts = kernel(backward_normed_kernel, (chunk,) * 8, (ids,), (grad_proj, weights_in), "backward_normed", 4)
    far_in, *parts = after(far_in, *parts)
    both = kernel(
        add_slots_kernel, (S((2, HD, WIDE + 128), BF),) * 4, (), (near_in, far_in, near_out, far_out), "add_slots", 1
    )
    both = scatter_ring(*both, "y")
    goa, gob, gra, grb, gfa, gfb, gla, glb = parts
    gfa, gfb, grb, gla = right(gfa), left(gfb), right(grb), left(gla)

    ra, lb = add(ra, fa), add(lb, fb)
    ra, lb = right(ra), left(lb)
    rb, la = right(rb), left(la)
    slot = S((HD, WIDE + 128), BF)
    gra, glb = right(add(gra, gfa)), left(add(glb, gfb))
    both, grb, gla, gra, glb = after(both, grb, gla, gra, glb)
    mine, other = kernel(sum_slots_kernel, (slot, slot), (), both, "sum_slots", 2)
    across, far = swap(mine, "zl"), swap(other, "zh")
    far_across = lax.ppermute(other, ("zh", "zl"), [(i, 3 - i) for i in range(4)])
    ob = swap(add(ob, rb, lb), "zl")
    gob = swap(add(gob, grb, glb), "zl")
    across, rb_, la_, ra_, lb_ = after(across, rb, la, ra, lb)
    a0, b0 = kernel(pair_slots_kernel, (slot, slot), (), (mine, far, across, far_across), "pair_slots", 1)
    al, ar, bl, br = right(a0), left(a0), right(b0), left(b0)
    br, ar = after(br, ar)
    af, bf = right(al), left(br)
    ra, la = ra_, la_
    out = kernel(finish_out_kernel, chunk, (), (oa, ra, la, ob, inputs, b_out[None]), "finish_out", 1)
    grad_inputs = kernel(finish_in_kernel, chunk, (), (goa, gra, gla, gob, inputs, cotangent, gain), "finish_in", 1)
    row = S((8, 128), F32)
    grad_w_in, grad_w_out, grad_gain, grad_shift, grad_b_out, grad_b_in = kernel(
        finish_weights_kernel, (S((448, D), F32), S((HD, 5120), F32), row, row, row, S((56, 128), F32)),
        (ids, shard_table), (a0, b0, ar, br, af, bf, al, bl), "finish_weights", 3, [pltpu.VMEM((8, HD, WIDE + 128), BF)],
    )
    return (
        out, grad_inputs, grad_gain.reshape(D), grad_shift.reshape(D),
        grad_w_in, grad_b_in.reshape(7168), grad_w_out, grad_b_out.reshape(D),
    )


def solution(mesh):
    fine = Mesh(mesh.devices.reshape(4, 2, 2, 4, 2), SHARD + CONTEXT)
    rows = P(SHARD + CONTEXT, None)
    in_specs = (rows, P(), P(), P(SHARD, None), P(), P(SHARD, None), P(), rows)
    out_specs = (rows, rows, P(), P(), P(SHARD, None), P(), P(SHARD, None), P())
    return jax.shard_map(on_device, mesh=fine, in_specs=in_specs, out_specs=out_specs, check_vma=False)
```

```python
import functools
import math

import jax
import jax.numpy as jnp
import numpy as np
from jax import lax
from jax.experimental import pallas as pl
from jax.experimental.pallas import tpu as pltpu
from jax.sharding import Mesh
from jax.sharding import PartitionSpec as P

D = 1024
FF = 4096
H = 16
HD = 64
ROT = 32
SEQ = 1024
EPS = 1e-05
WIDE = D + 640
BF = jnp.bfloat16
F32 = jnp.float32
MIB = 1 << 20

COST = {'prepare': 0.2, 'project': 0.7000000000000001, 'attend': 0.30000000000000004, 'project_out': 0.30000000000000004, 'backward_out': 0.30000000000000004, 'backward_attend': 0.5, 'backward_w_in': 0.6000000000000001, 'backward_w_out': 0.30000000000000004, 'add_slots': 0.1, 'backward_normed': 0.4, 'sum_slots': 0.2, 'finish_out': 0.1, 'add_slot': 0.1, 'finish_in': 0.1, 'finish_weights': 0.30000000000000004}

SHARD = ("y", "zh", "core")
CONTEXT = ("x", "zl")

HEADS = ((0, 7), (8, 1), (14, 9), (6, 15), (12, 5), (4, 13), (10, 3), (2, 11))
UNITS_PER_SHARD = 7


def deal_units():
    columns = [[[], []] for _ in range(8)]
    qkv = [[kind * H + head for kind in range(3) for head in pair] for pair in HEADS]
    taken = [{unit // UNITS_PER_SHARD for unit in units} for units in qkv]
    order = []

    def place(unit):
        if unit == 112:
            return True
        shard, parity = unit // UNITS_PER_SHARD, unit % 2
        choices = sorted(range(8), key=lambda c: len(columns[c][0]) + len(columns[c][1]))
        for c in choices:
            if shard in taken[c] or len(columns[c][parity]) == 4:
                continue
            taken[c].add(shard)
            columns[c][parity].append(unit)
            if place(unit + 1):
                return True
            taken[c].remove(shard)
            columns[c][parity].pop()
        return False

    assert place(48)
    for c in range(8):
        pairs = [unit for pair in zip(*columns[c]) for unit in pair]
        order.append(qkv[c] + pairs)
    return np.array(order, np.int32)


UNITS = deal_units()
SLOT = UNITS // UNITS_PER_SHARD
SEND = np.zeros((16, 8), np.int32)
for _c in range(8):
    for _u in UNITS[_c]:
        SEND[_u // UNITS_PER_SHARD, _c] = _u % UNITS_PER_SHARD
HOME = np.zeros((112, 2), np.int32)
for _c in range(8):
    for _i, _u in enumerate(UNITS[_c]):
        HOME[_u] = (_c, _i)
COLUMN_UNITS = np.concatenate([np.array(HEADS, np.int32), UNITS[:, 6:] - 32], axis=1)
COLUMN_HOME = np.zeros((80, 2), np.int32)
for _c in range(8):
    for _i, _u in enumerate(COLUMN_UNITS[_c]):
        COLUMN_HOME[_u] = (_c, _i)


TABLE = np.concatenate([SLOT, COLUMN_UNITS // 2, UNITS // 2], axis=1).astype(np.int32)
SHARD_TABLE = np.concatenate([SEND, HOME[:, 0].reshape(16, 7)], axis=1).astype(np.int32)

def nn(left, right):
    return lax.dot_general(left, right, (((1,), (0,)), ((), ())), preferred_element_type=F32)


def nt(left, right):
    return lax.dot_general(left, right, (((1,), (1,)), ((), ())), preferred_element_type=F32)


def tn(left, right):
    return lax.dot_general(left, right, (((0,), (0,)), ((), ())), preferred_element_type=F32)


def normal(rows):
    average = jnp.mean(rows, axis=-1, keepdims=True)
    centred = rows - average
    variance = jnp.mean(centred * centred, axis=-1, keepdims=True)
    scale = lax.rsqrt(variance + EPS)
    return centred * scale, scale


def turn(values, cosines, sines):
    lane = lax.broadcasted_iota(jnp.int32, values.shape, 1) % HD
    ahead = pltpu.roll(values, 2 * HD - ROT // 2, 1)
    behind = pltpu.roll(values, ROT // 2, 1)
    return values * cosines + jnp.where(lane < ROT // 2, ahead, behind) * sines


def head_mask(values, head):
    lane = lax.broadcasted_iota(jnp.int32, values.shape, 1)
    return jnp.where((lane // HD) == head, values, jnp.zeros_like(values))


SCALE2 = HD ** (-0.5) * math.log2(math.e)
GELU_C = math.sqrt(2.0 / math.pi)
BLOCK = 256


def causal(shape, first_key, first_query):
    key = first_key + lax.broadcasted_iota(jnp.int32, shape, 0)
    query = first_query + lax.broadcasted_iota(jnp.int32, shape, 1)
    return key <= query


def block_scores(q_block, k_head, block):
    extent = (block + 1) * BLOCK
    scores = nt(k_head[:extent], q_block) * SCALE2
    last = scores[block * BLOCK:]
    last = jnp.where(causal(last.shape, 0, 0), last, -1e30)
    if block == 0:
        return last
    return jnp.concatenate([scores[: block * BLOCK], last], axis=0)


def index_of(ring, step, which, mine):
    return lax.rem(ring + step, 4) * 2 + (mine if which == 0 else 1 - mine)


def prepare_kernel(ids, table, shard_table, w_in, w_out, b_in, message, bias):
    shard, context = ids[3], ids[4]
    unit = shard_table[shard, context]
    message[:, :D] = w_in[pl.ds(pl.multiple_of(unit * HD, HD), HD), :]
    lower = lax.broadcasted_iota(jnp.int32, (HD, 128), 1) < HD
    for j in range(5):
        even = w_out[:, pl.ds(pl.multiple_of(table[context, 14 + 2 * j] * 128, 128), 128)]
        odd = w_out[:, pl.ds(pl.multiple_of(table[context, 15 + 2 * j] * 128, 128), 128)]
        tile = jnp.where(lower, even, odd)
        message[:, D + j * 128 : D + (j + 1) * 128] = tile
    lower = lax.broadcasted_iota(jnp.int32, (1, 128), 1) < HD
    for j in range(7):
        even = b_in[pl.ds(table[context, 24 + 2 * j], 1), :]
        odd = b_in[pl.ds(table[context, 25 + 2 * j], 1), :]
        bias[:, j * 128 : (j + 1) * 128] = jnp.where(lower, even, odd)


def project_kernel(ids, table, a0, b0, ar, br, af, bf, al, bl,
                   na0, nb0, nar, nbr, naf, nbf, nal, nbl, fa0, fb0, far_, fbr, faf, fbf, fal, fbl,
                   bias, gain, shift, cosines, sines, xhat, weights, weights_out, qkv, slope, gated, hidden, held):
    x, zl, core, context, y, zh = ids[0], ids[1], ids[2], ids[4], ids[5], ids[6]
    near = ((na0, nb0), (nar, nbr), (naf, nbf), (nal, nbl))
    far = ((fa0, fb0), (far_, fbr), (faf, fbf), (fal, fbl))
    for step in range(4):
        for which in (0, 1):
            place = 2 * index_of(y, step, which, zh)
            for piece, slot in ((near[step][which], place + core), (far[step][which], place + 1 - core)):
                held[slot] = piece[:, :D]
                weights_out[pl.ds(pl.multiple_of(slot * HD, HD), HD), :] = piece[:, D:]
    for i in range(14):
        weights[i * HD : (i + 1) * HD, :] = held[table[context, i]]

    for step, pair in enumerate(((a0, b0), (ar, br), (af, bf), (al, bl))):
        for which in (0, 1):
            rows = pl.ds(pl.multiple_of(index_of(x, step, which, zl) * 128, 128), 128)
            normed, _ = normal(pair[which][...].astype(F32))
            xhat[rows, :] = normed.astype(BF)
            hidden[rows, :] = (normed * gain[...] + shift[...]).astype(BF)

    @pl.loop(0, 4)
    def _(i):
        rows = pl.ds(pl.multiple_of(i * 256, 256), 256)
        proj = nt(hidden[rows, :], weights[...]) + bias[...]
        cos_rows, sin_rows = cosines[rows, :], sines[rows, :]
        qkv[rows, 0:128] = turn(proj[:, 0:128], cos_rows, sin_rows).astype(BF)
        qkv[rows, 128:256] = turn(proj[:, 128:256], cos_rows, sin_rows).astype(BF)
        qkv[rows, 256:384] = proj[:, 256:384].astype(BF)
        act = proj[:, 384:]
        square = act * act
        th = jnp.tanh(GELU_C * act * (1.0 + 0.044715 * square))
        half = 0.5 * (1.0 + th)
        gated[rows, :] = (act * half).astype(BF)
        slope[rows, :] = (
            half + 0.5 * act * (1.0 - th * th) * (GELU_C * (1.0 + 3 * 0.044715 * square))
        ).astype(BF)


def attend_kernel(qkv, gated, joined, lse):
    joined[:, 128:] = gated[...]
    keys, values = qkv[:, 128:256], qkv[:, 256:384]
    for head in range(2):
        k_head = head_mask(keys, head)
        v_head = head_mask(values, head)
        for block in range(SEQ // BLOCK):
            rows = pl.ds(block * BLOCK, BLOCK)
            scores = block_scores(qkv[rows, 0:128], k_head, block)
            largest = jnp.max(scores, axis=0, keepdims=True)
            raised = jnp.exp2(scores - largest)
            mass = jnp.sum(raised, axis=0, keepdims=True)
            lse[head : head + 1, block * BLOCK : (block + 1) * BLOCK] = largest + jnp.log2(mass)
            probs = (raised * (1.0 / mass)).astype(BF)
            result = tn(probs, v_head[: (block + 1) * BLOCK])
            if head == 0:
                joined[rows, 0:128] = result.astype(BF)
            else:
                joined[rows, 0:128] = (joined[rows, 0:128].astype(F32) + result).astype(BF)


def store_pair(zl, product, a, b):
    @pl.when(zl == 0)
    def _():
        a[...] = product[:128]
        b[...] = product[128:]

    @pl.when(zl != 0)
    def _():
        a[...] = product[128:]
        b[...] = product[:128]


def project_out_kernel(ids, joined, weights, oa, ob, ra, rb, fa, fb, la, lb):
    x, zl = ids[0], ids[1]
    for step, a, b in ((2, fa, fb), (1, ra, rb), (3, la, lb), (0, oa, ob)):
        rows = pl.ds(pl.multiple_of(lax.rem(x + step, 4) * 256, 256), 256)
        store_pair(zl, nt(joined[rows, :], weights[...]).astype(BF), a, b)


def backward_out_kernel(ids, a0, b0, ar, br, af, bf, al, bl, weights_out, slope, grad_attn, grad_ff, cot):
    x, zl = ids[0], ids[1]
    for step, pair in enumerate(((a0, b0), (ar, br), (af, bf), (al, bl))):
        for which in (0, 1):
            cot[pl.ds(pl.multiple_of(index_of(x, step, which, zl) * 128, 128), 128), :] = pair[which][...]

    @pl.loop(0, 4)
    def _(i):
        rows = pl.ds(pl.multiple_of(i * 256, 256), 256)
        grad = nn(cot[rows, :], weights_out[...])
        grad_attn[rows, :] = grad[:, :128].astype(BF)
        grad_ff[rows, :] = (grad[:, 128:] * slope[rows, :].astype(F32)).astype(BF)


def backward_attend_kernel(qkv, lse, grad_attn, grad_ff, cosines, sines, grad_proj, grad_q, grad_k, grad_v):
    keys, values = qkv[:, 128:256], qkv[:, 256:384]
    grad_k[...] = jnp.zeros_like(grad_k)
    grad_v[...] = jnp.zeros_like(grad_v)
    for head in range(2):
        k_head = head_mask(keys, head)
        v_head = head_mask(values, head)
        for block in range(SEQ // BLOCK):
            rows = pl.ds(block * BLOCK, BLOCK)
            extent = (block + 1) * BLOCK
            scores = block_scores(qkv[rows, 0:128], k_head, block)
            probs = jnp.exp2(scores - lse[head : head + 1, block * BLOCK : (block + 1) * BLOCK])
            grad_out = grad_attn[rows, :]
            grad_probs = nt(v_head[:extent], grad_out)
            delta = jnp.sum(grad_probs * probs, axis=0, keepdims=True)
            grad_scores = (probs * (grad_probs - delta)).astype(BF)
            grad_v[:extent, :] += nn(probs.astype(BF), head_mask(grad_out, head))
            grad_k[:extent, :] += nn(grad_scores, head_mask(qkv[rows, 0:128], head))
            result = tn(grad_scores, k_head[:extent])
            if head == 0:
                grad_q[rows, :] = result
            else:
                grad_q[rows, :] += result
    scale = HD ** (-0.5)
    cos_all, sin_all = cosines[...], -sines[...]
    grad_proj[:, 0:128] = turn((grad_q[...] * scale).astype(BF).astype(F32), cos_all, sin_all).astype(BF)
    grad_proj[:, 128:256] = turn((grad_k[...] * scale).astype(BF).astype(F32), cos_all, sin_all).astype(BF)
    grad_proj[:, 256:384] = grad_v[...].astype(BF)
    grad_proj[:, 384:] = grad_ff[...]


def split(values):
    high = values.astype(BF)
    return high, (values - high.astype(F32)).astype(BF)


def slot_place(ids, slot):
    return lax.rem(slot // 4 - ids[5] + 4, 4), jnp.where((slot // 2) % 2 == ids[6], 0, 1)


def backward_w_in_kernel(ids, table, grad_proj, weights, xhat, gain, shift, own, near, far, vectors):
    core, context = ids[2], ids[4]
    ones = jnp.ones((SEQ, 128), BF)
    grad_gain, grad_shift = jnp.zeros((1, D), F32), jnp.zeros((1, D), F32)
    for step in range(4):
        for side in (0, 1):
            near[step, side, :, :D] = jnp.zeros((HD, D), BF)
            far[step, side, :, :D] = jnp.zeros((HD, D), BF)
    for i in range(7):
        proj = grad_proj[:, i * 128 : (i + 1) * 128]
        product = tn(proj, xhat[...])
        column = tn(proj, ones)
        vectors[24 + i : 25 + i, :] = column.T[0:1]
        column = column[:, 0:1]
        rows = weights[i * 128 : (i + 1) * 128, :].astype(F32)
        grad_gain += jnp.sum(product * rows, axis=0, keepdims=True)
        grad_shift += jnp.sum(column * rows, axis=0, keepdims=True)
        grad = (product * gain[...] + column * shift[...]).astype(BF)
        for j in (0, 1):
            slot = table[context, 2 * i + j]
            step, side = slot_place(ids, slot)

            @pl.when(slot % 2 == core)
            def _():
                near[step, side, :, :D] = grad[j * HD : (j + 1) * HD]

            @pl.when(slot % 2 != core)
            def _():
                far[step, side, :, :D] = grad[j * HD : (j + 1) * HD]

    vectors[31:32, :] = jnp.zeros((1, 128), F32)
    grad_b_out = jnp.sum(own[...].astype(F32), axis=0, keepdims=True)
    for j in range(8):
        lanes = slice(j * 128, (j + 1) * 128)
        vectors[j : j + 1, :] = grad_gain[:, lanes]
        vectors[8 + j : 9 + j, :] = grad_shift[:, lanes]
        vectors[16 + j : 17 + j, :] = grad_b_out[:, lanes]
    high, low = split(vectors[...])
    for step in range(4):
        for side in (0, 1):
            for ref in (near, far):
                ref[step, side, :32, D:] = high
                ref[step, side, 32:, D:] = low


def backward_w_out_kernel(ids, cot, joined, near, far):
    core = ids[2]
    for j in range(8):
        grad = tn(cot[:, j * 128 : (j + 1) * 128], joined[...]).astype(BF)
        step, side = slot_place(ids, 2 * j)

        @pl.when(core == 0)
        def _():
            near[step, side] = grad[:HD]
            far[step, side] = grad[HD:]

        @pl.when(core != 0)
        def _():
            near[step, side] = grad[HD:]
            far[step, side] = grad[:HD]


def backward_normed_kernel(ids, grad_proj, weights, oa, ob, ra, rb, fa, fb, la, lb):
    x, zl = ids[0], ids[1]
    for step, a, b in ((2, fa, fb), (1, ra, rb), (3, la, lb), (0, oa, ob)):
        rows = pl.ds(pl.multiple_of(lax.rem(x + step, 4) * 256, 256), 256)
        store_pair(zl, nn(grad_proj[rows, :], weights[...]).astype(BF), a, b)


def total_vectors(*terms):
    return split(sum(term[rows, :].astype(F32) for term in terms for rows in (slice(0, 32), slice(32, 64))))


def add_slots_kernel(near_in, far_in, near_out, far_out, *parts):
    high, low = total_vectors(near_in[0, 0, :, D:], far_in[0, 0, :, D:])
    for step in range(4):
        for side in (0, 1):
            part = parts[2 * step + side]
            part[:, :D] = (near_in[step, side, :, :D].astype(F32) + far_in[step, side, :, :D].astype(F32)).astype(BF)
            part[:, D:WIDE] = (near_out[step, side].astype(F32) + far_out[step, side].astype(F32)).astype(BF)
            part[:32, WIDE:] = high
            part[32:, WIDE:] = low


def sum_slots_kernel(a0, a1, a2, b0, b1, b2, mine, other):
    high, low = total_vectors(*(part[:, WIDE:] for part in (a0, a1, a2)))
    for total, parts in ((mine, (a0, a1, a2)), (other, (b0, b1, b2))):
        total[:, :WIDE] = sum(part[:, :WIDE].astype(F32) for part in parts).astype(BF)
        total[:32, WIDE:] = high
        total[32:, WIDE:] = low


def add_slot_kernel(mine, far, total):
    total[:, :WIDE] = (mine[:, :WIDE].astype(F32) + far[:, :WIDE].astype(F32)).astype(BF)
    high, low = total_vectors(mine[:, WIDE:], far[:, WIDE:])
    total[:32, WIDE:] = high
    total[32:, WIDE:] = low


def finish_out_kernel(oa, ra, la, far, inputs, b_out, out):
    mixed = sum(term[...].astype(F32) for term in (oa, ra, la, far))
    out[...] = (inputs[...].astype(F32) + mixed + b_out[...]).astype(BF)


def finish_in_kernel(oa, ra, la, far, inputs, cotangent, gain, grad_inputs):
    grad = sum(term[...].astype(F32) for term in (oa, ra, la, far))
    own, scale = normal(inputs[...].astype(F32))
    pulled = grad * gain[...]
    rows = (
        pulled
        - jnp.mean(pulled, axis=-1, keepdims=True)
        - own * jnp.mean(pulled * own, axis=-1, keepdims=True)
    ) * scale
    grad_inputs[...] = (cotangent[...].astype(F32) + rows).astype(BF)


def finish_weights_kernel(ids, shard_table, a0, b0, ar, br, af, bf, al, bl,
                          grad_w_in, grad_w_out, grad_gain, grad_shift, grad_b_out, grad_b_in, held):
    for step, pair in enumerate(((a0, b0), (ar, br), (af, bf), (al, bl))):
        for which in (0, 1):
            held[index_of(ids[0], step, which, ids[1])] = pair[which][...]
    for i in range(7):
        grad_w_in[i * HD : (i + 1) * HD, :] = held[shard_table[ids[3], 8 + i], :, :D].astype(F32)
    lower = lax.broadcasted_iota(jnp.int32, (HD, 128), 1) < HD
    for t in range(40):
        tiles = []
        for unit in (2 * t, 2 * t + 1):
            c, i = (int(n) for n in COLUMN_HOME[unit])
            first = D + (i // 2) * 128
            tiles.append(held[c, :, first : first + 128].astype(F32))
        grad_w_out[:, t * 128 : (t + 1) * 128] = jnp.where(lower, *tiles)
    terms = [held[c, :32, WIDE:].astype(F32) + held[c, 32:, WIDE:].astype(F32) for c in range(8)]
    total = sum(term[:24] for term in terms)
    grad_gain[...] = total[0:8]
    grad_shift[...] = total[8:16]
    grad_b_out[...] = total[16:24]
    lower = lax.broadcasted_iota(jnp.int32, (1, 128), 1) < HD
    for row in range(56):
        (c, i), (d, j) = (tuple(int(n) for n in HOME[unit]) for unit in (2 * row, 2 * row + 1))
        grad_b_in[row : row + 1, :] = jnp.where(
            lower, terms[c][24 + i // 2 : 25 + i // 2], terms[d][24 + j // 2 : 25 + j // 2]
        )


VM = pl.BlockSpec(memory_space=pltpu.VMEM)
SM = pl.BlockSpec(memory_space=pltpu.SMEM)
S = jax.ShapeDtypeStruct


def kernel(body, outs, scalars, operands, name, us, scratch=()):
    return pl.pallas_call(
        body,
        out_shape=outs,
        in_specs=[SM] * len(scalars) + [VM] * len(operands),
        out_specs=jax.tree.map(lambda _: VM, outs),
        scratch_shapes=list(scratch),
        compiler_params=pltpu.CompilerParams(vmem_limit_bytes=24 * MIB),
        cost_estimate=pl.CostEstimate(flops=int(COST[name] * 1e9), bytes_accessed=int(COST[name] * 3e6), transcendentals=0),
        name=name,
    )(*scalars, *operands)


def hbm(*arrays):
    return tuple(pltpu.with_memory_space_constraint(array, pltpu.HBM) for array in arrays)


def shift(values, axis, by):
    return lax.ppermute(values, axis, [(i, (i + by) % 4) for i in range(4)])


def swap(values, axis):
    return lax.ppermute(values, axis, [(0, 1), (1, 0)])


def gather_ring(pair, axis):
    ahead, behind = shift(pair, axis, -1), shift(pair, axis, 1)
    return pair, ahead, shift(pair, axis, 2), behind


def scatter_ring(p0, p1, p2, p3, axis):
    return p0, shift(p1, axis, 1), shift(p3, axis, -1), shift(p2, axis, 2)


def ordered(index, mine, other):
    return jnp.stack([jnp.where(index == 0, mine, other), jnp.where(index == 0, other, mine)])


def pick(pair, index):
    return lax.dynamic_index_in_dim(pair, index, 0, keepdims=False)


def add(*terms):
    return sum(term.astype(F32) for term in terms).astype(BF)


def after(values, *events):
    return lax.optimization_barrier((values,) + events)


def turn_tables():
    steps = np.arange(ROT // 2)
    angles = np.arange(SEQ)[:, None] * (10000.0 ** (-2.0 * steps / ROT))[None, :]
    cosine, sine = np.cos(angles), np.sin(angles)
    still = np.ones((SEQ, HD - ROT))
    cosines = np.concatenate([cosine, cosine, still] * 2, axis=1)
    sines = np.concatenate([-sine, sine, 0.0 * still] * 2, axis=1)
    return jnp.asarray(cosines.astype(np.float32)), jnp.asarray(sines.astype(np.float32))


def on_device(inputs, ln_gain, ln_bias, w_in, b_in, w_out, b_out, cotangent):
    ids = jnp.stack(
        [lax.axis_index(axes) for axes in ("x", "zl", "core", SHARD, CONTEXT, "y", "zh")]
    ).astype(jnp.int32)
    table, shard_table = jnp.asarray(TABLE), jnp.asarray(SHARD_TABLE)
    cosines, sines = turn_tables()
    gain, shift_row = ln_gain[None], ln_bias[None]
    right, left = lambda v: shift(v, "x", 1), lambda v: shift(v, "x", -1)
    up, down = lambda v: shift(v, "y", 1), lambda v: shift(v, "y", -1)

    chunk = S((128, D), BF)
    message, bias = kernel(
        prepare_kernel, (S((HD, 1664), BF), S((1, 896), F32)), (ids, *hbm(table, shard_table)),
        hbm(w_in, w_out, b_in.reshape(56, 128)), "prepare", 2,
    )
    first = inputs
    b0, al, ar = swap(first, "zl"), right(first), left(first)
    later, b0_ = after(message, b0)
    nb0 = swap(later, "zh")
    nal, nar = up(message), down(message)
    bl, br, af = right(b0), left(b0), right(al)
    cot = cotangent
    br, ar, al = after(br, ar, al)
    bf = left(br)
    nbl, nbr, naf = up(nb0), down(nb0), up(nal)
    nbf = down(nbr)
    af_, bl_ = af, bl
    nbf, af_, bl_ = after(nbf, af, bl)
    near = later, nb0, nar, nbr, naf, nbf, nal, nbl
    far = [swap(piece, "core") for piece in near]
    cot, bl_ = after(cot, bl_)
    cb0, cal, car = swap(cot, "zl"), right(cot), left(cot)
    caf = shift(cot, "x", 2)

    xhat, weights_in, weights_out, qkv, slope, gated = kernel(
        project_kernel,
        (S((SEQ, D), BF), S((896, D), BF), S((D, 640), BF), S((SEQ, 384), BF), S((SEQ, 512), BF), S((SEQ, 512), BF)),
        (ids, table), (inputs, b0_, ar, br, af_, bf, al, bl_, *near, *far, bias, gain, shift_row, cosines, sines),
        "project", 7, [pltpu.VMEM((SEQ, D), BF), pltpu.VMEM((16, HD, D), BF)],
    )
    qkv, cb0 = after(qkv, cb0)
    cbl, cbr = right(cb0), left(cb0)
    cbf = shift(cb0, "x", 2)
    joined, lse = kernel(attend_kernel, (S((SEQ, 640), BF), S((8, SEQ), F32)), (), (qkv, gated), "attend", 3)
    oa, ob, ra, rb, fa, fb, la, lb = kernel(
        project_out_kernel, (chunk,) * 8, (ids,), (joined, weights_out), "project_out", 3
    )
    fa, fb = right(fa), left(fb)
    grad_attn, grad_ff, cots = kernel(
        backward_out_kernel, (S((SEQ, 128), BF), S((SEQ, 512), BF), S((SEQ, D), BF)), (ids,),
        (cot, cb0, car, cbr, caf, cbf, cal, cbl, weights_out, slope), "backward_out", 3,
    )
    grad_proj = kernel(
        backward_attend_kernel, S((SEQ, 896), BF), (), (qkv, lse, grad_attn, grad_ff, cosines, sines),
        "backward_attend", 5, [pltpu.VMEM((SEQ, 128), F32)] * 3,
    )
    grad_proj, fa, fb = after(grad_proj, fa, fb)
    slots = lambda columns: S((4, 2, HD, columns), BF)
    wide = D + 128
    near_in, far_in = kernel(
        backward_w_in_kernel, (slots(wide), slots(wide)), (ids, table),
        (grad_proj, weights_in, xhat, gain, shift_row, cotangent), "backward_w_in", 6, [pltpu.VMEM((32, 128), F32)],
    )
    far_in = swap(far_in, "core")

    near_out, far_out = kernel(
        backward_w_out_kernel, (slots(640), slots(640)), (ids,), (cots, joined), "backward_w_out", 3
    )
    far_out = swap(far_out, "core")
    grad_proj, near_out = after(grad_proj, near_out)
    parts = kernel(backward_normed_kernel, (chunk,) * 8, (ids,), (grad_proj, weights_in), "backward_normed", 4)
    far_in, *parts = after(far_in, *parts)
    slot = S((HD, WIDE + 128), BF)
    wa, wb, wua, wub, wfa, wfb, wda, wdb = kernel(
        add_slots_kernel, (slot,) * 8, (), (near_in, far_in, near_out, far_out), "add_slots", 1
    )
    wfa, wfb, wub, wda = up(wfa), down(wfb), up(wub), down(wda)
    wua = up(kernel(add_slot_kernel, slot, (), (wua, wfa), "add_slot", 1))
    wdb = down(kernel(add_slot_kernel, slot, (), (wdb, wfb), "add_slot", 1))
    goa, gob, gra, grb, gfa, gfb, gla, glb = parts
    gfa, gfb, grb, gla = right(gfa), left(gfb), right(grb), left(gla)

    ra, lb = add(ra, fa), add(lb, fb)
    ra, lb = right(ra), left(lb)
    rb, la = right(rb), left(la)
    gra, glb = right(add(gra, gfa)), left(add(glb, gfb))
    wua, grb, gla, gra, glb = after(wua, grb, gla, gra, glb)
    mine, other = kernel(sum_slots_kernel, (slot, slot), (), (wa, wua, wda, wb, wub, wdb), "sum_slots", 2)
    far = swap(other, "zh")
    ob = swap(add(ob, rb, lb), "zl")
    gob = swap(add(gob, grb, glb), "zl")
    far, rb, la = after(far, rb, la)
    a0 = kernel(add_slot_kernel, slot, (), (mine, far), "add_slot", 1)
    b0, al, ar = swap(a0, "zl"), right(a0), left(a0)
    bl, br, af = right(b0), left(b0), right(al)
    br, ar, al = after(br, ar, al)
    bf = left(br)
    out = kernel(finish_out_kernel, chunk, (), (oa, ra, la, ob, inputs, b_out[None]), "finish_out", 1)
    grad_inputs = kernel(finish_in_kernel, chunk, (), (goa, gra, gla, gob, inputs, cotangent, gain), "finish_in", 1)
    row = S((8, 128), F32)
    grad_w_in, grad_w_out, grad_gain, grad_shift, grad_b_out, grad_b_in = kernel(
        finish_weights_kernel, (S((448, D), F32), S((HD, 5120), F32), row, row, row, S((56, 128), F32)),
        (ids, shard_table), (a0, b0, ar, br, af, bf, al, bl), "finish_weights", 3, [pltpu.VMEM((8, HD, WIDE + 128), BF)],
    )
    return (
        out, grad_inputs, grad_gain.reshape(D), grad_shift.reshape(D),
        grad_w_in, grad_b_in.reshape(7168), grad_w_out, grad_b_out.reshape(D),
    )


def solution(mesh):
    fine = Mesh(mesh.devices.reshape(4, 2, 2, 4, 2), SHARD + CONTEXT)
    rows = P(SHARD + CONTEXT, None)
    in_specs = (rows, P(), P(), P(SHARD, None), P(), P(SHARD, None), P(), rows)
    out_specs = (rows, rows, P(), P(), P(SHARD, None), P(), P(SHARD, None), P())
    return jax.shard_map(on_device, mesh=fine, in_specs=in_specs, out_specs=out_specs, check_vma=False)
```

```python
import functools
import math

import jax
import jax.numpy as jnp
import numpy as np
from jax import lax
from jax.experimental import pallas as pl
from jax.experimental.pallas import tpu as pltpu
from jax.sharding import Mesh
from jax.sharding import PartitionSpec as P

D = 1024
FF = 4096
H = 16
HD = 64
ROT = 32
SEQ = 1024
EPS = 1e-05
WIDE = D + 640
BF = jnp.bfloat16
F32 = jnp.float32
MIB = 1 << 20

COST = {'prepare': 0.2, 'project': 0.7000000000000001, 'attend': 0.30000000000000004, 'project_out': 0.30000000000000004, 'backward_out': 0.30000000000000004, 'backward_attend': 0.5, 'backward_w_in': 0.6000000000000001, 'backward_w_out': 0.30000000000000004, 'add_slots': 0.1, 'backward_normed': 0.4, 'sum_slots': 0.2, 'add_slot': 0.1, 'finish_tokens': 0.1, 'finish_weights': 0.30000000000000004}

SHARD = ("y", "zh", "core")
CONTEXT = ("x", "zl")

HEADS = ((0, 7), (8, 1), (14, 9), (6, 15), (12, 5), (4, 13), (10, 3), (2, 11))
UNITS_PER_SHARD = 7


def deal_units():
    columns = [[[], []] for _ in range(8)]
    qkv = [[kind * H + head for kind in range(3) for head in pair] for pair in HEADS]
    taken = [{unit // UNITS_PER_SHARD for unit in units} for units in qkv]
    order = []

    def place(unit):
        if unit == 112:
            return True
        shard, parity = unit // UNITS_PER_SHARD, unit % 2
        choices = sorted(range(8), key=lambda c: len(columns[c][0]) + len(columns[c][1]))
        for c in choices:
            if shard in taken[c] or len(columns[c][parity]) == 4:
                continue
            taken[c].add(shard)
            columns[c][parity].append(unit)
            if place(unit + 1):
                return True
            taken[c].remove(shard)
            columns[c][parity].pop()
        return False

    assert place(48)
    for c in range(8):
        pairs = [unit for pair in zip(*columns[c]) for unit in pair]
        order.append(qkv[c] + pairs)
    return np.array(order, np.int32)


UNITS = deal_units()
SLOT = UNITS // UNITS_PER_SHARD
SEND = np.zeros((16, 8), np.int32)
for _c in range(8):
    for _u in UNITS[_c]:
        SEND[_u // UNITS_PER_SHARD, _c] = _u % UNITS_PER_SHARD
HOME = np.zeros((112, 2), np.int32)
for _c in range(8):
    for _i, _u in enumerate(UNITS[_c]):
        HOME[_u] = (_c, _i)
COLUMN_UNITS = np.concatenate([np.array(HEADS, np.int32), UNITS[:, 6:] - 32], axis=1)
COLUMN_HOME = np.zeros((80, 2), np.int32)
for _c in range(8):
    for _i, _u in enumerate(COLUMN_UNITS[_c]):
        COLUMN_HOME[_u] = (_c, _i)


TABLE = np.concatenate([SLOT, COLUMN_UNITS // 2, UNITS // 2], axis=1).astype(np.int32)
SHARD_TABLE = np.concatenate([SEND, HOME[:, 0].reshape(16, 7)], axis=1).astype(np.int32)

def nn(left, right):
    return lax.dot_general(left, right, (((1,), (0,)), ((), ())), preferred_element_type=F32)


def nt(left, right):
    return lax.dot_general(left, right, (((1,), (1,)), ((), ())), preferred_element_type=F32)


def tn(left, right):
    return lax.dot_general(left, right, (((0,), (0,)), ((), ())), preferred_element_type=F32)


def normal(rows):
    average = jnp.mean(rows, axis=-1, keepdims=True)
    centred = rows - average
    variance = jnp.mean(centred * centred, axis=-1, keepdims=True)
    scale = lax.rsqrt(variance + EPS)
    return centred * scale, scale


def turn(values, cosines, sines):
    lane = lax.broadcasted_iota(jnp.int32, values.shape, 1) % HD
    ahead = pltpu.roll(values, 2 * HD - ROT // 2, 1)
    behind = pltpu.roll(values, ROT // 2, 1)
    return values * cosines + jnp.where(lane < ROT // 2, ahead, behind) * sines


def head_mask(values, head):
    lane = lax.broadcasted_iota(jnp.int32, values.shape, 1)
    return jnp.where((lane // HD) == head, values, jnp.zeros_like(values))


SCALE2 = HD ** (-0.5) * math.log2(math.e)
GELU_C = math.sqrt(2.0 / math.pi)
BLOCK = 256


def causal(shape, first_key, first_query):
    key = first_key + lax.broadcasted_iota(jnp.int32, shape, 0)
    query = first_query + lax.broadcasted_iota(jnp.int32, shape, 1)
    return key <= query


def block_scores(q_block, k_head, block):
    extent = (block + 1) * BLOCK
    scores = nt(k_head[:extent], q_block) * SCALE2
    last = scores[block * BLOCK:]
    last = jnp.where(causal(last.shape, 0, 0), last, -1e30)
    if block == 0:
        return last
    return jnp.concatenate([scores[: block * BLOCK], last], axis=0)


def index_of(ring, step, which, mine):
    return lax.rem(ring + step, 4) * 2 + (mine if which == 0 else 1 - mine)


def prepare_kernel(ids, table, shard_table, w_in, w_out, b_in, message, bias):
    shard, context = ids[3], ids[4]
    unit = shard_table[shard, context]
    message[:, :D] = w_in[pl.ds(pl.multiple_of(unit * HD, HD), HD), :]
    lower = lax.broadcasted_iota(jnp.int32, (HD, 128), 1) < HD
    for j in range(5):
        even = w_out[:, pl.ds(pl.multiple_of(table[context, 14 + 2 * j] * 128, 128), 128)]
        odd = w_out[:, pl.ds(pl.multiple_of(table[context, 15 + 2 * j] * 128, 128), 128)]
        tile = jnp.where(lower, even, odd)
        message[:, D + j * 128 : D + (j + 1) * 128] = tile
    lower = lax.broadcasted_iota(jnp.int32, (1, 128), 1) < HD
    for j in range(7):
        even = b_in[pl.ds(table[context, 24 + 2 * j], 1), :]
        odd = b_in[pl.ds(table[context, 25 + 2 * j], 1), :]
        bias[:, j * 128 : (j + 1) * 128] = jnp.where(lower, even, odd)


def project_kernel(ids, table, a0, b0, ar, br, af, bf, al, bl,
                   na0, nb0, nar, nbr, naf, nbf, nal, nbl, fa0, fb0, far_, fbr, faf, fbf, fal, fbl,
                   bias, gain, shift, cosines, sines, xhat, weights, weights_out, qkv, slope, gated, hidden, held):
    x, zl, core, context, y, zh = ids[0], ids[1], ids[2], ids[4], ids[5], ids[6]
    near = ((na0, nb0), (nar, nbr), (naf, nbf), (nal, nbl))
    far = ((fa0, fb0), (far_, fbr), (faf, fbf), (fal, fbl))
    for step in range(4):
        for which in (0, 1):
            place = 2 * index_of(y, step, which, zh)
            for piece, slot in ((near[step][which], place + core), (far[step][which], place + 1 - core)):
                held[slot] = piece[:, :D]
                weights_out[pl.ds(pl.multiple_of(slot * HD, HD), HD), :] = piece[:, D:]
    for i in range(14):
        weights[i * HD : (i + 1) * HD, :] = held[table[context, i]]

    for step, pair in enumerate(((a0, b0), (ar, br), (af, bf), (al, bl))):
        for which in (0, 1):
            rows = pl.ds(pl.multiple_of(index_of(x, step, which, zl) * 128, 128), 128)
            normed, _ = normal(pair[which][...].astype(F32))
            xhat[rows, :] = normed.astype(BF)
            hidden[rows, :] = (normed * gain[...] + shift[...]).astype(BF)

    @pl.loop(0, 4)
    def _(i):
        rows = pl.ds(pl.multiple_of(i * 256, 256), 256)
        proj = nt(hidden[rows, :], weights[...]) + bias[...]
        cos_rows, sin_rows = cosines[rows, :], sines[rows, :]
        qkv[rows, 0:128] = turn(proj[:, 0:128], cos_rows, sin_rows).astype(BF)
        qkv[rows, 128:256] = turn(proj[:, 128:256], cos_rows, sin_rows).astype(BF)
        qkv[rows, 256:384] = proj[:, 256:384].astype(BF)
        act = proj[:, 384:]
        square = act * act
        th = jnp.tanh(GELU_C * act * (1.0 + 0.044715 * square))
        half = 0.5 * (1.0 + th)
        gated[rows, :] = (act * half).astype(BF)
        slope[rows, :] = (
            half + 0.5 * act * (1.0 - th * th) * (GELU_C * (1.0 + 3 * 0.044715 * square))
        ).astype(BF)


def attend_kernel(qkv, gated, joined, lse):
    joined[:, 128:] = gated[...]
    keys, values = qkv[:, 128:256], qkv[:, 256:384]
    for head in range(2):
        k_head = head_mask(keys, head)
        v_head = head_mask(values, head)
        for block in range(SEQ // BLOCK):
            rows = pl.ds(block * BLOCK, BLOCK)
            scores = block_scores(qkv[rows, 0:128], k_head, block)
            largest = jnp.max(scores, axis=0, keepdims=True)
            raised = jnp.exp2(scores - largest)
            mass = jnp.sum(raised, axis=0, keepdims=True)
            lse[head : head + 1, block * BLOCK : (block + 1) * BLOCK] = largest + jnp.log2(mass)
            probs = (raised * (1.0 / mass)).astype(BF)
            result = tn(probs, v_head[: (block + 1) * BLOCK])
            if head == 0:
                joined[rows, 0:128] = result.astype(BF)
            else:
                joined[rows, 0:128] = (joined[rows, 0:128].astype(F32) + result).astype(BF)


def store_pair(zl, product, a, b):
    @pl.when(zl == 0)
    def _():
        a[...] = product[:128]
        b[...] = product[128:]

    @pl.when(zl != 0)
    def _():
        a[...] = product[128:]
        b[...] = product[:128]


def project_out_kernel(ids, joined, weights, oa, ob, ra, rb, fa, fb, la, lb):
    x, zl = ids[0], ids[1]
    for step, a, b in ((2, fa, fb), (1, ra, rb), (3, la, lb), (0, oa, ob)):
        rows = pl.ds(pl.multiple_of(lax.rem(x + step, 4) * 256, 256), 256)
        store_pair(zl, nt(joined[rows, :], weights[...]).astype(BF), a, b)


def backward_out_kernel(ids, a0, b0, ar, br, af, bf, al, bl, weights_out, slope, grad_attn, grad_ff, cot):
    x, zl = ids[0], ids[1]
    for step, pair in enumerate(((a0, b0), (ar, br), (af, bf), (al, bl))):
        for which in (0, 1):
            cot[pl.ds(pl.multiple_of(index_of(x, step, which, zl) * 128, 128), 128), :] = pair[which][...]

    @pl.loop(0, 4)
    def _(i):
        rows = pl.ds(pl.multiple_of(i * 256, 256), 256)
        grad = nn(cot[rows, :], weights_out[...])
        grad_attn[rows, :] = grad[:, :128].astype(BF)
        grad_ff[rows, :] = (grad[:, 128:] * slope[rows, :].astype(F32)).astype(BF)


def backward_attend_kernel(qkv, lse, grad_attn, grad_ff, cosines, sines, grad_proj, grad_q, grad_k, grad_v):
    keys, values = qkv[:, 128:256], qkv[:, 256:384]
    grad_k[...] = jnp.zeros_like(grad_k)
    grad_v[...] = jnp.zeros_like(grad_v)
    for head in range(2):
        k_head = head_mask(keys, head)
        v_head = head_mask(values, head)
        for block in range(SEQ // BLOCK):
            rows = pl.ds(block * BLOCK, BLOCK)
            extent = (block + 1) * BLOCK
            scores = block_scores(qkv[rows, 0:128], k_head, block)
            probs = jnp.exp2(scores - lse[head : head + 1, block * BLOCK : (block + 1) * BLOCK])
            grad_out = grad_attn[rows, :]
            grad_probs = nt(v_head[:extent], grad_out)
            delta = jnp.sum(grad_probs * probs, axis=0, keepdims=True)
            grad_scores = (probs * (grad_probs - delta)).astype(BF)
            grad_v[:extent, :] += nn(probs.astype(BF), head_mask(grad_out, head))
            grad_k[:extent, :] += nn(grad_scores, head_mask(qkv[rows, 0:128], head))
            result = tn(grad_scores, k_head[:extent])
            if head == 0:
                grad_q[rows, :] = result
            else:
                grad_q[rows, :] += result
    scale = HD ** (-0.5)
    cos_all, sin_all = cosines[...], -sines[...]
    grad_proj[:, 0:128] = turn((grad_q[...] * scale).astype(BF).astype(F32), cos_all, sin_all).astype(BF)
    grad_proj[:, 128:256] = turn((grad_k[...] * scale).astype(BF).astype(F32), cos_all, sin_all).astype(BF)
    grad_proj[:, 256:384] = grad_v[...].astype(BF)
    grad_proj[:, 384:] = grad_ff[...]


def split(values):
    high = values.astype(BF)
    return high, (values - high.astype(F32)).astype(BF)


def slot_place(ids, slot):
    return lax.rem(slot // 4 - ids[5] + 4, 4), jnp.where((slot // 2) % 2 == ids[6], 0, 1)


def backward_w_in_kernel(ids, table, grad_proj, weights, xhat, gain, shift, own, near, far, vectors):
    core, context = ids[2], ids[4]
    ones = jnp.ones((SEQ, 128), BF)
    grad_gain, grad_shift = jnp.zeros((1, D), F32), jnp.zeros((1, D), F32)
    for step in range(4):
        for side in (0, 1):
            near[step, side, :, :D] = jnp.zeros((HD, D), BF)
            far[step, side, :, :D] = jnp.zeros((HD, D), BF)
    for i in range(7):
        proj = grad_proj[:, i * 128 : (i + 1) * 128]
        product = tn(proj, xhat[...])
        column = tn(proj, ones)
        vectors[24 + i : 25 + i, :] = column.T[0:1]
        column = column[:, 0:1]
        rows = weights[i * 128 : (i + 1) * 128, :].astype(F32)
        grad_gain += jnp.sum(product * rows, axis=0, keepdims=True)
        grad_shift += jnp.sum(column * rows, axis=0, keepdims=True)
        grad = (product * gain[...] + column * shift[...]).astype(BF)
        for j in (0, 1):
            slot = table[context, 2 * i + j]
            step, side = slot_place(ids, slot)

            @pl.when(slot % 2 == core)
            def _():
                near[step, side, :, :D] = grad[j * HD : (j + 1) * HD]

            @pl.when(slot % 2 != core)
            def _():
                far[step, side, :, :D] = grad[j * HD : (j + 1) * HD]

    vectors[31:32, :] = jnp.zeros((1, 128), F32)
    grad_b_out = jnp.sum(own[...].astype(F32), axis=0, keepdims=True)
    for j in range(8):
        lanes = slice(j * 128, (j + 1) * 128)
        vectors[j : j + 1, :] = grad_gain[:, lanes]
        vectors[8 + j : 9 + j, :] = grad_shift[:, lanes]
        vectors[16 + j : 17 + j, :] = grad_b_out[:, lanes]
    high, low = split(vectors[...])
    for step in range(4):
        for side in (0, 1):
            for ref in (near, far):
                ref[step, side, :32, D:] = high
                ref[step, side, 32:, D:] = low


def backward_w_out_kernel(ids, cot, joined, near, far):
    core = ids[2]
    for j in range(8):
        grad = tn(cot[:, j * 128 : (j + 1) * 128], joined[...]).astype(BF)
        step, side = slot_place(ids, 2 * j)

        @pl.when(core == 0)
        def _():
            near[step, side] = grad[:HD]
            far[step, side] = grad[HD:]

        @pl.when(core != 0)
        def _():
            near[step, side] = grad[HD:]
            far[step, side] = grad[:HD]


def backward_normed_kernel(ids, grad_proj, weights, out_rb, out_la, oa, ob, ra, rb, fa, fb, la, lb):
    x, zl = ids[0], ids[1]
    for step, a, b in ((2, fa, fb), (1, ra, rb.at[0]), (3, la.at[0], lb), (0, oa, ob)):
        rows = pl.ds(pl.multiple_of(lax.rem(x + step, 4) * 256, 256), 256)
        store_pair(zl, nn(grad_proj[rows, :], weights[...]).astype(BF), a, b)
    rb[1] = out_rb[...]
    la[1] = out_la[...]


def total_vectors(*terms):
    return split(sum(term[rows, :].astype(F32) for term in terms for rows in (slice(0, 32), slice(32, 64))))


def add_slots_kernel(near_in, far_in, near_out, far_out, *parts):
    high, low = total_vectors(near_in[0, 0, :, D:], far_in[0, 0, :, D:])
    for step in range(4):
        for side in (0, 1):
            part = parts[2 * step + side]
            part[:, :D] = (near_in[step, side, :, :D].astype(F32) + far_in[step, side, :, :D].astype(F32)).astype(BF)
            part[:, D:WIDE] = (near_out[step, side].astype(F32) + far_out[step, side].astype(F32)).astype(BF)
            part[:32, WIDE:] = high
            part[32:, WIDE:] = low


def sum_slots_kernel(a0, a1, a2, b0, b1, b2, mine, other):
    high, low = total_vectors(*(part[:, WIDE:] for part in (a0, a1, a2)))
    for total, parts in ((mine, (a0, a1, a2)), (other, (b0, b1, b2))):
        total[:, :WIDE] = sum(part[:, :WIDE].astype(F32) for part in parts).astype(BF)
        total[:32, WIDE:] = high
        total[32:, WIDE:] = low


def add_slot_kernel(mine, far, total):
    total[:, :WIDE] = (mine[:, :WIDE].astype(F32) + far[:, :WIDE].astype(F32)).astype(BF)
    high, low = total_vectors(mine[:, WIDE:], far[:, WIDE:])
    total[:32, WIDE:] = high
    total[32:, WIDE:] = low


def finish_tokens_kernel(goa, oa, ra, la, far, inputs, cotangent, gain, b_out, grad_inputs, out):
    grad, mixed = (
        own[...].astype(F32) + sum(term[k].astype(F32) for term in (ra, la, far)) for k, own in ((0, goa), (1, oa))
    )
    rows = inputs[...].astype(F32)
    out[...] = (rows + mixed + b_out[...]).astype(BF)
    own, scale = normal(rows)
    pulled = grad * gain[...]
    pulled = (
        pulled
        - jnp.mean(pulled, axis=-1, keepdims=True)
        - own * jnp.mean(pulled * own, axis=-1, keepdims=True)
    ) * scale
    grad_inputs[...] = (cotangent[...].astype(F32) + pulled).astype(BF)


def finish_weights_kernel(ids, shard_table, a0, b0, ar, br, af, bf, al, bl,
                          grad_w_in, grad_w_out, grad_gain, grad_shift, grad_b_out, grad_b_in, held):
    for step, pair in enumerate(((a0, b0), (ar, br), (af, bf), (al, bl))):
        for which in (0, 1):
            held[index_of(ids[0], step, which, ids[1])] = pair[which][...]
    for i in range(7):
        grad_w_in[i * HD : (i + 1) * HD, :] = held[shard_table[ids[3], 8 + i], :, :D].astype(F32)
    lower = lax.broadcasted_iota(jnp.int32, (HD, 128), 1) < HD
    for t in range(40):
        tiles = []
        for unit in (2 * t, 2 * t + 1):
            c, i = (int(n) for n in COLUMN_HOME[unit])
            first = D + (i // 2) * 128
            tiles.append(held[c, :, first : first + 128].astype(F32))
        grad_w_out[:, t * 128 : (t + 1) * 128] = jnp.where(lower, *tiles)
    terms = [held[c, :32, WIDE:].astype(F32) + held[c, 32:, WIDE:].astype(F32) for c in range(8)]
    total = sum(term[:24] for term in terms)
    grad_gain[...] = total[0:8]
    grad_shift[...] = total[8:16]
    grad_b_out[...] = total[16:24]
    lower = lax.broadcasted_iota(jnp.int32, (1, 128), 1) < HD
    for row in range(56):
        (c, i), (d, j) = (tuple(int(n) for n in HOME[unit]) for unit in (2 * row, 2 * row + 1))
        grad_b_in[row : row + 1, :] = jnp.where(
            lower, terms[c][24 + i // 2 : 25 + i // 2], terms[d][24 + j // 2 : 25 + j // 2]
        )


VM = pl.BlockSpec(memory_space=pltpu.VMEM)
SM = pl.BlockSpec(memory_space=pltpu.SMEM)
S = jax.ShapeDtypeStruct


def kernel(body, outs, scalars, operands, name, us, scratch=()):
    return pl.pallas_call(
        body,
        out_shape=outs,
        in_specs=[SM] * len(scalars) + [VM] * len(operands),
        out_specs=jax.tree.map(lambda _: VM, outs),
        scratch_shapes=list(scratch),
        compiler_params=pltpu.CompilerParams(vmem_limit_bytes=24 * MIB),
        cost_estimate=pl.CostEstimate(flops=int(COST[name] * 1e9), bytes_accessed=int(COST[name] * 3e6), transcendentals=0),
        name=name,
    )(*scalars, *operands)


def hbm(*arrays):
    return tuple(pltpu.with_memory_space_constraint(array, pltpu.HBM) for array in arrays)


def shift(values, axis, by):
    return lax.ppermute(values, axis, [(i, (i + by) % 4) for i in range(4)])


def swap(values, axis):
    return lax.ppermute(values, axis, [(0, 1), (1, 0)])


def gather_ring(pair, axis):
    ahead, behind = shift(pair, axis, -1), shift(pair, axis, 1)
    return pair, ahead, shift(pair, axis, 2), behind


def scatter_ring(p0, p1, p2, p3, axis):
    return p0, shift(p1, axis, 1), shift(p3, axis, -1), shift(p2, axis, 2)


def ordered(index, mine, other):
    return jnp.stack([jnp.where(index == 0, mine, other), jnp.where(index == 0, other, mine)])


def pick(pair, index):
    return lax.dynamic_index_in_dim(pair, index, 0, keepdims=False)


def add(*terms):
    return sum(term.astype(F32) for term in terms).astype(BF)


def after(values, *events):
    return lax.optimization_barrier((values,) + events)


def turn_tables():
    steps = np.arange(ROT // 2)
    angles = np.arange(SEQ)[:, None] * (10000.0 ** (-2.0 * steps / ROT))[None, :]
    cosine, sine = np.cos(angles), np.sin(angles)
    still = np.ones((SEQ, HD - ROT))
    cosines = np.concatenate([cosine, cosine, still] * 2, axis=1)
    sines = np.concatenate([-sine, sine, 0.0 * still] * 2, axis=1)
    return jnp.asarray(cosines.astype(np.float32)), jnp.asarray(sines.astype(np.float32))


def on_device(inputs, ln_gain, ln_bias, w_in, b_in, w_out, b_out, cotangent):
    ids = jnp.stack(
        [lax.axis_index(axes) for axes in ("x", "zl", "core", SHARD, CONTEXT, "y", "zh")]
    ).astype(jnp.int32)
    table, shard_table = jnp.asarray(TABLE), jnp.asarray(SHARD_TABLE)
    cosines, sines = turn_tables()
    gain, shift_row = ln_gain[None], ln_bias[None]
    right, left = lambda v: shift(v, "x", 1), lambda v: shift(v, "x", -1)
    up, down = lambda v: shift(v, "y", 1), lambda v: shift(v, "y", -1)

    chunk = S((128, D), BF)
    message, bias = kernel(
        prepare_kernel, (S((HD, 1664), BF), S((1, 896), F32)), (ids, *hbm(table, shard_table)),
        hbm(w_in, w_out, b_in.reshape(56, 128)), "prepare", 2,
    )
    first = inputs
    b0, al, ar = swap(first, "zl"), right(first), left(first)
    later, b0_ = after(message, b0)
    nb0 = swap(later, "zh")
    nal, nar = up(message), down(message)
    bl, br, af = right(b0), left(b0), right(al)
    cot = cotangent
    br, ar, al = after(br, ar, al)
    bf = left(br)
    nbl, nbr, naf = up(nb0), down(nb0), up(nal)
    nbf = down(nbr)
    af_, bl_ = af, bl
    nbf, af_, bl_ = after(nbf, af, bl)
    near = later, nb0, nar, nbr, naf, nbf, nal, nbl
    far = [swap(piece, "core") for piece in near]
    cot, bl_ = after(cot, bl_)
    cb0, cal, car = swap(cot, "zl"), right(cot), left(cot)
    caf = shift(cot, "x", 2)

    xhat, weights_in, weights_out, qkv, slope, gated = kernel(
        project_kernel,
        (S((SEQ, D), BF), S((896, D), BF), S((D, 640), BF), S((SEQ, 384), BF), S((SEQ, 512), BF), S((SEQ, 512), BF)),
        (ids, table), (inputs, b0_, ar, br, af_, bf, al, bl_, *near, *far, bias, gain, shift_row, cosines, sines),
        "project", 7, [pltpu.VMEM((SEQ, D), BF), pltpu.VMEM((16, HD, D), BF)],
    )
    qkv, cb0 = after(qkv, cb0)
    cbl, cbr = right(cb0), left(cb0)
    cbf = shift(cb0, "x", 2)
    joined, lse = kernel(attend_kernel, (S((SEQ, 640), BF), S((8, SEQ), F32)), (), (qkv, gated), "attend", 3)
    oa, ob, ra, rb, fa, fb, la, lb = kernel(
        project_out_kernel, (chunk,) * 8, (ids,), (joined, weights_out), "project_out", 3
    )
    fa, fb = right(fa), left(fb)
    grad_attn, grad_ff, cots = kernel(
        backward_out_kernel, (S((SEQ, 128), BF), S((SEQ, 512), BF), S((SEQ, D), BF)), (ids,),
        (cot, cb0, car, cbr, caf, cbf, cal, cbl, weights_out, slope), "backward_out", 3,
    )
    grad_proj = kernel(
        backward_attend_kernel, S((SEQ, 896), BF), (), (qkv, lse, grad_attn, grad_ff, cosines, sines),
        "backward_attend", 5, [pltpu.VMEM((SEQ, 128), F32)] * 3,
    )
    grad_proj, fa, fb = after(grad_proj, fa, fb)
    slots = lambda columns: S((4, 2, HD, columns), BF)
    wide = D + 128
    near_in, far_in = kernel(
        backward_w_in_kernel, (slots(wide), slots(wide)), (ids, table),
        (grad_proj, weights_in, xhat, gain, shift_row, cotangent), "backward_w_in", 6, [pltpu.VMEM((32, 128), F32)],
    )
    far_in = swap(far_in, "core")

    near_out, far_out = kernel(
        backward_w_out_kernel, (slots(640), slots(640)), (ids,), (cots, joined), "backward_w_out", 3
    )
    far_out = swap(far_out, "core")
    grad_proj, near_out = after(grad_proj, near_out)
    pair = S((2, 128, D), BF)
    parts = kernel(
        backward_normed_kernel, (chunk, chunk, chunk, pair, chunk, chunk, pair, chunk), (ids,),
        (grad_proj, weights_in, rb, la), "backward_normed", 4,
    )
    far_in, *parts = after(far_in, *parts)
    slot = S((HD, WIDE + 128), BF)
    wa, wb, wua, wub, wfa, wfb, wda, wdb = kernel(
        add_slots_kernel, (slot,) * 8, (), (near_in, far_in, near_out, far_out), "add_slots", 1
    )
    wfa, wfb, wub, wda = up(wfa), down(wfb), up(wub), down(wda)
    wua = up(kernel(add_slot_kernel, slot, (), (wua, wfa), "add_slot", 1))
    wdb = down(kernel(add_slot_kernel, slot, (), (wdb, wfb), "add_slot", 1))
    goa, gob, gra, grb, gfa, gfb, gla, glb = parts
    gfa, gfb, rb, la = right(gfa), left(gfb), right(grb), left(gla)
    gfa, wub = after(gfa, wub)
    gfb, wda = after(gfb, wda)
    ra = right(jnp.stack([add(gra, gfa), add(ra, fa)]))
    lb = left(jnp.stack([add(glb, gfb), add(lb, fb)]))
    wua, rb, la = after(wua, rb, la)
    mine, other = kernel(sum_slots_kernel, (slot, slot), (), (wa, wua, wda, wb, wub, wdb), "sum_slots", 2)
    far = swap(other, "zh")
    ob = swap(jnp.stack([add(gob, rb[0], lb[0]), add(ob, rb[1], lb[1])]), "zl")
    a0 = kernel(add_slot_kernel, slot, (), (mine, far), "add_slot", 1)
    b0, al, ar = swap(a0, "zl"), right(a0), left(a0)
    bl, br, af = right(b0), left(b0), right(al)
    br, ar, al = after(br, ar, al)
    bf = left(br)
    grad_inputs, out = kernel(
        finish_tokens_kernel, (chunk, chunk), (),
        (goa, oa, ra, la, ob, inputs, cotangent, gain, b_out[None]), "finish_tokens", 1,
    )
    row = S((8, 128), F32)
    grad_w_in, grad_w_out, grad_gain, grad_shift, grad_b_out, grad_b_in = kernel(
        finish_weights_kernel, (S((448, D), F32), S((HD, 5120), F32), row, row, row, S((56, 128), F32)),
        (ids, shard_table), (a0, b0, ar, br, af, bf, al, bl), "finish_weights", 3, [pltpu.VMEM((8, HD, WIDE + 128), BF)],
    )
    return (
        out, grad_inputs, grad_gain.reshape(D), grad_shift.reshape(D),
        grad_w_in, grad_b_in.reshape(7168), grad_w_out, grad_b_out.reshape(D),
    )


def solution(mesh):
    fine = Mesh(mesh.devices.reshape(4, 2, 2, 4, 2), SHARD + CONTEXT)
    rows = P(SHARD + CONTEXT, None)
    in_specs = (rows, P(), P(), P(SHARD, None), P(), P(SHARD, None), P(), rows)
    out_specs = (rows, rows, P(), P(), P(SHARD, None), P(), P(SHARD, None), P())
    return jax.shard_map(on_device, mesh=fine, in_specs=in_specs, out_specs=out_specs, check_vma=False)
```

```python
import functools
import math

import jax
import jax.numpy as jnp
import numpy as np
from jax import lax
from jax.experimental import pallas as pl
from jax.experimental.pallas import tpu as pltpu
from jax.sharding import Mesh
from jax.sharding import PartitionSpec as P

D = 1024
FF = 4096
H = 16
HD = 64
ROT = 32
SEQ = 1024
EPS = 1e-05
WIDE = D + 640
BF = jnp.bfloat16
F32 = jnp.float32
MIB = 1 << 20

COST = {'prepare': 0.2, 'project': 0.7000000000000001, 'attend': 0.30000000000000004, 'project_out': 0.30000000000000004, 'backward_out': 0.30000000000000004, 'backward_attend': 0.5, 'backward_w_in': 0.6000000000000001, 'backward_w_out': 0.30000000000000004, 'add_slots': 0.1, 'backward_normed': 0.4, 'sum_slots': 0.2, 'add_slot': 0.1, 'finish_tokens': 0.1, 'finish_weights': 0.30000000000000004}

SHARD = ("y", "zh", "core")
CONTEXT = ("x", "zl")

HEADS = ((0, 7), (8, 1), (14, 9), (6, 15), (12, 5), (4, 13), (10, 3), (2, 11))
UNITS_PER_SHARD = 7


def deal_units():
    columns = [[[], []] for _ in range(8)]
    qkv = [[kind * H + head for kind in range(3) for head in pair] for pair in HEADS]
    taken = [{unit // UNITS_PER_SHARD for unit in units} for units in qkv]
    order = []

    def place(unit):
        if unit == 112:
            return True
        shard, parity = unit // UNITS_PER_SHARD, unit % 2
        choices = sorted(range(8), key=lambda c: len(columns[c][0]) + len(columns[c][1]))
        for c in choices:
            if shard in taken[c] or len(columns[c][parity]) == 4:
                continue
            taken[c].add(shard)
            columns[c][parity].append(unit)
            if place(unit + 1):
                return True
            taken[c].remove(shard)
            columns[c][parity].pop()
        return False

    assert place(48)
    for c in range(8):
        pairs = [unit for pair in zip(*columns[c]) for unit in pair]
        order.append(qkv[c] + pairs)
    return np.array(order, np.int32)


UNITS = deal_units()
SLOT = UNITS // UNITS_PER_SHARD
SEND = np.zeros((16, 8), np.int32)
for _c in range(8):
    for _u in UNITS[_c]:
        SEND[_u // UNITS_PER_SHARD, _c] = _u % UNITS_PER_SHARD
HOME = np.zeros((112, 2), np.int32)
for _c in range(8):
    for _i, _u in enumerate(UNITS[_c]):
        HOME[_u] = (_c, _i)
COLUMN_UNITS = np.concatenate([np.array(HEADS, np.int32), UNITS[:, 6:] - 32], axis=1)
COLUMN_HOME = np.zeros((80, 2), np.int32)
for _c in range(8):
    for _i, _u in enumerate(COLUMN_UNITS[_c]):
        COLUMN_HOME[_u] = (_c, _i)


TABLE = np.concatenate([SLOT, COLUMN_UNITS // 2, UNITS // 2], axis=1).astype(np.int32)
SHARD_TABLE = np.concatenate([SEND, HOME[:, 0].reshape(16, 7)], axis=1).astype(np.int32)

def nn(left, right):
    return lax.dot_general(left, right, (((1,), (0,)), ((), ())), preferred_element_type=F32)


def nt(left, right):
    return lax.dot_general(left, right, (((1,), (1,)), ((), ())), preferred_element_type=F32)


def tn(left, right):
    return lax.dot_general(left, right, (((0,), (0,)), ((), ())), preferred_element_type=F32)


def normal(rows):
    average = jnp.mean(rows, axis=-1, keepdims=True)
    centred = rows - average
    variance = jnp.mean(centred * centred, axis=-1, keepdims=True)
    scale = lax.rsqrt(variance + EPS)
    return centred * scale, scale


def turn(values, cosines, sines):
    lane = lax.broadcasted_iota(jnp.int32, values.shape, 1) % HD
    ahead = pltpu.roll(values, 2 * HD - ROT // 2, 1)
    behind = pltpu.roll(values, ROT // 2, 1)
    return values * cosines + jnp.where(lane < ROT // 2, ahead, behind) * sines


def head_mask(values, head):
    lane = lax.broadcasted_iota(jnp.int32, values.shape, 1)
    return jnp.where((lane // HD) == head, values, jnp.zeros_like(values))


SCALE2 = HD ** (-0.5) * math.log2(math.e)
GELU_C = math.sqrt(2.0 / math.pi)
BLOCK = 256


def causal(shape, first_key, first_query):
    key = first_key + lax.broadcasted_iota(jnp.int32, shape, 0)
    query = first_query + lax.broadcasted_iota(jnp.int32, shape, 1)
    return key <= query


def block_scores(q_block, k_head, block):
    extent = (block + 1) * BLOCK
    scores = nt(k_head[:extent], q_block) * SCALE2
    last = scores[block * BLOCK:]
    last = jnp.where(causal(last.shape, 0, 0), last, -1e30)
    if block == 0:
        return last
    return jnp.concatenate([scores[: block * BLOCK], last], axis=0)


def index_of(ring, step, which, mine):
    return lax.rem(ring + step, 4) * 2 + (mine if which == 0 else 1 - mine)


def prepare_kernel(ids, table, shard_table, w_in, w_out, b_in, message, bias):
    shard, context = ids[3], ids[4]
    unit = shard_table[shard, context]
    message[:, :D] = w_in[pl.ds(pl.multiple_of(unit * HD, HD), HD), :]
    lower = lax.broadcasted_iota(jnp.int32, (HD, 128), 1) < HD
    for j in range(5):
        even = w_out[:, pl.ds(pl.multiple_of(table[context, 14 + 2 * j] * 128, 128), 128)]
        odd = w_out[:, pl.ds(pl.multiple_of(table[context, 15 + 2 * j] * 128, 128), 128)]
        tile = jnp.where(lower, even, odd)
        message[:, D + j * 128 : D + (j + 1) * 128] = tile
    lower = lax.broadcasted_iota(jnp.int32, (1, 128), 1) < HD
    for j in range(7):
        even = b_in[pl.ds(table[context, 24 + 2 * j], 1), :]
        odd = b_in[pl.ds(table[context, 25 + 2 * j], 1), :]
        bias[:, j * 128 : (j + 1) * 128] = jnp.where(lower, even, odd)


def project_kernel(ids, table, a0, b0, ar, br, af, bf, al, bl,
                   na0, nb0, nar, nbr, naf, nbf, nal, nbl, fa0, fb0, far_, fbr, faf, fbf, fal, fbl,
                   bias, gain, shift, cosines, sines, xhat, weights, weights_out, qkv, slope, gated, hidden, held):
    x, zl, core, context, y, zh = ids[0], ids[1], ids[2], ids[4], ids[5], ids[6]
    near = ((na0, nb0), (nar, nbr), (naf, nbf), (nal, nbl))
    far = ((fa0, fb0), (far_, fbr), (faf, fbf), (fal, fbl))
    for step in range(4):
        for which in (0, 1):
            place = 2 * index_of(y, step, which, zh)
            for piece, slot in ((near[step][which], place + core), (far[step][which], place + 1 - core)):
                held[slot] = piece[:, :D]
                weights_out[pl.ds(pl.multiple_of(slot * HD, HD), HD), :] = piece[:, D:]
    for i in range(14):
        weights[i * HD : (i + 1) * HD, :] = held[table[context, i]]

    for step, pair in enumerate(((a0, b0), (ar, br), (af, bf), (al, bl))):
        for which in (0, 1):
            rows = pl.ds(pl.multiple_of(index_of(x, step, which, zl) * 128, 128), 128)
            normed, _ = normal(pair[which][...].astype(F32))
            xhat[rows, :] = normed.astype(BF)
            hidden[rows, :] = (normed * gain[...] + shift[...]).astype(BF)

    @pl.loop(0, 4)
    def _(i):
        rows = pl.ds(pl.multiple_of(i * 256, 256), 256)
        proj = nt(hidden[rows, :], weights[...]) + bias[...]
        cos_rows, sin_rows = cosines[rows, :], sines[rows, :]
        qkv[rows, 0:128] = turn(proj[:, 0:128], cos_rows, sin_rows).astype(BF)
        qkv[rows, 128:256] = turn(proj[:, 128:256], cos_rows, sin_rows).astype(BF)
        qkv[rows, 256:384] = proj[:, 256:384].astype(BF)
        act = proj[:, 384:]
        square = act * act
        th = jnp.tanh(GELU_C * act * (1.0 + 0.044715 * square))
        half = 0.5 * (1.0 + th)
        gated[rows, :] = (act * half).astype(BF)
        slope[rows, :] = (
            half + 0.5 * act * (1.0 - th * th) * (GELU_C * (1.0 + 3 * 0.044715 * square))
        ).astype(BF)


def attend_kernel(qkv, gated, joined, lse):
    joined[:, 128:] = gated[...]
    keys, values = qkv[:, 128:256], qkv[:, 256:384]
    for head in range(2):
        k_head = head_mask(keys, head)
        v_head = head_mask(values, head)
        for block in range(SEQ // BLOCK):
            rows = pl.ds(block * BLOCK, BLOCK)
            scores = block_scores(qkv[rows, 0:128], k_head, block)
            largest = jnp.max(scores, axis=0, keepdims=True)
            raised = jnp.exp2(scores - largest)
            mass = jnp.sum(raised, axis=0, keepdims=True)
            lse[head : head + 1, block * BLOCK : (block + 1) * BLOCK] = largest + jnp.log2(mass)
            probs = (raised * (1.0 / mass)).astype(BF)
            result = tn(probs, v_head[: (block + 1) * BLOCK])
            if head == 0:
                joined[rows, 0:128] = result.astype(BF)
            else:
                joined[rows, 0:128] = (joined[rows, 0:128].astype(F32) + result).astype(BF)


def store_pair(zl, product, a, b):
    @pl.when(zl == 0)
    def _():
        a[...] = product[:128]
        b[...] = product[128:]

    @pl.when(zl != 0)
    def _():
        a[...] = product[128:]
        b[...] = product[:128]


def project_out_kernel(ids, joined, weights, oa, ob, ra, rb, fa, fb, la, lb):
    x, zl = ids[0], ids[1]
    for step, a, b in ((2, fa, fb), (1, ra, rb), (3, la, lb), (0, oa, ob)):
        rows = pl.ds(pl.multiple_of(lax.rem(x + step, 4) * 256, 256), 256)
        store_pair(zl, nt(joined[rows, :], weights[...]).astype(BF), a, b)


def backward_out_kernel(ids, a0, b0, ar, br, af, bf, al, bl, weights_out, slope, grad_attn, grad_ff, cot):
    x, zl = ids[0], ids[1]
    for step, pair in enumerate(((a0, b0), (ar, br), (af, bf), (al, bl))):
        for which in (0, 1):
            cot[pl.ds(pl.multiple_of(index_of(x, step, which, zl) * 128, 128), 128), :] = pair[which][...]

    @pl.loop(0, 4)
    def _(i):
        rows = pl.ds(pl.multiple_of(i * 256, 256), 256)
        grad = nn(cot[rows, :], weights_out[...])
        grad_attn[rows, :] = grad[:, :128].astype(BF)
        grad_ff[rows, :] = (grad[:, 128:] * slope[rows, :].astype(F32)).astype(BF)


def backward_attend_kernel(qkv, lse, grad_attn, grad_ff, cosines, sines, grad_proj, grad_q, grad_k, grad_v):
    keys, values = qkv[:, 128:256], qkv[:, 256:384]
    grad_k[...] = jnp.zeros_like(grad_k)
    grad_v[...] = jnp.zeros_like(grad_v)
    for head in range(2):
        k_head = head_mask(keys, head)
        v_head = head_mask(values, head)
        for block in range(SEQ // BLOCK):
            rows = pl.ds(block * BLOCK, BLOCK)
            extent = (block + 1) * BLOCK
            scores = block_scores(qkv[rows, 0:128], k_head, block)
            probs = jnp.exp2(scores - lse[head : head + 1, block * BLOCK : (block + 1) * BLOCK])
            grad_out = grad_attn[rows, :]
            grad_probs = nt(v_head[:extent], grad_out)
            delta = jnp.sum(grad_probs * probs, axis=0, keepdims=True)
            grad_scores = (probs * (grad_probs - delta)).astype(BF)
            grad_v[:extent, :] += nn(probs.astype(BF), head_mask(grad_out, head))
            grad_k[:extent, :] += nn(grad_scores, head_mask(qkv[rows, 0:128], head))
            result = tn(grad_scores, k_head[:extent])
            if head == 0:
                grad_q[rows, :] = result
            else:
                grad_q[rows, :] += result
    scale = HD ** (-0.5)
    cos_all, sin_all = cosines[...], -sines[...]
    grad_proj[:, 0:128] = turn((grad_q[...] * scale).astype(BF).astype(F32), cos_all, sin_all).astype(BF)
    grad_proj[:, 128:256] = turn((grad_k[...] * scale).astype(BF).astype(F32), cos_all, sin_all).astype(BF)
    grad_proj[:, 256:384] = grad_v[...].astype(BF)
    grad_proj[:, 384:] = grad_ff[...]


def split(values):
    high = values.astype(BF)
    return high, (values - high.astype(F32)).astype(BF)


def slot_place(ids, slot):
    return lax.rem(slot // 4 - ids[5] + 4, 4), jnp.where((slot // 2) % 2 == ids[6], 0, 1)


def backward_w_in_kernel(ids, table, grad_proj, weights, xhat, gain, shift, own, near, far, vectors):
    core, context = ids[2], ids[4]
    ones = jnp.ones((SEQ, 128), BF)
    grad_gain, grad_shift = jnp.zeros((1, D), F32), jnp.zeros((1, D), F32)
    for step in range(4):
        for side in (0, 1):
            near[step, side, :, :D] = jnp.zeros((HD, D), BF)
            far[step, side, :, :D] = jnp.zeros((HD, D), BF)
    for i in range(4):
        first, last = i * 256, min((i + 1) * 256, 896)
        proj = grad_proj[:, first:last]
        product = tn(proj, xhat[...])
        column = tn(proj, ones)
        sums = column.T[0:1]
        for j in range((last - first) // 128):
            vectors[24 + 2 * i + j : 25 + 2 * i + j, :] = sums[:, j * 128 : (j + 1) * 128]
        column = column[:, 0:1]
        rows = weights[first:last, :].astype(F32)
        grad_gain += jnp.sum(product * rows, axis=0, keepdims=True)
        grad_shift += jnp.sum(column * rows, axis=0, keepdims=True)
        grad = (product * gain[...] + column * shift[...]).astype(BF)
        for j in range((last - first) // HD):
            slot = table[context, 4 * i + j]
            step, side = slot_place(ids, slot)

            @pl.when(slot % 2 == core)
            def _():
                near[step, side, :, :D] = grad[j * HD : (j + 1) * HD]

            @pl.when(slot % 2 != core)
            def _():
                far[step, side, :, :D] = grad[j * HD : (j + 1) * HD]

    vectors[31:32, :] = jnp.zeros((1, 128), F32)
    grad_b_out = jnp.sum(own[...].astype(F32), axis=0, keepdims=True)
    for j in range(8):
        lanes = slice(j * 128, (j + 1) * 128)
        vectors[j : j + 1, :] = grad_gain[:, lanes]
        vectors[8 + j : 9 + j, :] = grad_shift[:, lanes]
        vectors[16 + j : 17 + j, :] = grad_b_out[:, lanes]
    high, low = split(vectors[...])
    for step in range(4):
        for side in (0, 1):
            for ref in (near, far):
                ref[step, side, :32, D:] = high
                ref[step, side, 32:, D:] = low


def backward_w_out_kernel(ids, cot, joined, near, far):
    core = ids[2]
    for i in range(4):
        pairs = tn(cot[:, i * 256 : (i + 1) * 256], joined[...]).astype(BF)
        for j in (0, 1):
            grad = pairs[j * 128 : (j + 1) * 128]
            step, side = slot_place(ids, 4 * i + 2 * j)

            @pl.when(core == 0)
            def _():
                near[step, side] = grad[:HD]
                far[step, side] = grad[HD:]

            @pl.when(core != 0)
            def _():
                near[step, side] = grad[HD:]
                far[step, side] = grad[:HD]


def backward_normed_kernel(ids, grad_proj, weights, out_rb, out_la, oa, ob, ra, rb, fa, fb, la, lb):
    x, zl = ids[0], ids[1]
    for step, a, b in ((2, fa, fb), (1, ra, rb.at[0]), (3, la.at[0], lb), (0, oa, ob)):
        rows = pl.ds(pl.multiple_of(lax.rem(x + step, 4) * 256, 256), 256)
        store_pair(zl, nn(grad_proj[rows, :], weights[...]).astype(BF), a, b)
    rb[1] = out_rb[...]
    la[1] = out_la[...]


def total_vectors(*terms):
    return split(sum(term[rows, :].astype(F32) for term in terms for rows in (slice(0, 32), slice(32, 64))))


def add_slots_kernel(near_in, far_in, near_out, far_out, *parts):
    high, low = total_vectors(near_in[0, 0, :, D:], far_in[0, 0, :, D:])
    for step in range(4):
        for side in (0, 1):
            part = parts[2 * step + side]
            part[:, :D] = (near_in[step, side, :, :D].astype(F32) + far_in[step, side, :, :D].astype(F32)).astype(BF)
            part[:, D:WIDE] = (near_out[step, side].astype(F32) + far_out[step, side].astype(F32)).astype(BF)
            part[:32, WIDE:] = high
            part[32:, WIDE:] = low


def sum_slots_kernel(a0, a1, a2, b0, b1, b2, mine, other):
    high, low = total_vectors(*(part[:, WIDE:] for part in (a0, a1, a2)))
    for total, parts in ((mine, (a0, a1, a2)), (other, (b0, b1, b2))):
        total[:, :WIDE] = sum(part[:, :WIDE].astype(F32) for part in parts).astype(BF)
        total[:32, WIDE:] = high
        total[32:, WIDE:] = low


def add_slot_kernel(mine, far, total):
    total[:, :WIDE] = (mine[:, :WIDE].astype(F32) + far[:, :WIDE].astype(F32)).astype(BF)
    high, low = total_vectors(mine[:, WIDE:], far[:, WIDE:])
    total[:32, WIDE:] = high
    total[32:, WIDE:] = low


def finish_tokens_kernel(goa, oa, ra, la, far, inputs, cotangent, gain, b_out, grad_inputs, out):
    grad, mixed = (
        own[...].astype(F32) + sum(term[k].astype(F32) for term in (ra, la, far)) for k, own in ((0, goa), (1, oa))
    )
    rows = inputs[...].astype(F32)
    out[...] = (rows + mixed + b_out[...]).astype(BF)
    own, scale = normal(rows)
    pulled = grad * gain[...]
    pulled = (
        pulled
        - jnp.mean(pulled, axis=-1, keepdims=True)
        - own * jnp.mean(pulled * own, axis=-1, keepdims=True)
    ) * scale
    grad_inputs[...] = (cotangent[...].astype(F32) + pulled).astype(BF)


def finish_weights_kernel(ids, shard_table, a0, b0, ar, br, af, bf, al, bl,
                          grad_w_in, grad_w_out, grad_gain, grad_shift, grad_b_out, grad_b_in, held):
    for step, pair in enumerate(((a0, b0), (ar, br), (af, bf), (al, bl))):
        for which in (0, 1):
            held[index_of(ids[0], step, which, ids[1])] = pair[which][...]
    for i in range(7):
        grad_w_in[i * HD : (i + 1) * HD, :] = held[shard_table[ids[3], 8 + i], :, :D].astype(F32)
    lower = lax.broadcasted_iota(jnp.int32, (HD, 128), 1) < HD
    for t in range(40):
        tiles = []
        for unit in (2 * t, 2 * t + 1):
            c, i = (int(n) for n in COLUMN_HOME[unit])
            first = D + (i // 2) * 128
            tiles.append(held[c, :, first : first + 128].astype(F32))
        grad_w_out[:, t * 128 : (t + 1) * 128] = jnp.where(lower, *tiles)
    terms = [held[c, :32, WIDE:].astype(F32) + held[c, 32:, WIDE:].astype(F32) for c in range(8)]
    total = sum(term[:24] for term in terms)
    grad_gain[...] = total[0:8]
    grad_shift[...] = total[8:16]
    grad_b_out[...] = total[16:24]
    lower = lax.broadcasted_iota(jnp.int32, (1, 128), 1) < HD
    for row in range(56):
        (c, i), (d, j) = (tuple(int(n) for n in HOME[unit]) for unit in (2 * row, 2 * row + 1))
        grad_b_in[row : row + 1, :] = jnp.where(
            lower, terms[c][24 + i // 2 : 25 + i // 2], terms[d][24 + j // 2 : 25 + j // 2]
        )


VM = pl.BlockSpec(memory_space=pltpu.VMEM)
SM = pl.BlockSpec(memory_space=pltpu.SMEM)
S = jax.ShapeDtypeStruct


def kernel(body, outs, scalars, operands, name, us, scratch=()):
    return pl.pallas_call(
        body,
        out_shape=outs,
        in_specs=[SM] * len(scalars) + [VM] * len(operands),
        out_specs=jax.tree.map(lambda _: VM, outs),
        scratch_shapes=list(scratch),
        compiler_params=pltpu.CompilerParams(vmem_limit_bytes=24 * MIB),
        cost_estimate=pl.CostEstimate(flops=int(COST[name] * 1e9), bytes_accessed=int(COST[name] * 3e6), transcendentals=0),
        name=name,
    )(*scalars, *operands)


def hbm(*arrays):
    return tuple(pltpu.with_memory_space_constraint(array, pltpu.HBM) for array in arrays)


def shift(values, axis, by):
    return lax.ppermute(values, axis, [(i, (i + by) % 4) for i in range(4)])


def swap(values, axis):
    return lax.ppermute(values, axis, [(0, 1), (1, 0)])


def gather_ring(pair, axis):
    ahead, behind = shift(pair, axis, -1), shift(pair, axis, 1)
    return pair, ahead, shift(pair, axis, 2), behind


def scatter_ring(p0, p1, p2, p3, axis):
    return p0, shift(p1, axis, 1), shift(p3, axis, -1), shift(p2, axis, 2)


def ordered(index, mine, other):
    return jnp.stack([jnp.where(index == 0, mine, other), jnp.where(index == 0, other, mine)])


def pick(pair, index):
    return lax.dynamic_index_in_dim(pair, index, 0, keepdims=False)


def add(*terms):
    return sum(term.astype(F32) for term in terms).astype(BF)


def after(values, *events):
    return lax.optimization_barrier((values,) + events)


def turn_tables():
    steps = np.arange(ROT // 2)
    angles = np.arange(SEQ)[:, None] * (10000.0 ** (-2.0 * steps / ROT))[None, :]
    cosine, sine = np.cos(angles), np.sin(angles)
    still = np.ones((SEQ, HD - ROT))
    cosines = np.concatenate([cosine, cosine, still] * 2, axis=1)
    sines = np.concatenate([-sine, sine, 0.0 * still] * 2, axis=1)
    return jnp.asarray(cosines.astype(np.float32)), jnp.asarray(sines.astype(np.float32))


def on_device(inputs, ln_gain, ln_bias, w_in, b_in, w_out, b_out, cotangent):
    ids = jnp.stack(
        [lax.axis_index(axes) for axes in ("x", "zl", "core", SHARD, CONTEXT, "y", "zh")]
    ).astype(jnp.int32)
    table, shard_table = jnp.asarray(TABLE), jnp.asarray(SHARD_TABLE)
    cosines, sines = turn_tables()
    gain, shift_row = ln_gain[None], ln_bias[None]
    right, left = lambda v: shift(v, "x", 1), lambda v: shift(v, "x", -1)
    up, down = lambda v: shift(v, "y", 1), lambda v: shift(v, "y", -1)

    chunk = S((128, D), BF)
    message, bias = kernel(
        prepare_kernel, (S((HD, 1664), BF), S((1, 896), F32)), (ids, *hbm(table, shard_table)),
        hbm(w_in, w_out, b_in.reshape(56, 128)), "prepare", 2,
    )
    first = inputs
    b0, al, ar = swap(first, "zl"), right(first), left(first)
    later, b0_ = after(message, b0)
    nb0 = swap(later, "zh")
    nal, nar = up(message), down(message)
    bl, br, af = right(b0), left(b0), right(al)
    cot = cotangent
    br, ar, al = after(br, ar, al)
    bf = left(br)
    nbl, nbr, naf = up(nb0), down(nb0), up(nal)
    nbf = down(nbr)
    af_, bl_ = af, bl
    nbf, af_, bl_ = after(nbf, af, bl)
    near = later, nb0, nar, nbr, naf, nbf, nal, nbl
    far = [swap(piece, "core") for piece in near]
    cot, bl_ = after(cot, bl_)
    cb0, cal, car = swap(cot, "zl"), right(cot), left(cot)
    caf = shift(cot, "x", 2)

    xhat, weights_in, weights_out, qkv, slope, gated = kernel(
        project_kernel,
        (S((SEQ, D), BF), S((896, D), BF), S((D, 640), BF), S((SEQ, 384), BF), S((SEQ, 512), BF), S((SEQ, 512), BF)),
        (ids, table), (inputs, b0_, ar, br, af_, bf, al, bl_, *near, *far, bias, gain, shift_row, cosines, sines),
        "project", 7, [pltpu.VMEM((SEQ, D), BF), pltpu.VMEM((16, HD, D), BF)],
    )
    qkv, cb0 = after(qkv, cb0)
    cbl, cbr = right(cb0), left(cb0)
    cbf = shift(cb0, "x", 2)
    joined, lse = kernel(attend_kernel, (S((SEQ, 640), BF), S((8, SEQ), F32)), (), (qkv, gated), "attend", 3)
    oa, ob, ra, rb, fa, fb, la, lb = kernel(
        project_out_kernel, (chunk,) * 8, (ids,), (joined, weights_out), "project_out", 3
    )
    fa, fb = right(fa), left(fb)
    grad_attn, grad_ff, cots = kernel(
        backward_out_kernel, (S((SEQ, 128), BF), S((SEQ, 512), BF), S((SEQ, D), BF)), (ids,),
        (cot, cb0, car, cbr, caf, cbf, cal, cbl, weights_out, slope), "backward_out", 3,
    )
    grad_proj = kernel(
        backward_attend_kernel, S((SEQ, 896), BF), (), (qkv, lse, grad_attn, grad_ff, cosines, sines),
        "backward_attend", 5, [pltpu.VMEM((SEQ, 128), F32)] * 3,
    )
    grad_proj, fa, fb = after(grad_proj, fa, fb)
    slots = lambda columns: S((4, 2, HD, columns), BF)
    wide = D + 128
    near_in, far_in = kernel(
        backward_w_in_kernel, (slots(wide), slots(wide)), (ids, table),
        (grad_proj, weights_in, xhat, gain, shift_row, cotangent), "backward_w_in", 6, [pltpu.VMEM((32, 128), F32)],
    )
    far_in = swap(far_in, "core")

    near_out, far_out = kernel(
        backward_w_out_kernel, (slots(640), slots(640)), (ids,), (cots, joined), "backward_w_out", 3
    )
    far_out = swap(far_out, "core")
    grad_proj, near_out = after(grad_proj, near_out)
    pair = S((2, 128, D), BF)
    parts = kernel(
        backward_normed_kernel, (chunk, chunk, chunk, pair, chunk, chunk, pair, chunk), (ids,),
        (grad_proj, weights_in, rb, la), "backward_normed", 4,
    )
    far_in, *parts = after(far_in, *parts)
    slot = S((HD, WIDE + 128), BF)
    wa, wb, wua, wub, wfa, wfb, wda, wdb = kernel(
        add_slots_kernel, (slot,) * 8, (), (near_in, far_in, near_out, far_out), "add_slots", 1
    )
    wfa, wfb, wub, wda = up(wfa), down(wfb), up(wub), down(wda)
    wua = up(kernel(add_slot_kernel, slot, (), (wua, wfa), "add_slot", 1))
    wdb = down(kernel(add_slot_kernel, slot, (), (wdb, wfb), "add_slot", 1))
    goa, gob, gra, grb, gfa, gfb, gla, glb = parts
    gfa, gfb, rb, la = right(gfa), left(gfb), right(grb), left(gla)
    gfa, wub = after(gfa, wub)
    gfb, wda = after(gfb, wda)
    ra = right(jnp.stack([add(gra, gfa), add(ra, fa)]))
    lb = left(jnp.stack([add(glb, gfb), add(lb, fb)]))
    wua, rb, la = after(wua, rb, la)
    mine, other = kernel(sum_slots_kernel, (slot, slot), (), (wa, wua, wda, wb, wub, wdb), "sum_slots", 2)
    far = swap(other, "zh")
    ob = swap(jnp.stack([add(gob, rb[0], lb[0]), add(ob, rb[1], lb[1])]), "zl")
    a0 = kernel(add_slot_kernel, slot, (), (mine, far), "add_slot", 1)
    b0, al, ar = swap(a0, "zl"), right(a0), left(a0)
    bl, br, af = right(b0), left(b0), right(al)
    br, ar, al = after(br, ar, al)
    bf = left(br)
    grad_inputs, out = kernel(
        finish_tokens_kernel, (chunk, chunk), (),
        (goa, oa, ra, la, ob, inputs, cotangent, gain, b_out[None]), "finish_tokens", 1,
    )
    row = S((8, 128), F32)
    grad_w_in, grad_w_out, grad_gain, grad_shift, grad_b_out, grad_b_in = kernel(
        finish_weights_kernel, (S((448, D), F32), S((HD, 5120), F32), row, row, row, S((56, 128), F32)),
        (ids, shard_table), (a0, b0, ar, br, af, bf, al, bl), "finish_weights", 3, [pltpu.VMEM((8, HD, WIDE + 128), BF)],
    )
    return (
        out, grad_inputs, grad_gain.reshape(D), grad_shift.reshape(D),
        grad_w_in, grad_b_in.reshape(7168), grad_w_out, grad_b_out.reshape(D),
    )


def solution(mesh):
    fine = Mesh(mesh.devices.reshape(4, 2, 2, 4, 2), SHARD + CONTEXT)
    rows = P(SHARD + CONTEXT, None)
    in_specs = (rows, P(), P(), P(SHARD, None), P(), P(SHARD, None), P(), rows)
    out_specs = (rows, rows, P(), P(), P(SHARD, None), P(), P(SHARD, None), P())
    return jax.shard_map(on_device, mesh=fine, in_specs=in_specs, out_specs=out_specs, check_vma=False)
```
